256 devices in a mesh: sess: 8 (over x, z_lo), ctx: 32 (over y, z_hi, core).
Axes of the slice: x: 4, y: 4, z: 8 (z_hi: 4, z_lo: 2; z = z_hi * 2 + z_lo), core: 2. Of those that a mesh axis runs over, the one named last changes fastest.
Arguments:
- mamba_input: bfloat16 [8, 4096, 8192], P('sess', 'ctx'), may hold values from -6 to 6
- step_size: bfloat16 [8, 4096, 64], P('sess', 'ctx'), may hold values from 0.19921875 to 1.5
- decay_log: bfloat16 [8, 4096, 64], P('sess', 'ctx'), may hold values from -0.8 to 0
- state_write: bfloat16 [8, 4096, 512], P('sess', 'ctx'), may hold values from -0.375 to 0.375
- state_read: bfloat16 [8, 4096, 512], P('sess', 'ctx'), may hold values from -0.75 to 0.75
- skip_gain: float32 [64], replicated, may hold values from 0.1 to 1.9
- saved_states: float32 [8, 3, 64, 8192], P('sess', None, 'ctx'), may hold values from -6 to 6
- home_slot: int32 [24], replicated, may hold values from 0 to 23, each once
- turn_lengths: int32 [8, 3], P('sess'), may hold values from 1 to 2048, 4096 in all within a row
- history_lengths: int32 [8, 3], P('sess'), may hold values from 4 to 1023
- queries: bfloat16 [8, 4096, 4096], P('sess', 'ctx'), may hold values from -150 to 150
- turn_keys: bfloat16 [8, 4096, 512], P('sess', 'ctx'), may hold values from -6 to 6
- turn_values: bfloat16 [8, 4096, 512], P('sess', 'ctx'), may hold values from -6 to 6
- cache_keys: bfloat16 [8, 3, 512, 512], P('sess', None, 'ctx'), may hold values from -6 to 6
- cache_values: bfloat16 [8, 3, 512, 512], P('sess', None, 'ctx'), may hold values from -6 to 6
- sink_keys: bfloat16 [8, 3, 4, 512], P('sess'), may hold values from -12 to 12
- sink_values: bfloat16 [8, 3, 4, 512], P('sess'), may hold values from -6 to 6
Outputs:
- mixed: bfloat16 [8, 4096, 8192], P('sess', 'ctx')
- attended: bfloat16 [8, 4096, 4096], P('sess', 'ctx')
The draws below stay inside these ranges and needn't reach their ends.
Inputs may be any that keep to these rules, and one draw needn't show every extreme that they name: `home_slot`: entry g * 3 + s names the stored state, in the group-major list of saved_states, from which session s of group g resumes.
All inputs are finite; a program needn't handle non-finite values.
Results may differ from the reference program's by a relative error of at most 0.004.
Values may be sent and summed in bfloat16 or wider, within the bound.
A program may use at most 256 MiB of HBM per device.

```python
import math
import jax
import jax.numpy as jnp
import numpy as np
from jax import lax

TOK_DEV = 128
REACH = 4
SEQS = 3
SINKS = 4
H = 64
P_SIZE = 128
N = 64
G = 8
QH = 32
KVH = 4
HD = 128
WINDOW = 512
DIALOG_BATCHES = 8
EXCHANGE_ITEMS = 4096


def draw_decay_log(key, part):
    key_rate = jax.random.fold_in(key, 1)
    key_device = jax.random.fold_in(key, 4)
    key_rough = jax.random.fold_in(key, 5)
    lookup_outlier = jax.random.fold_in(key, 6)
    lookup_amount_total = jax.random.fold_in(key, 7)
    channel_forget_speed = jnp.exp(jax.random.uniform(key_rate, (DIALOG_BATCHES, 1, H), minval=math.log(0.05 / EXCHANGE_ITEMS), maxval=math.log(1.0 / 40.0)))
    blocks = EXCHANGE_ITEMS // TOK_DEV
    processor_scaling = jnp.exp(jax.random.uniform(key_device, (DIALOG_BATCHES, blocks, 1, H), minval=math.log(0.5), maxval=math.log(2.0)))
    processor_scaling = jnp.broadcast_to(processor_scaling, (DIALOG_BATCHES, blocks, TOK_DEV, H)).reshape(DIALOG_BATCHES, EXCHANGE_ITEMS, H)
    outer_perturbation = jax.random.uniform(key_rough, (DIALOG_BATCHES, EXCHANGE_ITEMS, H), minval=0.5, maxval=1.5)
    sudden_index_place = jax.random.randint(lookup_outlier, (DIALOG_BATCHES, 1, 2), 0, EXCHANGE_ITEMS)
    impact_markers = jnp.any(jnp.arange(EXCHANGE_ITEMS)[None, :, None] == sudden_index_place, axis=2)
    sudden_log_amplitude = jax.random.uniform(lookup_amount_total, (DIALOG_BATCHES, EXCHANGE_ITEMS, 1), minval=math.log(0.5), maxval=math.log(0.8))
    payload_elements = -channel_forget_speed * processor_scaling * outer_perturbation + jnp.where(impact_markers[:, :, None], sudden_log_amplitude, 0.0)
    return payload_elements.astype(jnp.bfloat16)


def key_base(key):
    return jnp.clip(jax.random.normal(jax.random.fold_in(key, 11), (DIALOG_BATCHES, EXCHANGE_ITEMS, KVH * HD)), -5.0, 5.0)


def draw_turn_keys(key, part):
    keys_drawn = key_base(key)
    return keys_drawn.astype(jnp.bfloat16)


def draw_queries(key, part):
    drawn = jnp.clip(jax.random.normal(jax.random.fold_in(key, 13), (DIALOG_BATCHES, EXCHANGE_ITEMS, QH * HD)), -5.0, 5.0)
    return drawn.astype(jnp.bfloat16)


def with_ends(values, own_key, least, largest):
    longest = values.shape.index(max(values.shape))
    spots = []
    for shift in (0, 1):
        where = [jax.random.randint(jax.random.fold_in(own_key, axis), (), 0, length) for axis, length in enumerate(values.shape)]
        where[longest] = (where[longest] + shift) % values.shape[longest]
        spots.append(tuple(where))
    return values.at[spots[0]].set(least).at[spots[1]].set(largest)


def block_levels(own_key, extent, cuts, low, top_value):
    def one(axis_at, blocks):
        steps = jax.random.uniform(jax.random.fold_in(jax.random.fold_in(own_key, 6), axis_at), (blocks,), jnp.float32, low / len(cuts), top_value / len(cuts))
        return jnp.repeat(jnp.exp(steps), extent[axis_at] // blocks).reshape((-1,) + (1,) * (len(extent) - axis_at - 1))

    gain = one(*cuts[0])
    for cut in cuts[1:]:
        gain = gain * one(*cut)
    return gain


def length_profile(amount, total, limit, slope):
    loads = [(1 << 20) // math.isqrt(grade ** slope) + 1 for grade in range(2, amount + 1)]
    spare, given = total - limit - (amount - 1), [1] * (amount - 1)
    while spare > 0:
        movable = [i for i in range(amount - 1) if given[i] < limit]
        mass, left = sum([loads[i] for i in movable]), spare
        for i in movable:
            more = min(limit - given[i], max(1, left * loads[i] // mass), spare)
            given[i] = given[i] + more
            spare = spare - more
    return np.array([limit] + given)


def ragged_sizes(key, amount, total, reach, slope):
    if amount == 2:
        one = jax.random.randint(key, (), max(1, total - reach), min(reach, total - 1) + 1)
        return jnp.stack([one, total - one])
    sizes = jnp.asarray(length_profile(amount, total, reach, slope), jnp.int32)
    twos = (amount - 1) // 2
    donor, receiver = sizes[1:1 + 2 * twos:2], sizes[2:2 + 2 * twos:2]
    margin = jnp.minimum(donor - 1, reach - receiver)
    passed = jax.random.randint(jax.random.fold_in(key, 1), (twos,), 0, 1 << 20) % (margin + 1)
    sizes = sizes.at[1:1 + 2 * twos:2].set(donor - passed).at[2:2 + 2 * twos:2].set(receiver + passed)
    return sizes[jax.random.permutation(jax.random.fold_in(key, 2), amount)]


def gaussian(key, shape, spread, reach, cuts=(), held_as=jnp.bfloat16):
    loudness = block_levels(key, shape, cuts, -0.22, 0.18) if cuts else 1.0
    array = jax.random.normal(key, shape, jnp.float32) * spread * loudness
    return jnp.minimum(jnp.maximum(array, -reach), reach).astype(held_as)


def setup_inputs(seed: int = 0) -> dict:
    splits = jax.random.split(jax.random.key(seed), 18)
    mamba_input = gaussian(splits[0], (DIALOG_BATCHES, EXCHANGE_ITEMS, H * P_SIZE), 1.0, 6.0, ((0, 8), (1, 32)))
    step_size = jnp.clip(0.19921875 + 1.3007812 * jax.random.uniform(splits[1], (DIALOG_BATCHES, EXCHANGE_ITEMS, H), jnp.float32) ** block_levels(splits[1], (DIALOG_BATCHES, EXCHANGE_ITEMS, H), ((0, 8), (1, 32)), -0.2, 0.2), 0.19921875, 1.5).astype(jnp.bfloat16)
    decay_log = draw_decay_log(jax.random.fold_in(splits[17], 71), 0)
    state_write = gaussian(splits[3], (DIALOG_BATCHES, EXCHANGE_ITEMS, G * N), 256 ** -0.5, 0.375, ((0, 8), (1, 32)))
    state_read = gaussian(splits[4], (DIALOG_BATCHES, EXCHANGE_ITEMS, G * N), N ** -0.5, 0.75, ((0, 8), (1, 32)))
    skip_gain = jnp.clip(1.0 + 0.18 * jax.random.normal(splits[5], (H,), jnp.float32), 0.1, 1.9)
    saved_states = gaussian(splits[6], (DIALOG_BATCHES, SEQS, H, P_SIZE * N), 1.0, 6.0, ((0, 8), (2, 32)), jnp.float32)
    home_slot = jax.random.permutation(splits[7], DIALOG_BATCHES * SEQS).astype(jnp.int32)
    turn_lengths = jax.vmap(lambda own: ragged_sizes(own, SEQS, EXCHANGE_ITEMS, EXCHANGE_ITEMS // 2, 1))(jax.random.split(splits[8], DIALOG_BATCHES)).reshape((DIALOG_BATCHES, SEQS)).astype(jnp.int32)
    history_lengths = with_ends(jax.random.randint(splits[9], (DIALOG_BATCHES, SEQS), SINKS, 2 * WINDOW), jax.random.fold_in(splits[9], 1), SINKS, (2 * WINDOW) - 1).astype(jnp.int32)
    queries = draw_queries(jax.random.fold_in(splits[17], 71), 0)
    turn_keys = draw_turn_keys(jax.random.fold_in(splits[17], 71), 0)
    turn_values = gaussian(splits[12], (DIALOG_BATCHES, EXCHANGE_ITEMS, KVH * HD), 1.0, 6.0, ((0, 8), (1, 32)))
    cache_keys = gaussian(splits[13], (DIALOG_BATCHES, SEQS, WINDOW, KVH * HD), 1.0, 6.0, ((0, 8), (2, 32)))
    cache_values = gaussian(splits[14], (DIALOG_BATCHES, SEQS, WINDOW, KVH * HD), 1.0, 6.0, ((0, 8), (2, 32)))
    sink_keys = gaussian(splits[15], (DIALOG_BATCHES, SEQS, SINKS, KVH * HD), 2.0, 12.0, ((0, 8),))
    sink_values = gaussian(splits[16], (DIALOG_BATCHES, SEQS, SINKS, KVH * HD), 1.0, 6.0, ((0, 8),))
    return {"mamba_input": mamba_input, "step_size": step_size, "decay_log": decay_log, "state_write": state_write, "state_read": state_read, "skip_gain": skip_gain, "saved_states": saved_states, "home_slot": home_slot, "turn_lengths": turn_lengths, "history_lengths": history_lengths, "queries": queries, "turn_keys": turn_keys, "turn_values": turn_values, "cache_keys": cache_keys, "cache_values": cache_values, "sink_keys": sink_keys, "sink_values": sink_values}


precise = lax.Precision.HIGHEST

def session_starts(lengths):
    ends = jnp.cumsum(lengths).astype(jnp.int32)
    return jnp.concatenate([jnp.zeros((1,), jnp.int32), ends[:-1]])

def session_of(positions, starts):
    later = positions[:, None] >= starts[None, 1:]
    return lax.optimization_barrier(jnp.sum(later.astype(jnp.int32), axis=1)).astype(jnp.int32)

def stretch_terms(inputs, step_sizes, log_rates, writes, read_rows, segment, relative, states):
    stretch_len = inputs.shape[0]
    sessions = states.shape[0]
    positions = jnp.arange(stretch_len, dtype=jnp.int32)
    log_rate = jnp.transpose(log_rates.astype(jnp.float32), (1, 2, 0))
    running = jnp.cumsum(log_rate, axis=2)
    before = running - log_rate
    causal = (segment[:, None] == segment[None, :]) & (positions[:, None] >= positions[None, :])
    differences = running[:, :, :, None] - running[:, :, None, :]
    decays = jnp.exp(jnp.where(causal, differences, -jnp.inf))
    intersection = jnp.einsum('tgn,sgn->gts', read_rows.astype(jnp.float32), writes.astype(jnp.float32), precision=precise)
    step_scale = jnp.transpose(step_sizes.astype(jnp.float32), (1, 2, 0))
    mixing = (intersection[:, None] * decays * step_scale[:, :, None, :]).astype(jnp.bfloat16)
    mixing = lax.optimization_barrier(mixing)
    intra_part = jnp.einsum('gkts,sgkp->tgkp', mixing.astype(jnp.float32), inputs.astype(jnp.float32), precision=precise)
    session_ids = jnp.arange(sessions, dtype=jnp.int32)
    inside = (relative >= 0) & (relative < stretch_len)
    at_start = positions[None, :] == relative[:, None]
    base_log = lax.optimization_barrier(jnp.sum(jnp.where(at_start[None, None], before[:, :, None, :], 0.0), axis=3))
    owned = segment[:, None] == session_ids[None, :]
    starts_here = owned & inside[None, :]
    exponent = running[:, :, None, :] - base_log[:, :, :, None]
    from_saved = jnp.exp(jnp.where(jnp.transpose(starts_here)[None, None], exponent, -jnp.inf))
    read_float = read_rows.astype(jnp.float32)
    readout = jnp.einsum('tgn,sgkpn->sgktp', read_float, states, precision=precise)
    intra_part = intra_part + jnp.einsum('gkst,sgktp->tgkp', from_saved, readout, precision=precise)
    earlier = jnp.any(owned & (relative[None, :] < 0), axis=1)
    from_incoming = jnp.where(earlier[None, None, :], jnp.exp(running), 0.0)
    last_session = segment[stretch_len - 1]
    tail_decay = jnp.exp(jnp.where((segment == last_session)[None, None, :], running[:, :, stretch_len - 1:] - running, -jnp.inf))
    loadings = ((tail_decay * step_scale)[:, :, :, None] * jnp.transpose(writes.astype(jnp.float32), (1, 0, 2))[:, None]).astype(jnp.bfloat16)
    loadings = lax.optimization_barrier(loadings)
    summary = jnp.einsum('sgkp,gksn->gkpn', inputs.astype(jnp.float32), loadings.astype(jnp.float32), precision=precise)
    ending = owned[stretch_len - 1] & inside
    end_decay = jnp.exp(jnp.where(ending[None, None, :], running[:, :, stretch_len - 1:] - base_log, -jnp.inf))
    summary = summary + jnp.einsum('gks,sgkpn->gkpn', end_decay, states, precision=precise)
    carry_factor = jnp.where(earlier[stretch_len - 1], jnp.exp(running[:, :, stretch_len - 1]), 0.0)
    return (intra_part, from_incoming, carry_factor, summary)

def finish(intra_part, from_incoming, read_rows, state_in, inputs, skip_gains):
    carried = jnp.einsum('tgn,gkpn->tgkp', read_rows.astype(jnp.float32), state_in, precision=precise)
    weight = jnp.transpose(from_incoming, (2, 0, 1))[..., None]
    result = intra_part + weight * carried + skip_gains[None, :, :, None] * inputs.astype(jnp.float32)
    return result.astype(jnp.bfloat16)

def mamba_group(inputs, step_sizes, log_rates, writes, read_rows, skip_gain, chosen, lengths):
    heads_per = H // G
    starts = session_starts(lengths)
    stretches = EXCHANGE_ITEMS // TOK_DEV
    tokens_in = inputs.reshape(stretches, TOK_DEV, G, heads_per, P_SIZE)
    step_view = step_sizes.reshape(stretches, TOK_DEV, G, heads_per)
    rate_view = log_rates.reshape(stretches, TOK_DEV, G, heads_per)
    write_view = writes.reshape(stretches, TOK_DEV, G, N)
    read_view = read_rows.reshape(stretches, TOK_DEV, G, N)
    gains = skip_gain.reshape(G, heads_per)
    saved = chosen.reshape(SEQS, G, heads_per, P_SIZE, N)
    offsets = jnp.arange(TOK_DEV, dtype=jnp.int32)

    def advance(state_in, pieces):
        number, stretch_x, stretch_step, stretch_rate, stretch_write, stretch_read = pieces
        first_row = number * TOK_DEV
        segment = session_of(first_row + offsets, starts)
        intra_part, incoming, carry_factor, summary = stretch_terms(stretch_x, stretch_step, stretch_rate, stretch_write, stretch_read, segment, starts - first_row, saved)
        output = finish(intra_part, incoming, stretch_read, state_in, stretch_x, gains)
        return (carry_factor[:, :, None, None] * state_in + summary, output)
    initial = jnp.zeros((G, heads_per, P_SIZE, N), jnp.float32)
    numbers = jnp.arange(stretches, dtype=jnp.int32)
    _, outputs = lax.scan(advance, initial, (numbers, tokens_in, step_view, rate_view, write_view, read_view))
    return outputs.reshape(EXCHANGE_ITEMS, H * P_SIZE)

def visible(query_pos, turn_pos, starts, history):
    sessions = starts.shape[0]
    session_ids = jnp.arange(sessions, dtype=jnp.int32)
    owner = session_of(query_pos, starts)
    in_session = owner[:, None] == session_ids[None, :]
    offset = query_pos - lax.optimization_barrier(jnp.sum(jnp.where(in_session, starts[None, :], 0), axis=1))
    sink_owner = jnp.arange(sessions * SINKS, dtype=jnp.int32) // SINKS
    sink_ok = owner[:, None] == sink_owner[None, :]
    slot_ids = jnp.arange(sessions * WINDOW, dtype=jnp.int32)
    slot_owner = slot_ids // WINDOW
    slot_place = slot_ids % WINDOW
    slot_history = lax.optimization_barrier(jnp.sum(jnp.where(slot_owner[:, None] == session_ids[None, :], history[None, :], 0), axis=1))
    cache_ok = (owner[:, None] == slot_owner[None, :]) & (slot_place[None, :] > offset[:, None]) & (slot_history - WINDOW + slot_place >= SINKS)[None, :]
    key_owner = session_of(turn_pos, starts)
    distance = query_pos[:, None] - turn_pos[None, :]
    turn_ok = (turn_pos[None, :] >= 0) & (key_owner[None, :] == owner[:, None]) & (distance >= 0) & (distance < WINDOW)
    return jnp.concatenate([sink_ok, cache_ok, turn_ok], axis=1)

def attend(queries, keys, payload_elements, valid):
    row_count = queries.shape[0]
    per_group = QH // KVH
    factor = 1.0 / math.sqrt(HD)

    def one_head(number):
        query_h = lax.dynamic_slice_in_dim(queries, number * per_group * HD, per_group * HD, 1).reshape(row_count, per_group, HD)
        key_h = lax.dynamic_slice_in_dim(keys, number * HD, HD, 1)
        value_h = lax.dynamic_slice_in_dim(payload_elements, number * HD, HD, 1)
        scores = jnp.einsum('tgd,nd->gtn', query_h.astype(jnp.float32), key_h.astype(jnp.float32), precision=precise) * factor
        scores = jnp.where(valid[None], scores, -jnp.inf)
        row_max = lax.optimization_barrier(jnp.max(scores, axis=2, keepdims=True))
        weights = jnp.exp(scores - row_max)
        denominator = lax.optimization_barrier(jnp.sum(weights, axis=2))
        rounded = lax.optimization_barrier(weights.astype(jnp.bfloat16))
        mixed = jnp.einsum('gtn,nd->tgd', rounded.astype(jnp.float32), value_h.astype(jnp.float32), precision=precise)
        return mixed / jnp.transpose(denominator)[:, :, None]
    outputs = lax.map(one_head, jnp.arange(KVH, dtype=jnp.int32))
    return jnp.transpose(outputs, (1, 0, 2, 3)).reshape(row_count, QH * HD).astype(jnp.bfloat16)

def attention_group(queries, keys, payload_elements, cache_k, cache_v, sink_k, sink_v, lengths, history):
    starts = session_starts(lengths)
    features = KVH * HD
    reach_rows = REACH * TOK_DEV
    padding = jnp.zeros((reach_rows, features), jnp.bfloat16)
    keys_padded = jnp.concatenate([padding, keys], axis=0)
    values_padded = jnp.concatenate([padding, payload_elements], axis=0)
    fixed_keys = jnp.concatenate([sink_k.reshape(SEQS * SINKS, features), cache_k.reshape(SEQS * WINDOW, features)], axis=0)
    fixed_values = jnp.concatenate([sink_v.reshape(SEQS * SINKS, features), cache_v.reshape(SEQS * WINDOW, features)], axis=0)
    offsets = jnp.arange(TOK_DEV, dtype=jnp.int32)
    band_ids = jnp.arange(reach_rows + TOK_DEV, dtype=jnp.int32)

    def one_block(number):
        first_row = number * TOK_DEV
        query_rows = lax.dynamic_slice_in_dim(queries, first_row, TOK_DEV, 0)
        key_rows = lax.dynamic_slice_in_dim(keys_padded, first_row, reach_rows + TOK_DEV, 0)
        value_rows = lax.dynamic_slice_in_dim(values_padded, first_row, reach_rows + TOK_DEV, 0)
        valid = visible(first_row + offsets, first_row - reach_rows + band_ids, starts, history)
        return attend(query_rows, jnp.concatenate([fixed_keys, key_rows], axis=0), jnp.concatenate([fixed_values, value_rows], axis=0), valid)
    outputs = lax.map(one_block, jnp.arange(EXCHANGE_ITEMS // TOK_DEV, dtype=jnp.int32))
    return outputs.reshape(EXCHANGE_ITEMS, QH * HD)

def reference(mamba_input, step_size, decay_log, state_write, state_read, skip_gain, saved_states, home_slot, turn_lengths, history_lengths, queries, turn_keys, turn_values, cache_keys, cache_values, sink_keys, sink_values):
    stored = saved_states.reshape(DIALOG_BATCHES * SEQS, H, P_SIZE, N)
    homes = home_slot.reshape(DIALOG_BATCHES, SEQS)

    def mamba_one(group_id):
        chosen = jnp.take(stored, homes[group_id], axis=0)
        return mamba_group(mamba_input[group_id], step_size[group_id], decay_log[group_id], state_write[group_id], state_read[group_id], skip_gain, chosen, turn_lengths[group_id])

    def attention_one(group_id):
        return attention_group(queries[group_id], turn_keys[group_id], turn_values[group_id], cache_keys[group_id], cache_values[group_id], sink_keys[group_id], sink_values[group_id], turn_lengths[group_id], history_lengths[group_id])
    group_ids = jnp.arange(DIALOG_BATCHES, dtype=jnp.int32)
    mixed = lax.map(mamba_one, group_ids)
    attended = lax.map(attention_one, group_ids)
    return (mixed, attended)
```

```python
import functools
import math

import jax
import jax.numpy as jnp
from jax import lax
from jax.experimental import pallas as pl
from jax.experimental.pallas import tpu as pltpu
from jax.sharding import PartitionSpec as P

TOK = 128
REACH = 4
SEQS = 3
SINKS = 4
H = 64
P_SIZE = 128
N = 64
G = 8
QH = 32
KVH = 4
HD = 128
WINDOW = 512
CTX = 32

F32 = jnp.float32
BF16 = jnp.bfloat16
I32 = jnp.int32
PAIR = 2 * P_SIZE
ROWS = N + 16
STEPS = 4
HEADS = H // STEPS
WIDE = HEADS * P_SIZE
BLOCKS = REACH + 1 + 1 + SEQS * 4 + 1
SINK_BLOCK = REACH + 1
CACHE_BLOCK = SINK_BLOCK + 1
NULL_BLOCK = BLOCKS - 1


def iota(shape, axis):
    return lax.broadcasted_iota(I32, shape, axis)


def nn(a, b):
    return lax.dot_general(a, b, (((1,), (0,)), ((), ())), preferred_element_type=F32)


def nt(a, b):
    return lax.dot_general(a, b, (((1,), (1,)), ((), ())), preferred_element_type=F32)


def starts_of(lengths):
    first = lengths[0, 0]
    return first, first + lengths[0, 1]


def segment(positions, one, two):
    return (positions >= one).astype(I32) + (positions >= two).astype(I32)


def same_causal(one, two):
    t, u = iota((TOK, TOK), 0), iota((TOK, TOK), 1)
    return (segment(t, one, two) == segment(u, one, two)) & (t >= u)


def spread_matrix(step):
    rows = iota((H, WIDE), 0)
    lanes = iota((H, WIDE), 1)
    return jnp.where(rows == step * HEADS + lanes // P_SIZE, 1.0, 0.0).astype(BF16)


def summary_kernel(lengths, x, dt, dlog, write, send, weight):
    step = pl.program_id(0)
    first = lax.axis_index("ctx") * TOK
    one, two = starts_of(lengths)
    one, two = one - first, two - first
    mask = jnp.where(same_causal(one, two), 1.0, 0.0).astype(BF16)
    rates = dlog[...]

    @pl.when(step == 0)
    def _():
        run = nn(mask, rates).T
        u = iota((1, TOK), 1)
        last = (TOK - 1 >= one).astype(I32) + (TOK - 1 >= two).astype(I32)
        held = segment(u, one, two) == last
        gap = jnp.where(held, run[:, TOK - 1 :] - run, -jnp.inf)
        weight[...] = jnp.exp(gap) * dt[...].astype(F32).T

    turned = write[...].astype(F32).T
    for k in range(HEADS):
        row = weight[pl.ds(step * HEADS + k, 1), :]
        b = k // G
        loads = (row * turned[b * N : (b + 1) * N]).astype(BF16)
        made = nn(loads, x[:, k * P_SIZE : (k + 1) * P_SIZE])
        lane = (k % 2) * P_SIZE
        send[k // 2, :N, lane : lane + P_SIZE] = made.astype(BF16)
    spread = nn(rates, spread_matrix(step)).astype(BF16)
    carry = jnp.exp(nn(mask[TOK - 16 :], spread)[15:16])
    high = carry.astype(BF16).astype(F32)
    low = carry - high
    tile = iota((16, PAIR), 0)
    for j in range(HEADS // 2):
        lanes = slice(j * PAIR, (j + 1) * PAIR)
        part = jnp.where(tile == 0, high[:, lanes], jnp.where(tile == 1, low[:, lanes], 0.0))
        send[j, N:, :] = part.astype(BF16)


def scan_kernel(home, lengths, recv, stored, entering, extra):
    group = lax.axis_index("sess")
    one, two = starts_of(lengths)
    back = [stored[home[group * SEQS + s]].astype(F32) for s in range(SEQS)]
    extra[0] = back[1].astype(BF16)
    extra[1] = back[2].astype(BF16)

    def turn(c, state):
        entering[c] = state.astype(BF16)
        end = c * TOK + TOK - 1
        inside_one = (end >= one) & (end < two) & (one >= c * TOK)
        inside_two = (end >= two) & (two >= c * TOK)
        base = jnp.where(inside_two, back[2], jnp.where(inside_one, back[1], state))
        carry = recv[c, N : N + 16, :].astype(F32)
        return (carry[0:1] + carry[1:2]) * base + recv[c, :N, :].astype(F32)

    lax.fori_loop(0, CTX, turn, back[0])


def output_kernel(lengths, x, dt, dlog, write, read, gain, state, extra, out, run_rows, step_rows):
    step = pl.program_id(0)
    first = lax.axis_index("ctx") * TOK
    one, two = starts_of(lengths)
    one, two = one - first, two - first
    seen = same_causal(one, two)
    mask = jnp.where(seen, 1.0, 0.0).astype(BF16)
    bias = jnp.where(seen, 0.0, -jnp.inf)
    rates = dlog[...]

    @pl.when(step == 0)
    def _():
        run_rows[...] = nn(mask, rates).T
        step_rows[...] = dt[...].astype(F32).T

    t = iota((TOK, N), 0)
    new_one = (t >= one) & (t < two) & (one >= 0)
    new_two = (t >= two) & (two >= 0)
    spread = nn(rates, spread_matrix(step)).astype(BF16)
    run = nn(mask, spread)
    for b in range(HEADS // G):
        c = read[:, b * N : (b + 1) * N].astype(F32)
        c_in = jnp.where(new_one | new_two, 0.0, c).astype(BF16)
        c_one = jnp.where(new_one, c, 0.0).astype(BF16)
        c_two = jnp.where(new_two, c, 0.0).astype(BF16)
        both = nt(read[:, b * N : (b + 1) * N], write[:, b * N : (b + 1) * N])
        for j in range(G // 2):
            chunk = b * (G // 2) + j
            from_state = (
                nn(c_in, state[chunk]) + nn(c_one, extra[chunk, 0]) + nn(c_two, extra[chunk, 1])
            )
            for i in range(2):
                k = chunk * 2 + i
                lanes = slice(k * P_SIZE, (k + 1) * P_SIZE)
                at = pl.ds(step * HEADS + k, 1)
                run_t = run[:, lanes]
                decay = jnp.exp(run_t - run_rows[at, :] + bias)
                mixing = (both * decay * step_rows[at, :]).astype(BF16)
                x_h = x[:, lanes]
                result = (
                    nn(mixing, x_h)
                    + jnp.exp(run_t) * from_state[:, i * P_SIZE : (i + 1) * P_SIZE]
                    + gain[:, lanes] * x_h.astype(F32)
                )
                out[:, lanes] = result.astype(BF16)


def attention_kernel(
    lengths,
    history,
    queries,
    band,
    sinks,
    cache,
    out,
    keys,
    rows,
    scores,
    top,
    total,
    sums,
    bias,
    listed,
    sems,
):
    place = lax.axis_index("ctx")
    first = place * TOK
    one, two = starts_of(lengths)
    copies = [
        pltpu.make_async_copy(band, keys.at[pl.ds(0, 8 * SINK_BLOCK)], sems.at[0]),
        pltpu.make_async_copy(sinks, keys.at[pl.ds(8 * SINK_BLOCK, 8)], sems.at[1]),
    ]
    for s in range(SEQS):
        for kv in range(2):
            copies.append(
                pltpu.make_async_copy(
                    cache.at[:, kv, s],
                    keys.at[pl.ds(8 * CACHE_BLOCK + 32 * s, 32), :, pl.ds(kv * KVH * HD, KVH * HD)],
                    sems.at[2 + 2 * s + kv],
                )
            )
    for copy in copies:
        copy.start()
    keys[8 * NULL_BLOCK :] = jnp.zeros((8, 16, 2 * KVH * HD), BF16)

    t = first + iota((TOK, TOK), 0)
    u = iota((TOK, TOK), 1)
    owner = segment(t, one, two)
    offset = t - jnp.where(owner == 2, two, jnp.where(owner == 1, one, 0))
    count = jnp.int32(0)
    head_owner = (first >= one).astype(I32) + (first >= two).astype(I32)
    for b in range(REACH + 1):
        pos = first + (b - REACH) * TOK + u
        gap = t - pos
        ok = (pos >= 0) & (segment(pos, one, two) == owner) & (gap >= 0) & (gap < WINDOW)
        bias[b] = jnp.where(ok, 0.0, -jnp.inf)
        end = first + (b - REACH) * TOK + TOK - 1
        end_owner = (end >= one).astype(I32) + (end >= two).astype(I32)
        live = (end >= 0) & (end_owner >= head_owner)
        listed[count] = b
        count = count + live.astype(I32)
    bias[SINK_BLOCK] = jnp.where(
        (u < SEQS * SINKS) & (u // SINKS == owner), 0.0, -jnp.inf
    )
    listed[count] = SINK_BLOCK
    count = count + 1
    edges = [jnp.int32(0), one, two, jnp.int32(CTX * TOK)]
    for s in range(SEQS):
        begin = jnp.maximum(edges[s], first)
        present = begin < jnp.minimum(edges[s + 1], first + TOK)
        for j in range(4):
            live = (
                present
                & (begin - edges[s] < j * TOK + TOK - 1)
                & (history[0, s] - WINDOW + j * TOK + TOK - 1 >= SINKS)
            )
            block = CACHE_BLOCK + 4 * s + j

            @pl.when(live)
            def _():
                slot = j * TOK + u
                ok = (owner == s) & (slot > offset) & (history[0, s] - WINDOW + slot >= SINKS)
                bias[block] = jnp.where(ok, 0.0, -jnp.inf)

            listed[count] = block
            count = count + live.astype(I32)
    bias[NULL_BLOCK] = jnp.full((TOK, TOK), -jnp.inf, F32)
    listed[count] = NULL_BLOCK
    pairs = lax.div(count + 1, jnp.int32(2))
    for copy in copies:
        copy.wait()

    per = QH // KVH
    scale = 1.0 / math.sqrt(HD) / math.log(2.0)

    def one_head(number, nothing):
        lanes = pl.ds(pl.multiple_of(number * HD, HD), HD)
        value_lanes = pl.ds(pl.multiple_of(number * HD + KVH * HD, HD), HD)
        for r in range(per):
            wide = pl.ds(pl.multiple_of((number * per + r) * HD, HD), HD)
            rows[r * TOK : (r + 1) * TOK, :] = queries[:, wide]
        top[...] = jnp.full(top.shape, -jnp.inf, F32)
        total[...] = jnp.zeros(total.shape, F32)
        sums[...] = jnp.zeros(sums.shape, F32)

        def score(i, nothing):
            for part in range(2):
                block = listed[2 * i + part]
                key = keys[pl.ds(block * 8, 8), :, lanes].reshape(TOK, HD)
                offset_rows = bias[block]
                for r in range(per):
                    at = slice(r * TOK, (r + 1) * TOK)
                    got = nt(rows[at, :], key) * scale + offset_rows
                    scores[2 * i + part, at, :] = got
                    top[at, :] = jnp.maximum(top[at, :], got)
            return nothing

        lax.fori_loop(0, pairs, score, 0)
        top[...] = jnp.broadcast_to(jnp.max(top[...], axis=1, keepdims=True), top.shape)

        def weigh(i, nothing):
            values = []
            for part in range(2):
                block = listed[2 * i + part]
                values.append(keys[pl.ds(block * 8, 8), :, value_lanes].reshape(TOK, HD))
            value = jnp.concatenate(values, axis=0)
            for r in range(per):
                at = slice(r * TOK, (r + 1) * TOK)
                left = jnp.exp2(scores[2 * i, at, :] - top[at, :])
                right = jnp.exp2(scores[2 * i + 1, at, :] - top[at, :])
                total[at, :] += left + right
                both = jnp.concatenate([left.astype(BF16), right.astype(BF16)], axis=1)
                sums[at, :] += nn(both, value)
            return nothing

        lax.fori_loop(0, pairs, weigh, 0)
        for r in range(per):
            at = slice(r * TOK, (r + 1) * TOK)
            whole = jnp.sum(total[at, :], axis=1, keepdims=True)
            wide = pl.ds(pl.multiple_of((number * per + r) * HD, HD), HD)
            out[:, wide] = (sums[at, :] / whole).astype(BF16)
        return nothing

    lax.fori_loop(0, KVH, one_head, 0)


SMEM = pl.BlockSpec(memory_space=pltpu.SMEM)
VMEM = pl.BlockSpec(memory_space=pltpu.VMEM)
ANY = pl.BlockSpec(memory_space=pl.ANY)
LIMIT = pltpu.CompilerParams(vmem_limit_bytes=48 * 2**20)


def full(shape):
    return pl.BlockSpec(shape, lambda i: (0,) * len(shape))


def lane_block(rows, width):
    return pl.BlockSpec((rows, width), lambda i: (0, i))


def summaries(lengths, x, dt, dlog, write):
    return pl.pallas_call(
        summary_kernel,
        grid=(STEPS,),
        out_shape=jax.ShapeDtypeStruct((CTX, ROWS, PAIR), BF16),
        in_specs=[
            SMEM,
            lane_block(TOK, WIDE),
            full((TOK, H)),
            full((TOK, H)),
            lane_block(TOK, 2 * N),
        ],
        out_specs=pl.BlockSpec((CTX // STEPS, ROWS, PAIR), lambda i: (i, 0, 0)),
        scratch_shapes=[pltpu.VMEM((H, TOK), F32)],
        compiler_params=LIMIT,
    )(lengths, x, dt, dlog, write)


def scan(home, lengths, recv, stored):
    return pl.pallas_call(
        scan_kernel,
        out_shape=(
            jax.ShapeDtypeStruct((CTX, N, PAIR), BF16),
            jax.ShapeDtypeStruct((2, N, PAIR), BF16),
        ),
        in_specs=[SMEM, SMEM, VMEM, VMEM],
        out_specs=(VMEM, VMEM),
        compiler_params=LIMIT,
    )(home, lengths, recv, stored)


def outputs(lengths, x, dt, dlog, write, read, gain, state, extra):
    return pl.pallas_call(
        output_kernel,
        grid=(STEPS,),
        out_shape=jax.ShapeDtypeStruct((TOK, H * P_SIZE), BF16),
        in_specs=[
            SMEM,
            lane_block(TOK, WIDE),
            full((TOK, H)),
            full((TOK, H)),
            lane_block(TOK, 2 * N),
            lane_block(TOK, 2 * N),
            lane_block(1, WIDE),
            pl.BlockSpec((CTX // STEPS, N, PAIR), lambda i: (i, 0, 0)),
            pl.BlockSpec((CTX // STEPS, 2, N, PAIR), lambda i: (i, 0, 0, 0)),
        ],
        out_specs=lane_block(TOK, WIDE),
        scratch_shapes=[pltpu.VMEM((H, TOK), F32), pltpu.VMEM((H, TOK), F32)],
        compiler_params=LIMIT,
    )(lengths, x, dt, dlog, write, read, gain, state, extra)


def attention(lengths, history, queries, band, sinks, cache):
    rows = (QH // KVH) * TOK
    return pl.pallas_call(
        attention_kernel,
        out_shape=jax.ShapeDtypeStruct((TOK, QH * HD), BF16),
        in_specs=[SMEM, SMEM, VMEM, ANY, ANY, ANY],
        out_specs=VMEM,
        scratch_shapes=[
            pltpu.VMEM((8 * BLOCKS, 16, 2 * KVH * HD), BF16),
            pltpu.VMEM((rows, HD), BF16),
            pltpu.VMEM((BLOCKS + 1, rows, TOK), F32),
            pltpu.VMEM((rows, TOK), F32),
            pltpu.VMEM((rows, TOK), F32),
            pltpu.VMEM((rows, HD), F32),
            pltpu.VMEM((BLOCKS, TOK, TOK), F32),
            pltpu.SMEM((BLOCKS + 1,), I32),
            pltpu.SemaphoreType.DMA((8,)),
        ],
        compiler_params=LIMIT,
        cost_estimate=pl.CostEstimate(
            flops=2_500_000_000, bytes_accessed=8_000_000, transcendentals=5_000_000
        ),
    )(lengths, history, queries, band, sinks, cache)


def shifted(block, distance):
    route = [(i - distance, i) for i in range(distance, CTX)]
    return lax.ppermute(block, "ctx", route)


def shards(
    mamba_input,
    step_size,
    decay_log,
    state_write,
    state_read,
    skip_gain,
    saved_states,
    home_slot,
    turn_lengths,
    history_lengths,
    queries,
    turn_keys,
    turn_values,
    cache_keys,
    cache_values,
    sink_keys,
    sink_values,
):
    x, dt, dlog = mamba_input[0], step_size[0], decay_log[0]
    write, read = state_write[0], state_read[0]
    saved = saved_states[0].astype(BF16).reshape(SEQS, 2, P_SIZE, N)
    saved = saved.transpose(0, 3, 1, 2).reshape(SEQS, N, PAIR)
    stored = lax.all_gather(saved, "sess", axis=0, tiled=True)
    cache = jnp.stack([cache_keys[0], cache_values[0]])
    cache = lax.all_gather(cache, "ctx", axis=0)
    key_value = jnp.concatenate([turn_keys[0], turn_values[0]], axis=1)
    band = [shifted(key_value, d) for d in range(REACH, 0, -1)] + [key_value]
    band = jnp.concatenate(band, axis=0).reshape(8 * (REACH + 1), 16, 2 * KVH * HD)
    sinks = jnp.concatenate(
        [sink_keys[0].reshape(SEQS * SINKS, -1), sink_values[0].reshape(SEQS * SINKS, -1)], axis=1
    )
    sinks = jnp.pad(sinks, ((0, TOK - SEQS * SINKS), (0, 0))).reshape(8, 16, 2 * KVH * HD)
    gain = jnp.repeat(skip_gain, P_SIZE)[None]

    send = summaries(turn_lengths, x, dt, dlog, write)
    recv = lax.all_to_all(send, "ctx", 0, 0, tiled=True)
    entering, extra = scan(home_slot, turn_lengths, recv, stored)
    state = lax.all_to_all(entering, "ctx", 0, 0, tiled=True)
    extras = lax.all_gather(extra, "ctx", axis=0)
    attended = attention(turn_lengths, history_lengths, queries[0], band, sinks, cache)
    mixed = outputs(turn_lengths, x, dt, dlog, write, read, gain, state, extras)
    return (mixed[None], attended[None])


def solution(mesh):
    token = P("sess", "ctx", None)
    spread = P("sess", None, "ctx", None)
    return jax.shard_map(
        shards,
        mesh=mesh,
        in_specs=(
            token,
            token,
            token,
            token,
            token,
            P(),
            spread,
            P(),
            P("sess", None),
            P("sess", None),
            token,
            token,
            token,
            spread,
            spread,
            P("sess", None, None, None),
            P("sess", None, None, None),
        ),
        out_specs=(token, token),
        check_vma=False,
    )
```

```python
import functools
import math

import jax
import jax.numpy as jnp
from jax import lax
from jax.experimental import pallas as pl
from jax.experimental.pallas import tpu as pltpu
from jax.sharding import PartitionSpec as P

TOK = 128
REACH = 4
SEQS = 3
SINKS = 4
H = 64
P_SIZE = 128
N = 64
G = 8
QH = 32
KVH = 4
HD = 128
WINDOW = 512
CTX = 32
MESH = pl.DeviceIdType.MESH

F32 = jnp.float32
BF16 = jnp.bfloat16
I32 = jnp.int32
PAIR = 2 * P_SIZE
ROWS = N + 16
STEPS = 4
HEADS = H // STEPS
WIDE = HEADS * P_SIZE
BLOCKS = REACH + 1 + 1 + SEQS * 4 + 1
SINK_BLOCK = REACH + 1
CACHE_BLOCK = SINK_BLOCK + 1
NULL_BLOCK = BLOCKS - 1


def iota(shape, axis):
    return lax.broadcasted_iota(I32, shape, axis)


def nn(a, b):
    return lax.dot_general(a, b, (((1,), (0,)), ((), ())), preferred_element_type=F32)


def nt(a, b):
    return lax.dot_general(a, b, (((1,), (1,)), ((), ())), preferred_element_type=F32)


def starts_of(lengths):
    first = lengths[0, 0]
    return first, first + lengths[0, 1]


def segment(positions, one, two):
    return (positions >= one).astype(I32) + (positions >= two).astype(I32)


def same_causal(one, two):
    t, u = iota((TOK, TOK), 0), iota((TOK, TOK), 1)
    return (segment(t, one, two) == segment(u, one, two)) & (t >= u)


def spread_matrix(step):
    rows = iota((H, WIDE), 0)
    lanes = iota((H, WIDE), 1)
    return jnp.where(rows == step * HEADS + lanes // P_SIZE, 1.0, 0.0).astype(BF16)


def summary_kernel(lengths, x, dt, dlog, write, send, weight):
    step = pl.program_id(0)
    first = lax.axis_index("ctx") * TOK
    one, two = starts_of(lengths)
    one, two = one - first, two - first
    mask = jnp.where(same_causal(one, two), 1.0, 0.0).astype(BF16)
    rates = dlog[...]

    @pl.when(step == 0)
    def _():
        run = nn(mask, rates).T
        u = iota((1, TOK), 1)
        last = (TOK - 1 >= one).astype(I32) + (TOK - 1 >= two).astype(I32)
        held = segment(u, one, two) == last
        gap = jnp.where(held, run[:, TOK - 1 :] - run, -jnp.inf)
        weight[...] = jnp.exp(gap) * dt[...].astype(F32).T

    turned = write[...].astype(F32).T
    for k in range(HEADS):
        row = weight[pl.ds(step * HEADS + k, 1), :]
        b = k // G
        loads = (row * turned[b * N : (b + 1) * N]).astype(BF16)
        made = nn(loads, x[:, k * P_SIZE : (k + 1) * P_SIZE])
        lane = (k % 2) * P_SIZE
        send[k // 2, :N, lane : lane + P_SIZE] = made.astype(BF16)
    spread = nn(rates, spread_matrix(step)).astype(BF16)
    carry = jnp.exp(nn(mask[TOK - 16 :], spread)[15:16])
    high = carry.astype(BF16).astype(F32)
    low = carry - high
    tile = iota((16, PAIR), 0)
    for j in range(HEADS // 2):
        lanes = slice(j * PAIR, (j + 1) * PAIR)
        part = jnp.where(tile == 0, high[:, lanes], jnp.where(tile == 1, low[:, lanes], 0.0))
        send[j, N:, :] = part.astype(BF16)


def await_bytes(ref, sem):
    pltpu.make_async_copy(ref, ref, sem).wait()


def exchange_kernel(
    home,
    lengths,
    saved,
    send,
    cache,
    key_value,
    state,
    extras,
    caches,
    band,
    recv,
    stored,
    entering,
    extra,
    sent,
    got,
    local,
):
    group, me = lax.axis_index("sess"), lax.axis_index("ctx")
    groups = lax.axis_size("sess")
    y, z, core = me // 8, (me // 2) % 4, me % 2
    sibling = me + 1 - 2 * core
    z_peers = [y * 8 + ((z + i) % 4) * 2 + core for i in range(1, 4)]
    y_peers = [((y + i) % 4) * 8 + z * 2 + core for i in range(1, 4)]
    KIND = {name: i for i, name in enumerate(EXCHANGES)}

    barrier = pltpu.get_barrier_semaphore()

    def greet(i, nothing):
        pl.semaphore_signal(barrier, inc=1, device_id=(group, (me + i) % CTX), device_id_type=MESH)
        return nothing

    lax.fori_loop(1, CTX, greet, 0)
    for i in range(1, groups):
        pl.semaphore_signal(
            barrier, inc=1, device_id=((group + i) % groups, me), device_id_type=MESH
        )
    pl.semaphore_wait(barrier, CTX - 1 + groups - 1)

    def push(kind, src, dst, peer, to=None):
        at = KIND[kind]
        pltpu.make_async_remote_copy(
            src_ref=src,
            dst_ref=dst,
            send_sem=sent.at[at],
            recv_sem=got.at[at],
            device_id=(group if to is None else to, peer),
            device_id_type=MESH,
        ).start()

    keep = []

    def hold(src, dst):
        copy = pltpu.make_async_copy(src, dst, local.at[len(keep)])
        copy.start()
        keep.append(copy)
        return copy

    for i in range(1, groups):
        push("home", saved, stored.at[group], me, (group + i) % groups)
    own_saved = hold(saved, stored.at[group])

    def pass_summary(i, nothing):
        peer = (me + i) % CTX
        push("summary", send.at[peer], recv.at[me], peer)
        return nothing

    lax.fori_loop(1, CTX, pass_summary, 0)
    own_summary = hold(send.at[me], recv.at[me])
    for peer in z_peers:
        push("cache_z", cache, caches.at[me], peer)
    for peer in y_peers:
        push("cache_y", cache, caches.at[me], peer)
    push("cache_core", cache, caches.at[me], sibling)
    own_cache = hold(cache, caches.at[me])
    for d in range(1, REACH + 1):
        push("band", key_value, band.at[pl.ds(8 * (REACH - d), 8)], (me + d) % CTX)
    own_band = hold(key_value, band.at[pl.ds(8 * REACH, 8)])

    def spread_z(name, array):
        for peer in z_peers:
            for to in y_peers:
                push(name + "_y", array.at[peer], array.at[peer], to)
            push(name + "_core", array.at[peer], array.at[peer], sibling)

    def spread_y(name, array):
        for i in range(4):
            for j in range(1, 4):
                at = ((y + j) % 4) * 8 + ((z + i) % 4) * 2 + core
                push(name + "_core", array.at[at], array.at[at], sibling)

    await_bytes(stored.at[pl.ds(0, groups - 1)], got.at[KIND["home"]])
    own_saved.wait()
    back = []
    for s in range(SEQS):
        at = home[group * SEQS + s]
        back.append(stored[at // SEQS, at % SEQS].astype(F32))
    extra[0] = back[1].astype(BF16)
    extra[1] = back[2].astype(BF16)
    for peer in z_peers:
        push("extra_z", extra, extras.at[me], peer)
    for peer in y_peers:
        push("extra_y", extra, extras.at[me], peer)
    push("extra_core", extra, extras.at[me], sibling)
    own_extra = hold(extra, extras.at[me])

    await_bytes(recv.at[pl.ds(0, CTX - 1)], got.at[KIND["summary"]])
    own_summary.wait()
    one, two = starts_of(lengths)

    def turn(c, held):
        entering[c] = held.astype(BF16)

        @pl.when(c != me)
        def _():
            push("state", entering.at[c], state.at[me], c)

        end = c * TOK + TOK - 1
        inside_one = (end >= one) & (end < two) & (one >= c * TOK)
        inside_two = (end >= two) & (two >= c * TOK)
        base = jnp.where(inside_two, back[2], jnp.where(inside_one, back[1], held))
        carry = recv[c, N : N + 16, :].astype(F32)
        return (carry[0:1] + carry[1:2]) * base + recv[c, :N, :].astype(F32)

    lax.fori_loop(0, CTX, turn, back[0])
    own_state = hold(entering.at[me], state.at[me])

    await_bytes(caches.at[pl.ds(0, 3)], got.at[KIND["cache_z"]])
    spread_z("cache", caches)
    await_bytes(extras.at[pl.ds(0, 3)], got.at[KIND["extra_z"]])
    spread_z("extra", extras)
    await_bytes(caches.at[pl.ds(0, 12)], got.at[KIND["cache_y"]])
    spread_y("cache", caches)
    await_bytes(extras.at[pl.ds(0, 12)], got.at[KIND["extra_y"]])
    spread_y("extra", extras)

    await_bytes(caches.at[pl.ds(0, 16)], got.at[KIND["cache_core"]])
    await_bytes(extras.at[pl.ds(0, 16)], got.at[KIND["extra_core"]])
    await_bytes(state.at[pl.ds(0, CTX - 1)], got.at[KIND["state"]])
    await_bytes(band.at[pl.ds(0, 8 * REACH)], got.at[KIND["band"]])
    for copy in (own_cache, own_band, own_extra, own_state):
        copy.wait()
    for kind, ref in (
        ("home", stored.at[pl.ds(0, groups - 1)]),
        ("summary", recv.at[pl.ds(0, CTX - 1)]),
        ("state", state.at[pl.ds(0, CTX - 1)]),
        ("band", band.at[pl.ds(0, 8 * REACH)]),
        ("cache_z", caches.at[pl.ds(0, 3)]),
        ("cache_y", caches.at[pl.ds(0, 12)]),
        ("cache_core", caches.at[pl.ds(0, 16)]),
        ("extra_z", extras.at[pl.ds(0, 3)]),
        ("extra_y", extras.at[pl.ds(0, 12)]),
        ("extra_core", extras.at[pl.ds(0, 16)]),
    ):
        await_bytes(ref, sent.at[KIND[kind]])


EXCHANGES = (
    "home",
    "summary",
    "state",
    "band",
    "cache_z",
    "cache_y",
    "cache_core",
    "extra_z",
    "extra_y",
    "extra_core",
)


def output_kernel(lengths, x, dt, dlog, write, read, gain, state, extra, out, run_rows, step_rows):
    step = pl.program_id(0)
    first = lax.axis_index("ctx") * TOK
    one, two = starts_of(lengths)
    one, two = one - first, two - first
    seen = same_causal(one, two)
    mask = jnp.where(seen, 1.0, 0.0).astype(BF16)
    bias = jnp.where(seen, 0.0, -jnp.inf)
    rates = dlog[...]

    @pl.when(step == 0)
    def _():
        run_rows[...] = nn(mask, rates).T
        step_rows[...] = dt[...].astype(F32).T

    t = iota((TOK, N), 0)
    new_one = (t >= one) & (t < two) & (one >= 0)
    new_two = (t >= two) & (two >= 0)
    spread = nn(rates, spread_matrix(step)).astype(BF16)
    run = nn(mask, spread)
    for b in range(HEADS // G):
        c = read[:, b * N : (b + 1) * N].astype(F32)
        c_in = jnp.where(new_one | new_two, 0.0, c).astype(BF16)
        c_one = jnp.where(new_one, c, 0.0).astype(BF16)
        c_two = jnp.where(new_two, c, 0.0).astype(BF16)
        both = nt(read[:, b * N : (b + 1) * N], write[:, b * N : (b + 1) * N])
        for j in range(G // 2):
            chunk = b * (G // 2) + j
            from_state = (
                nn(c_in, state[chunk]) + nn(c_one, extra[chunk, 0]) + nn(c_two, extra[chunk, 1])
            )
            for i in range(2):
                k = chunk * 2 + i
                lanes = slice(k * P_SIZE, (k + 1) * P_SIZE)
                at = pl.ds(step * HEADS + k, 1)
                run_t = run[:, lanes]
                decay = jnp.exp(run_t - run_rows[at, :] + bias)
                mixing = (both * decay * step_rows[at, :]).astype(BF16)
                x_h = x[:, lanes]
                result = (
                    nn(mixing, x_h)
                    + jnp.exp(run_t) * from_state[:, i * P_SIZE : (i + 1) * P_SIZE]
                    + gain[:, lanes] * x_h.astype(F32)
                )
                out[:, lanes] = result.astype(BF16)


def attention_kernel(
    lengths,
    history,
    queries,
    band,
    sinks,
    cache,
    out,
    keys,
    rows,
    scores,
    top,
    total,
    sums,
    bias,
    listed,
    sems,
):
    place = lax.axis_index("ctx")
    first = place * TOK
    one, two = starts_of(lengths)
    copies = [
        pltpu.make_async_copy(band, keys.at[pl.ds(0, 8 * SINK_BLOCK)], sems.at[0]),
        pltpu.make_async_copy(sinks, keys.at[pl.ds(8 * SINK_BLOCK, 8)], sems.at[1]),
    ]
    for s in range(SEQS):
        for kv in range(2):
            copies.append(
                pltpu.make_async_copy(
                    cache.at[:, kv, s],
                    keys.at[pl.ds(8 * CACHE_BLOCK + 32 * s, 32), :, pl.ds(kv * KVH * HD, KVH * HD)],
                    sems.at[2 + 2 * s + kv],
                )
            )
    for copy in copies:
        copy.start()
    keys[8 * NULL_BLOCK :] = jnp.zeros((8, 16, 2 * KVH * HD), BF16)

    t = first + iota((TOK, TOK), 0)
    u = iota((TOK, TOK), 1)
    owner = segment(t, one, two)
    offset = t - jnp.where(owner == 2, two, jnp.where(owner == 1, one, 0))
    count = jnp.int32(0)
    head_owner = (first >= one).astype(I32) + (first >= two).astype(I32)
    for b in range(REACH + 1):
        pos = first + (b - REACH) * TOK + u
        gap = t - pos
        ok = (pos >= 0) & (segment(pos, one, two) == owner) & (gap >= 0) & (gap < WINDOW)
        bias[b] = jnp.where(ok, 0.0, -jnp.inf)
        end = first + (b - REACH) * TOK + TOK - 1
        end_owner = (end >= one).astype(I32) + (end >= two).astype(I32)
        live = (end >= 0) & (end_owner >= head_owner)
        listed[count] = b
        count = count + live.astype(I32)
    bias[SINK_BLOCK] = jnp.where(
        (u < SEQS * SINKS) & (u // SINKS == owner), 0.0, -jnp.inf
    )
    listed[count] = SINK_BLOCK
    count = count + 1
    edges = [jnp.int32(0), one, two, jnp.int32(CTX * TOK)]
    for s in range(SEQS):
        begin = jnp.maximum(edges[s], first)
        present = begin < jnp.minimum(edges[s + 1], first + TOK)
        for j in range(4):
            live = (
                present
                & (begin - edges[s] < j * TOK + TOK - 1)
                & (history[0, s] - WINDOW + j * TOK + TOK - 1 >= SINKS)
            )
            block = CACHE_BLOCK + 4 * s + j

            @pl.when(live)
            def _():
                slot = j * TOK + u
                ok = (owner == s) & (slot > offset) & (history[0, s] - WINDOW + slot >= SINKS)
                bias[block] = jnp.where(ok, 0.0, -jnp.inf)

            listed[count] = block
            count = count + live.astype(I32)
    bias[NULL_BLOCK] = jnp.full((TOK, TOK), -jnp.inf, F32)
    listed[count] = NULL_BLOCK
    pairs = lax.div(count + 1, jnp.int32(2))
    for copy in copies:
        copy.wait()

    per = QH // KVH
    scale = 1.0 / math.sqrt(HD) / math.log(2.0)

    def one_head(number, nothing):
        lanes = pl.ds(pl.multiple_of(number * HD, HD), HD)
        value_lanes = pl.ds(pl.multiple_of(number * HD + KVH * HD, HD), HD)
        for r in range(per):
            wide = pl.ds(pl.multiple_of((number * per + r) * HD, HD), HD)
            rows[r * TOK : (r + 1) * TOK, :] = queries[:, wide]
        top[...] = jnp.full(top.shape, -jnp.inf, F32)
        total[...] = jnp.zeros(total.shape, F32)
        sums[...] = jnp.zeros(sums.shape, F32)

        def score(i, nothing):
            for part in range(2):
                block = listed[2 * i + part]
                key = keys[pl.ds(block * 8, 8), :, lanes].reshape(TOK, HD)
                offset_rows = bias[block]
                for r in range(per):
                    at = slice(r * TOK, (r + 1) * TOK)
                    got = nt(rows[at, :], key) * scale + offset_rows
                    scores[2 * i + part, at, :] = got
                    top[at, :] = jnp.maximum(top[at, :], got)
            return nothing

        lax.fori_loop(0, pairs, score, 0)
        top[...] = jnp.broadcast_to(jnp.max(top[...], axis=1, keepdims=True), top.shape)

        def weigh(i, nothing):
            values = []
            for part in range(2):
                block = listed[2 * i + part]
                values.append(keys[pl.ds(block * 8, 8), :, value_lanes].reshape(TOK, HD))
            value = jnp.concatenate(values, axis=0)
            for r in range(per):
                at = slice(r * TOK, (r + 1) * TOK)
                left = jnp.exp2(scores[2 * i, at, :] - top[at, :])
                right = jnp.exp2(scores[2 * i + 1, at, :] - top[at, :])
                total[at, :] += left + right
                both = jnp.concatenate([left.astype(BF16), right.astype(BF16)], axis=1)
                sums[at, :] += nn(both, value)
            return nothing

        lax.fori_loop(0, pairs, weigh, 0)
        for r in range(per):
            at = slice(r * TOK, (r + 1) * TOK)
            whole = jnp.sum(total[at, :], axis=1, keepdims=True)
            wide = pl.ds(pl.multiple_of((number * per + r) * HD, HD), HD)
            out[:, wide] = (sums[at, :] / whole).astype(BF16)
        return nothing

    lax.fori_loop(0, KVH, one_head, 0)


SMEM = pl.BlockSpec(memory_space=pltpu.SMEM)
VMEM = pl.BlockSpec(memory_space=pltpu.VMEM)
ANY = pl.BlockSpec(memory_space=pl.ANY)
LIMIT = pltpu.CompilerParams(vmem_limit_bytes=48 * 2**20)


def full(shape):
    return pl.BlockSpec(shape, lambda i: (0,) * len(shape))


def lane_block(rows, width):
    return pl.BlockSpec((rows, width), lambda i: (0, i))


def summaries(lengths, x, dt, dlog, write):
    return pl.pallas_call(
        summary_kernel,
        grid=(STEPS,),
        out_shape=jax.ShapeDtypeStruct((CTX, ROWS, PAIR), BF16),
        in_specs=[
            SMEM,
            lane_block(TOK, WIDE),
            full((TOK, H)),
            full((TOK, H)),
            lane_block(TOK, 2 * N),
        ],
        out_specs=pl.BlockSpec((CTX // STEPS, ROWS, PAIR), lambda i: (i, 0, 0)),
        scratch_shapes=[pltpu.VMEM((H, TOK), F32)],
        compiler_params=LIMIT,
    )(lengths, x, dt, dlog, write)


def exchange(groups, home, lengths, saved, send, cache, key_value):
    return pl.pallas_call(
        exchange_kernel,
        out_shape=(
            jax.ShapeDtypeStruct((CTX, N, PAIR), BF16),
            jax.ShapeDtypeStruct((CTX, 2, N, PAIR), BF16),
            jax.ShapeDtypeStruct((CTX,) + cache.shape, BF16),
            jax.ShapeDtypeStruct((8 * (REACH + 1), 16, 2 * KVH * HD), BF16),
        ),
        in_specs=[SMEM, SMEM, ANY, ANY, ANY, ANY],
        out_specs=(ANY, ANY, ANY, ANY),
        scratch_shapes=[
            pltpu.VMEM((CTX, ROWS, PAIR), BF16),
            pltpu.VMEM((groups, SEQS, N, PAIR), BF16),
            pltpu.VMEM((CTX, N, PAIR), BF16),
            pltpu.VMEM((2, N, PAIR), BF16),
            pltpu.SemaphoreType.DMA((len(EXCHANGES),)),
            pltpu.SemaphoreType.DMA((len(EXCHANGES),)),
            pltpu.SemaphoreType.DMA((6,)),
        ],
        compiler_params=pltpu.CompilerParams(
            collective_id=0, has_side_effects=True, vmem_limit_bytes=48 * 2**20
        ),
    )(home, lengths, saved, send, cache, key_value)


def outputs(lengths, x, dt, dlog, write, read, gain, state, extra):
    return pl.pallas_call(
        output_kernel,
        grid=(STEPS,),
        out_shape=jax.ShapeDtypeStruct((TOK, H * P_SIZE), BF16),
        in_specs=[
            SMEM,
            lane_block(TOK, WIDE),
            full((TOK, H)),
            full((TOK, H)),
            lane_block(TOK, 2 * N),
            lane_block(TOK, 2 * N),
            lane_block(1, WIDE),
            pl.BlockSpec((CTX // STEPS, N, PAIR), lambda i: (i, 0, 0)),
            pl.BlockSpec((CTX // STEPS, 2, N, PAIR), lambda i: (i, 0, 0, 0)),
        ],
        out_specs=lane_block(TOK, WIDE),
        scratch_shapes=[pltpu.VMEM((H, TOK), F32), pltpu.VMEM((H, TOK), F32)],
        compiler_params=LIMIT,
    )(lengths, x, dt, dlog, write, read, gain, state, extra)


def attention(lengths, history, queries, band, sinks, cache):
    rows = (QH // KVH) * TOK
    return pl.pallas_call(
        attention_kernel,
        out_shape=jax.ShapeDtypeStruct((TOK, QH * HD), BF16),
        in_specs=[SMEM, SMEM, VMEM, ANY, ANY, ANY],
        out_specs=VMEM,
        scratch_shapes=[
            pltpu.VMEM((8 * BLOCKS, 16, 2 * KVH * HD), BF16),
            pltpu.VMEM((rows, HD), BF16),
            pltpu.VMEM((BLOCKS + 1, rows, TOK), F32),
            pltpu.VMEM((rows, TOK), F32),
            pltpu.VMEM((rows, TOK), F32),
            pltpu.VMEM((rows, HD), F32),
            pltpu.VMEM((BLOCKS, TOK, TOK), F32),
            pltpu.SMEM((BLOCKS + 1,), I32),
            pltpu.SemaphoreType.DMA((8,)),
        ],
        compiler_params=LIMIT,
        cost_estimate=pl.CostEstimate(
            flops=2_500_000_000, bytes_accessed=8_000_000, transcendentals=5_000_000
        ),
    )(lengths, history, queries, band, sinks, cache)


def shards(
    mamba_input,
    step_size,
    decay_log,
    state_write,
    state_read,
    skip_gain,
    saved_states,
    home_slot,
    turn_lengths,
    history_lengths,
    queries,
    turn_keys,
    turn_values,
    cache_keys,
    cache_values,
    sink_keys,
    sink_values,
):
    x, dt, dlog = mamba_input[0], step_size[0], decay_log[0]
    write, read = state_write[0], state_read[0]
    saved = saved_states[0].astype(BF16).reshape(SEQS, 2, P_SIZE, N)
    saved = saved.transpose(0, 3, 1, 2).reshape(SEQS, N, PAIR)
    cache = jnp.stack([cache_keys[0], cache_values[0]])
    key_value = jnp.concatenate([turn_keys[0], turn_values[0]], axis=1)
    key_value = key_value.reshape(8, 16, 2 * KVH * HD)
    sinks = jnp.concatenate(
        [sink_keys[0].reshape(SEQS * SINKS, -1), sink_values[0].reshape(SEQS * SINKS, -1)], axis=1
    )
    sinks = jnp.pad(sinks, ((0, TOK - SEQS * SINKS), (0, 0))).reshape(8, 16, 2 * KVH * HD)
    gain = jnp.repeat(skip_gain, P_SIZE)[None]

    send = summaries(turn_lengths, x, dt, dlog, write)
    groups = lax.axis_size("sess")
    state, extras, caches, band = exchange(
        groups, home_slot, turn_lengths, saved, send, cache, key_value
    )
    attended = attention(turn_lengths, history_lengths, queries[0], band, sinks, caches)
    mixed = outputs(turn_lengths, x, dt, dlog, write, read, gain, state, extras)
    return (mixed[None], attended[None])


def solution(mesh):
    token = P("sess", "ctx", None)
    spread = P("sess", None, "ctx", None)
    return jax.shard_map(
        shards,
        mesh=mesh,
        in_specs=(
            token,
            token,
            token,
            token,
            token,
            P(),
            spread,
            P(),
            P("sess", None),
            P("sess", None),
            token,
            token,
            token,
            spread,
            spread,
            P("sess", None, None, None),
            P("sess", None, None, None),
        ),
        out_specs=(token, token),
        check_vma=False,
    )
```

```python
import functools
import math

import jax
import jax.numpy as jnp
from jax import lax
from jax.experimental import pallas as pl
from jax.experimental.pallas import tpu as pltpu
from jax.sharding import PartitionSpec as P

TOK = 128
REACH = 4
SEQS = 3
SINKS = 4
H = 64
P_SIZE = 128
N = 64
G = 8
QH = 32
KVH = 4
HD = 128
WINDOW = 512
CTX = 32
CHIPS = CTX // 2
MESH = pl.DeviceIdType.MESH

F32 = jnp.float32
BF16 = jnp.bfloat16
I32 = jnp.int32
PAIR = 2 * P_SIZE
ROWS = N + 16
STEPS = 4
HEADS = H // STEPS
WIDE = HEADS * P_SIZE
BLOCKS = REACH + 1 + 1 + SEQS * 4 + 1
SINK_BLOCK = REACH + 1
CACHE_BLOCK = SINK_BLOCK + 1
NULL_BLOCK = BLOCKS - 1


def iota(shape, axis):
    return lax.broadcasted_iota(I32, shape, axis)


def nn(a, b):
    return lax.dot_general(a, b, (((1,), (0,)), ((), ())), preferred_element_type=F32)


def nt(a, b):
    return lax.dot_general(a, b, (((1,), (1,)), ((), ())), preferred_element_type=F32)


def starts_of(lengths):
    first = lengths[0, 0]
    return first, first + lengths[0, 1]


def segment(positions, one, two):
    return (positions >= one).astype(I32) + (positions >= two).astype(I32)


def same_causal(one, two):
    t, u = iota((TOK, TOK), 0), iota((TOK, TOK), 1)
    return (segment(t, one, two) == segment(u, one, two)) & (t >= u)


def spread_matrix(step):
    rows = iota((H, WIDE), 0)
    lanes = iota((H, WIDE), 1)
    return jnp.where(rows == step * HEADS + lanes // P_SIZE, 1.0, 0.0).astype(BF16)


def summary_kernel(lengths, x, dt, dlog, write, send, weight):
    step = pl.program_id(0)
    first = lax.axis_index("ctx") * TOK
    one, two = starts_of(lengths)
    one, two = one - first, two - first
    mask = jnp.where(same_causal(one, two), 1.0, 0.0).astype(BF16)
    rates = dlog[...]

    @pl.when(step == 0)
    def _():
        run = nn(mask, rates).T
        u = iota((1, TOK), 1)
        last = (TOK - 1 >= one).astype(I32) + (TOK - 1 >= two).astype(I32)
        held = segment(u, one, two) == last
        gap = jnp.where(held, run[:, TOK - 1 :] - run, -jnp.inf)
        weight[...] = jnp.exp(gap) * dt[...].astype(F32).T

    turned = write[...].astype(F32).T
    for k in range(HEADS):
        row = weight[pl.ds(step * HEADS + k, 1), :]
        b = k // G
        loads = (row * turned[b * N : (b + 1) * N]).astype(BF16)
        made = nn(loads, x[:, k * P_SIZE : (k + 1) * P_SIZE])
        lane = (k % 2) * P_SIZE
        j = k // 2
        send[j % 2, j // 2, :N, lane : lane + P_SIZE] = made
    spread = nn(rates, spread_matrix(step)).astype(BF16)
    carry = jnp.exp(nn(mask[TOK - 16 :], spread)[15:16])
    for j in range(HEADS // 2):
        row = carry[:, j * PAIR : (j + 1) * PAIR]
        send[j % 2, j // 2, N:, :] = jnp.broadcast_to(row, (8, PAIR))


def await_bytes(ref, sem):
    pltpu.make_async_copy(ref, ref, sem).wait()


def exchange_kernel(
    home,
    lengths,
    saved,
    made,
    cache_keys,
    cache_values,
    turn_keys,
    turn_values,
    state,
    extras,
    caches,
    band,
    theirs,
    packed,
    recv,
    stored,
    entering,
    arrived,
    own_state,
    other_state,
    extra,
    plane,
    sent,
    got,
    local,
):
    group, me = lax.axis_index("sess"), lax.axis_index("ctx")
    x, deep = group // 2, group % 2
    y, z, core = me // 8, (me // 2) % 4, me % 2
    chip = me // 2
    sibling = me + 1 - 2 * core
    partner = group + 1 - 2 * deep
    x_groups = [((x + i) % 4) * 2 + deep for i in range(1, 4)]
    y_peers = [((y + i) % 4) * 8 + z * 2 + core for i in range(1, 4)]
    z_before = y * 8 + ((z + 3) % 4) * 2 + core
    z_after = [y * 8 + ((z + i) % 4) * 2 + core for i in range(1, 4)]
    onward = (me + 2) % CTX
    kinds = {name: i for i, name in enumerate(EXCHANGES)}

    def copy_in(src, dst, at):
        copy = pltpu.make_async_copy(src, dst, local.at[at])
        copy.start()
        return copy

    half = KVH * HD
    mine = [
        copy_in(cache_keys, caches.at[me, 0], 0),
        copy_in(cache_values, caches.at[me, 1], 1),
        copy_in(turn_keys, band.at[pl.ds(8 * REACH, 8), :, pl.ds(0, half)], 2),
        copy_in(turn_values, band.at[pl.ds(8 * REACH, 8), :, pl.ds(half, half)], 3),
        copy_in(saved, stored.at[group], 4),
    ]

    barrier = pltpu.get_barrier_semaphore()

    def greet(i, nothing):
        peer = ((chip + i) % CHIPS) * 2 + core
        pl.semaphore_signal(barrier, inc=1, device_id=(group, peer), device_id_type=MESH)
        return nothing

    lax.fori_loop(1, CHIPS, greet, 0)
    pl.semaphore_signal(barrier, inc=1, device_id=(group, sibling), device_id_type=MESH)
    for to in [partner] + x_groups:
        pl.semaphore_signal(barrier, inc=1, device_id=(to, me), device_id_type=MESH)
    pl.semaphore_wait(barrier, CHIPS - 1 + 1 + 4)

    def push(kind, src, dst, peer, to=None):
        at = kinds[kind]
        pltpu.make_async_remote_copy(
            src_ref=src,
            dst_ref=dst,
            send_sem=sent.at[at],
            recv_sem=got.at[at],
            device_id=(group if to is None else to, peer),
            device_id_type=MESH,
        ).start()

    counts = {}

    def arrive(kind, ref):
        counts[kind] = ref
        await_bytes(ref, got.at[kinds[kind]])

    def slot(distance):
        return band.at[pl.ds(8 * (REACH - distance), 8)]

    def spread(name, array, at):
        for to in y_peers:
            push(name + "_y", array.at[at], array.at[at], to)

    push("home_z", saved, stored.at[group], me, partner)
    for to in x_groups:
        push("home_x", saved, stored.at[group], me, to)
    push("pair", made.at[1 - core], theirs, sibling)
    mine[2].wait()
    mine[3].wait()
    push("band_2", slot(0), slot(2), onward)
    mine[0].wait()
    mine[1].wait()
    push("cache_1", caches.at[me], caches.at[me], z_before)
    spread("cache", caches, me)
    push("cache_core", caches.at[me], caches.at[me], sibling)

    arrive("home_z", stored.at[0])
    for to in x_groups:
        push("home_x", stored.at[partner], stored.at[partner], me, to)

    one, two = starts_of(lengths)

    def inside(c):
        end = c * TOK + TOK - 1
        first = (end >= one) & (end < two) & (one >= c * TOK)
        second = (end >= two) & (two >= c * TOK)
        return first, second

    arrive("pair", theirs)
    first_one, first_two = inside(2 * chip)
    last_one, last_two = inside(2 * chip + 1)
    fresh = last_one | last_two

    def both(m):
        own = made[core, m]
        other = theirs[m]
        even = jnp.where(core == 0, own, other)
        odd = jnp.where(core == 0, other, own)
        return even, odd

    def combine(i, nothing):
        m = (chip + i) % CHIPS
        even, odd = both(m)
        factor = odd[N : N + 1]
        total = odd[:N] + jnp.where(fresh, 0.0, factor) * even[:N]
        carry = factor * jnp.where(fresh, 1.0, even[N : N + 1])
        packed[m, :N, :] = total.astype(BF16)
        high = carry.astype(BF16).astype(F32)
        tile = iota((16, PAIR), 0)
        rows = jnp.where(tile == 0, high, jnp.where(tile == 1, carry - high, 0.0))
        packed[m, N:, :] = rows.astype(BF16)

        @pl.when(i != 0)
        def _():
            push("summary", packed.at[m], recv.at[chip], 2 * m + core)

        return nothing

    lax.fori_loop(0, CHIPS, combine, 0)
    own_summary = copy_in(packed.at[chip], recv.at[chip], 0)

    arrive("cache_1", caches.at[0])
    push("cache_2", caches.at[z_after[0]], caches.at[z_after[0]], z_before)
    spread("cache", caches, z_after[0])
    push("cache_core", caches.at[z_after[0]], caches.at[z_after[0]], sibling)
    arrive("band_2", slot(2))
    push("band_4", slot(2), slot(4), onward)

    mine[4].wait()
    arrive("home_x", stored.at[pl.ds(0, 6)])
    back = []
    for s in range(SEQS):
        at = home[group * SEQS + s]
        back.append(stored[at // SEQS, at % SEQS].astype(F32))
    extra[0] = back[1].astype(BF16)
    extra[1] = back[2].astype(BF16)
    push("extra_1", extra, plane.at[chip], z_before)
    for to in y_peers:
        push("extra_y", extra, plane.at[chip], to)
    own_extra = copy_in(extra, plane.at[chip], 1)

    arrive("cache_2", caches.at[0])
    push("cache_3", caches.at[z_after[1]], caches.at[z_after[1]], z_before)
    spread("cache", caches, z_after[1])
    push("cache_core", caches.at[z_after[1]], caches.at[z_after[1]], sibling)

    arrive("summary", recv.at[pl.ds(0, CHIPS - 1)])
    own_summary.wait()

    def turn(m, held):
        entering[m] = held.astype(BF16)

        @pl.when(m != chip)
        def _():
            push("state", entering.at[m], arrived.at[chip], 2 * m + core)

        even_one, even_two = inside(2 * m)
        odd_one, odd_two = inside(2 * m + 1)
        base = jnp.where(even_two, back[2], jnp.where(even_one, back[1], held))
        base = jnp.where(odd_two, back[2], jnp.where(odd_one, back[1], base))
        carry = recv[m, N : N + 16, :].astype(F32)
        return (carry[0:1] + carry[1:2]) * base + recv[m, :N, :].astype(F32)

    lax.fori_loop(0, CHIPS, turn, back[0])
    own_entering = copy_in(entering.at[chip], arrived.at[chip], 2)

    arrive("extra_1", plane.at[0])
    push("extra_2", plane.at[z_after[0] // 2], plane.at[z_after[0] // 2], z_before)
    spread("extra", plane, z_after[0] // 2)
    arrive("cache_3", caches.at[0])
    spread("cache", caches, z_after[2])
    push("cache_core", caches.at[z_after[2]], caches.at[z_after[2]], sibling)
    arrive("extra_2", plane.at[0])
    push("extra_3", plane.at[z_after[1] // 2], plane.at[z_after[1] // 2], z_before)
    spread("extra", plane, z_after[1] // 2)
    arrive("band_4", slot(4))
    push("band_core", slot(2 * core), slot(1), sibling)
    push("band_core", slot(2 * core + 2), slot(3), sibling)
    arrive("cache_y", caches.at[pl.ds(0, 12)])
    for i in range(4):
        for j in range(1, 4):
            at = ((y + j) % 4) * 8 + ((z + i) % 4) * 2 + core
            push("cache_core", caches.at[at], caches.at[at], sibling)
    arrive("extra_3", plane.at[0])
    spread("extra", plane, z_after[2] // 2)
    own_extra.wait()
    arrive("extra_y", plane.at[pl.ds(0, 12)])
    push("extra_core", plane, extras.at[core], sibling)
    keep_extra = copy_in(plane, extras.at[core], 0)

    arrive("state", arrived.at[pl.ds(0, CHIPS - 1)])
    own_entering.wait()

    def settle(m, nothing):
        even, _ = both(m)
        first = arrived[m].astype(F32)
        base = jnp.where(
            first_two,
            plane[m, 1].astype(F32),
            jnp.where(first_one, plane[m, 0].astype(F32), first),
        )
        second = even[N : N + 1] * base + even[:N]
        own_state[m] = jnp.where(core == 0, first, second).astype(BF16)
        other_state[m] = jnp.where(core == 0, second, first).astype(BF16)
        return nothing

    lax.fori_loop(0, CHIPS, settle, 0)
    push("state_core", other_state, state.at[core], sibling)
    keep_state = copy_in(own_state, state.at[core], 1)

    arrive("extra_core", extras.at[0])
    arrive("cache_core", caches.at[pl.ds(0, CHIPS)])
    arrive("band_core", band.at[pl.ds(0, 16)])
    arrive("state_core", state.at[0])
    keep_extra.wait()
    keep_state.wait()
    for kind, ref in counts.items():
        await_bytes(ref, sent.at[kinds[kind]])


EXCHANGES = (
    "home_z",
    "home_x",
    "pair",
    "summary",
    "state",
    "state_core",
    "band_2",
    "band_4",
    "band_core",
    "cache_1",
    "cache_2",
    "cache_3",
    "cache_y",
    "cache_core",
    "extra_1",
    "extra_2",
    "extra_3",
    "extra_y",
    "extra_core",
)


def output_kernel(lengths, x, dt, dlog, write, read, gain, state, extra, out, run_rows, step_rows):
    step = pl.program_id(0)
    first = lax.axis_index("ctx") * TOK
    one, two = starts_of(lengths)
    one, two = one - first, two - first
    seen = same_causal(one, two)
    mask = jnp.where(seen, 1.0, 0.0).astype(BF16)
    bias = jnp.where(seen, 0.0, -jnp.inf)
    rates = dlog[...]

    @pl.when(step == 0)
    def _():
        run_rows[...] = nn(mask, rates).T
        step_rows[...] = dt[...].astype(F32).T

    t = iota((TOK, N), 0)
    new_one = (t >= one) & (t < two) & (one >= 0)
    new_two = (t >= two) & (two >= 0)
    spread = nn(rates, spread_matrix(step)).astype(BF16)
    run = nn(mask, spread)
    for b in range(HEADS // G):
        c = read[:, b * N : (b + 1) * N].astype(F32)
        c_in = jnp.where(new_one | new_two, 0.0, c).astype(BF16)
        c_one = jnp.where(new_one, c, 0.0).astype(BF16)
        c_two = jnp.where(new_two, c, 0.0).astype(BF16)
        both = nt(read[:, b * N : (b + 1) * N], write[:, b * N : (b + 1) * N])
        for j in range(G // 2):
            chunk = b * (G // 2) + j
            from_state = (
                nn(c_in, state[chunk % 2, chunk // 2])
                + nn(c_one, extra[chunk % 2, chunk // 2, 0])
                + nn(c_two, extra[chunk % 2, chunk // 2, 1])
            )
            for i in range(2):
                k = chunk * 2 + i
                lanes = slice(k * P_SIZE, (k + 1) * P_SIZE)
                at = pl.ds(step * HEADS + k, 1)
                run_t = run[:, lanes]
                decay = jnp.exp(run_t - run_rows[at, :] + bias)
                mixing = (both * decay * step_rows[at, :]).astype(BF16)
                x_h = x[:, lanes]
                result = (
                    nn(mixing, x_h)
                    + jnp.exp(run_t) * from_state[:, i * P_SIZE : (i + 1) * P_SIZE]
                    + gain[:, lanes] * x_h.astype(F32)
                )
                out[:, lanes] = result.astype(BF16)


def attention_kernel(
    lengths,
    history,
    queries,
    band,
    sinks,
    cache,
    out,
    keys,
    rows,
    scores,
    top,
    total,
    sums,
    bias,
    listed,
    sems,
):
    place = lax.axis_index("ctx")
    first = place * TOK
    one, two = starts_of(lengths)
    copies = [
        pltpu.make_async_copy(band, keys.at[pl.ds(0, 8 * SINK_BLOCK)], sems.at[0]),
        pltpu.make_async_copy(sinks, keys.at[pl.ds(8 * SINK_BLOCK, 8)], sems.at[1]),
    ]
    for s in range(SEQS):
        for kv in range(2):
            copies.append(
                pltpu.make_async_copy(
                    cache.at[:, kv, s],
                    keys.at[pl.ds(8 * CACHE_BLOCK + 32 * s, 32), :, pl.ds(kv * KVH * HD, KVH * HD)],
                    sems.at[2 + 2 * s + kv],
                )
            )
    for copy in copies:
        copy.start()
    keys[8 * NULL_BLOCK :] = jnp.zeros((8, 16, 2 * KVH * HD), BF16)

    t = first + iota((TOK, TOK), 0)
    u = iota((TOK, TOK), 1)
    owner = segment(t, one, two)
    offset = t - jnp.where(owner == 2, two, jnp.where(owner == 1, one, 0))
    count = jnp.int32(0)
    head_owner = (first >= one).astype(I32) + (first >= two).astype(I32)
    for b in range(REACH + 1):
        pos = first + (b - REACH) * TOK + u
        gap = t - pos
        ok = (pos >= 0) & (segment(pos, one, two) == owner) & (gap >= 0) & (gap < WINDOW)
        bias[b] = jnp.where(ok, 0.0, -jnp.inf)
        end = first + (b - REACH) * TOK + TOK - 1
        end_owner = (end >= one).astype(I32) + (end >= two).astype(I32)
        live = (end >= 0) & (end_owner >= head_owner)
        listed[count] = b
        count = count + live.astype(I32)
    bias[SINK_BLOCK] = jnp.where(
        (u < SEQS * SINKS) & (u // SINKS == owner), 0.0, -jnp.inf
    )
    listed[count] = SINK_BLOCK
    count = count + 1
    edges = [jnp.int32(0), one, two, jnp.int32(CTX * TOK)]
    for s in range(SEQS):
        begin = jnp.maximum(edges[s], first)
        present = begin < jnp.minimum(edges[s + 1], first + TOK)
        for j in range(4):
            live = (
                present
                & (begin - edges[s] < j * TOK + TOK - 1)
                & (history[0, s] - WINDOW + j * TOK + TOK - 1 >= SINKS)
            )
            block = CACHE_BLOCK + 4 * s + j

            @pl.when(live)
            def _():
                slot = j * TOK + u
                ok = (owner == s) & (slot > offset) & (history[0, s] - WINDOW + slot >= SINKS)
                bias[block] = jnp.where(ok, 0.0, -jnp.inf)

            listed[count] = block
            count = count + live.astype(I32)
    bias[NULL_BLOCK] = jnp.full((TOK, TOK), -jnp.inf, F32)
    listed[count] = NULL_BLOCK
    pairs = lax.div(count + 1, jnp.int32(2))
    for copy in copies:
        copy.wait()

    per = QH // KVH
    scale = 1.0 / math.sqrt(HD) / math.log(2.0)

    def one_head(number, nothing):
        lanes = pl.ds(pl.multiple_of(number * HD, HD), HD)
        value_lanes = pl.ds(pl.multiple_of(number * HD + KVH * HD, HD), HD)
        for r in range(per):
            wide = pl.ds(pl.multiple_of((number * per + r) * HD, HD), HD)
            rows[r * TOK : (r + 1) * TOK, :] = queries[:, wide]
        top[...] = jnp.full(top.shape, -jnp.inf, F32)
        total[...] = jnp.zeros(total.shape, F32)
        sums[...] = jnp.zeros(sums.shape, F32)

        def score(i, nothing):
            for part in range(2):
                block = listed[2 * i + part]
                key = keys[pl.ds(block * 8, 8), :, lanes].reshape(TOK, HD)
                offset_rows = bias[block]
                for r in range(per):
                    at = slice(r * TOK, (r + 1) * TOK)
                    got = nt(rows[at, :], key) * scale + offset_rows
                    scores[2 * i + part, at, :] = got
                    top[at, :] = jnp.maximum(top[at, :], got)
            return nothing

        lax.fori_loop(0, pairs, score, 0)
        top[...] = jnp.broadcast_to(jnp.max(top[...], axis=1, keepdims=True), top.shape)

        def weigh(i, nothing):
            values = []
            for part in range(2):
                block = listed[2 * i + part]
                values.append(keys[pl.ds(block * 8, 8), :, value_lanes].reshape(TOK, HD))
            value = jnp.concatenate(values, axis=0)
            for r in range(per):
                at = slice(r * TOK, (r + 1) * TOK)
                left = jnp.exp2(scores[2 * i, at, :] - top[at, :])
                right = jnp.exp2(scores[2 * i + 1, at, :] - top[at, :])
                total[at, :] += left + right
                both = jnp.concatenate([left.astype(BF16), right.astype(BF16)], axis=1)
                sums[at, :] += nn(both, value)
            return nothing

        lax.fori_loop(0, pairs, weigh, 0)
        for r in range(per):
            at = slice(r * TOK, (r + 1) * TOK)
            whole = jnp.sum(total[at, :], axis=1, keepdims=True)
            wide = pl.ds(pl.multiple_of((number * per + r) * HD, HD), HD)
            out[:, wide] = (sums[at, :] / whole).astype(BF16)
        return nothing

    lax.fori_loop(0, KVH, one_head, 0)


SMEM = pl.BlockSpec(memory_space=pltpu.SMEM)
VMEM = pl.BlockSpec(memory_space=pltpu.VMEM)
ANY = pl.BlockSpec(memory_space=pl.ANY)
LIMIT = pltpu.CompilerParams(vmem_limit_bytes=48 * 2**20)


def full(shape):
    return pl.BlockSpec(shape, lambda i: (0,) * len(shape))


def lane_block(rows, width):
    return pl.BlockSpec((rows, width), lambda i: (0, i))


def summaries(lengths, x, dt, dlog, write):
    return pl.pallas_call(
        summary_kernel,
        grid=(STEPS,),
        out_shape=jax.ShapeDtypeStruct((2, CHIPS, N + 8, PAIR), F32),
        in_specs=[
            SMEM,
            lane_block(TOK, WIDE),
            full((TOK, H)),
            full((TOK, H)),
            lane_block(TOK, 2 * N),
        ],
        out_specs=pl.BlockSpec((2, CHIPS // STEPS, N + 8, PAIR), lambda i: (0, i, 0, 0)),
        scratch_shapes=[pltpu.VMEM((H, TOK), F32)],
        compiler_params=LIMIT,
    )(lengths, x, dt, dlog, write)


def exchange(groups, home, lengths, saved, made, cache_keys, cache_values, turn_keys, turn_values):
    return pl.pallas_call(
        exchange_kernel,
        out_shape=(
            jax.ShapeDtypeStruct((2, CHIPS, N, PAIR), BF16),
            jax.ShapeDtypeStruct((2, CHIPS, 2, N, PAIR), BF16),
            jax.ShapeDtypeStruct((CTX, 2) + cache_keys.shape, BF16),
            jax.ShapeDtypeStruct((8 * (REACH + 1), 16, 2 * KVH * HD), BF16),
        ),
        in_specs=[SMEM, SMEM, ANY, VMEM, ANY, ANY, ANY, ANY],
        out_specs=(ANY, ANY, ANY, ANY),
        scratch_shapes=[
            pltpu.VMEM((CHIPS, N + 8, PAIR), F32),
            pltpu.VMEM((CHIPS, ROWS, PAIR), BF16),
            pltpu.VMEM((CHIPS, ROWS, PAIR), BF16),
            pltpu.VMEM((groups, SEQS, N, PAIR), BF16),
            pltpu.VMEM((CHIPS, N, PAIR), BF16),
            pltpu.VMEM((CHIPS, N, PAIR), BF16),
            pltpu.VMEM((CHIPS, N, PAIR), BF16),
            pltpu.VMEM((CHIPS, N, PAIR), BF16),
            pltpu.VMEM((2, N, PAIR), BF16),
            pltpu.VMEM((CHIPS, 2, N, PAIR), BF16),
            pltpu.SemaphoreType.DMA((len(EXCHANGES),)),
            pltpu.SemaphoreType.DMA((len(EXCHANGES),)),
            pltpu.SemaphoreType.DMA((5,)),
        ],
        compiler_params=pltpu.CompilerParams(
            collective_id=0, has_side_effects=True, vmem_limit_bytes=48 * 2**20
        ),
    )(home, lengths, saved, made, cache_keys, cache_values, turn_keys, turn_values)


def outputs(lengths, x, dt, dlog, write, read, gain, state, extra):
    return pl.pallas_call(
        output_kernel,
        grid=(STEPS,),
        out_shape=jax.ShapeDtypeStruct((TOK, H * P_SIZE), BF16),
        in_specs=[
            SMEM,
            lane_block(TOK, WIDE),
            full((TOK, H)),
            full((TOK, H)),
            lane_block(TOK, 2 * N),
            lane_block(TOK, 2 * N),
            lane_block(1, WIDE),
            pl.BlockSpec((2, CHIPS // STEPS, N, PAIR), lambda i: (0, i, 0, 0)),
            pl.BlockSpec((2, CHIPS // STEPS, 2, N, PAIR), lambda i: (0, i, 0, 0, 0)),
        ],
        out_specs=lane_block(TOK, WIDE),
        scratch_shapes=[pltpu.VMEM((H, TOK), F32), pltpu.VMEM((H, TOK), F32)],
        compiler_params=LIMIT,
    )(lengths, x, dt, dlog, write, read, gain, state, extra)


def attention(lengths, history, queries, band, sinks, cache):
    rows = (QH // KVH) * TOK
    return pl.pallas_call(
        attention_kernel,
        out_shape=jax.ShapeDtypeStruct((TOK, QH * HD), BF16),
        in_specs=[SMEM, SMEM, VMEM, ANY, ANY, ANY],
        out_specs=VMEM,
        scratch_shapes=[
            pltpu.VMEM((8 * BLOCKS, 16, 2 * KVH * HD), BF16),
            pltpu.VMEM((rows, HD), BF16),
            pltpu.VMEM((BLOCKS + 1, rows, TOK), F32),
            pltpu.VMEM((rows, TOK), F32),
            pltpu.VMEM((rows, TOK), F32),
            pltpu.VMEM((rows, HD), F32),
            pltpu.VMEM((BLOCKS, TOK, TOK), F32),
            pltpu.SMEM((BLOCKS + 1,), I32),
            pltpu.SemaphoreType.DMA((8,)),
        ],
        compiler_params=LIMIT,
        cost_estimate=pl.CostEstimate(
            flops=2_500_000_000, bytes_accessed=8_000_000, transcendentals=5_000_000
        ),
    )(lengths, history, queries, band, sinks, cache)


def shards(
    mamba_input,
    step_size,
    decay_log,
    state_write,
    state_read,
    skip_gain,
    saved_states,
    home_slot,
    turn_lengths,
    history_lengths,
    queries,
    turn_keys,
    turn_values,
    cache_keys,
    cache_values,
    sink_keys,
    sink_values,
):
    x, dt, dlog = mamba_input[0], step_size[0], decay_log[0]
    write, read = state_write[0], state_read[0]
    saved = saved_states[0].astype(BF16).reshape(SEQS, 2, P_SIZE, N)
    saved = saved.transpose(0, 3, 1, 2).reshape(SEQS, N, PAIR)
    sinks = jnp.concatenate(
        [sink_keys[0].reshape(SEQS * SINKS, -1), sink_values[0].reshape(SEQS * SINKS, -1)], axis=1
    )
    sinks = jnp.pad(sinks, ((0, TOK - SEQS * SINKS), (0, 0))).reshape(8, 16, 2 * KVH * HD)
    gain = jnp.repeat(skip_gain, P_SIZE)[None]

    made = summaries(turn_lengths, x, dt, dlog, write)
    groups = lax.axis_size("sess")
    state, extras, caches, band = exchange(
        groups,
        home_slot,
        turn_lengths,
        saved,
        made,
        cache_keys[0],
        cache_values[0],
        turn_keys[0].reshape(8, 16, KVH * HD),
        turn_values[0].reshape(8, 16, KVH * HD),
    )
    attended = attention(turn_lengths, history_lengths, queries[0], band, sinks, caches)
    mixed = outputs(turn_lengths, x, dt, dlog, write, read, gain, state, extras)
    return (mixed[None], attended[None])


def solution(mesh):
    token = P("sess", "ctx", None)
    spread = P("sess", None, "ctx", None)
    return jax.shard_map(
        shards,
        mesh=mesh,
        in_specs=(
            token,
            token,
            token,
            token,
            token,
            P(),
            spread,
            P(),
            P("sess", None),
            P("sess", None),
            token,
            token,
            token,
            spread,
            spread,
            P("sess", None, None, None),
            P("sess", None, None, None),
        ),
        out_specs=(token, token),
        check_vma=False,
    )
```

```python
import functools
import math

import jax
import jax.numpy as jnp
from jax import lax
from jax.experimental import pallas as pl
from jax.experimental.pallas import tpu as pltpu
from jax.sharding import PartitionSpec as P

TOK = 128
REACH = 4
SEQS = 3
SINKS = 4
H = 64
P_SIZE = 128
N = 64
G = 8
QH = 32
KVH = 4
HD = 128
WINDOW = 512
CTX = 32
CHIPS = CTX // 2
MESH = pl.DeviceIdType.MESH

F32 = jnp.float32
BF16 = jnp.bfloat16
I32 = jnp.int32
PAIR = 2 * P_SIZE
ROWS = N + 16
STEPS = 4
HEADS = H // STEPS
WIDE = HEADS * P_SIZE
BLOCKS = REACH + 1 + 1 + SEQS * 4 + 1
SINK_BLOCK = REACH + 1
CACHE_BLOCK = SINK_BLOCK + 1
NULL_BLOCK = BLOCKS - 1


def iota(shape, axis):
    return lax.broadcasted_iota(I32, shape, axis)


def nn(a, b):
    return lax.dot_general(a, b, (((1,), (0,)), ((), ())), preferred_element_type=F32)


def nt(a, b):
    return lax.dot_general(a, b, (((1,), (1,)), ((), ())), preferred_element_type=F32)


def starts_of(lengths):
    first = lengths[0, 0]
    return first, first + lengths[0, 1]


def segment(positions, one, two):
    return (positions >= one).astype(I32) + (positions >= two).astype(I32)


def same_causal(one, two):
    t, u = iota((TOK, TOK), 0), iota((TOK, TOK), 1)
    return (segment(t, one, two) == segment(u, one, two)) & (t >= u)


def spread_matrix(step):
    rows = iota((H, WIDE), 0)
    lanes = iota((H, WIDE), 1)
    return jnp.where(rows == step * HEADS + lanes // P_SIZE, 1.0, 0.0).astype(BF16)


def summary_kernel(lengths, x, dt, dlog, write, send, weight):
    step = pl.program_id(0)
    first = lax.axis_index("ctx") * TOK
    one, two = starts_of(lengths)
    one, two = one - first, two - first
    mask = jnp.where(same_causal(one, two), 1.0, 0.0).astype(BF16)
    rates = dlog[...]

    @pl.when(step == 0)
    def _():
        run = nn(mask, rates).T
        u = iota((1, TOK), 1)
        last = (TOK - 1 >= one).astype(I32) + (TOK - 1 >= two).astype(I32)
        held = segment(u, one, two) == last
        gap = jnp.where(held, run[:, TOK - 1 :] - run, -jnp.inf)
        weight[...] = jnp.exp(gap) * dt[...].astype(F32).T

    turned = write[...].astype(F32).T
    for k in range(HEADS):
        row = weight[pl.ds(step * HEADS + k, 1), :]
        b = k // G
        loads = (row * turned[b * N : (b + 1) * N]).astype(BF16)
        made = nn(loads, x[:, k * P_SIZE : (k + 1) * P_SIZE])
        lane = (k % 2) * P_SIZE
        j = k // 2
        send[j % 2, j // 2, :N, lane : lane + P_SIZE] = made
    spread = nn(rates, spread_matrix(step)).astype(BF16)
    carry = jnp.exp(nn(mask[TOK - 16 :], spread)[15:16])
    for j in range(HEADS // 2):
        row = carry[:, j * PAIR : (j + 1) * PAIR]
        send[j % 2, j // 2, N:, :] = jnp.broadcast_to(row, (8, PAIR))


def await_bytes(ref, sem):
    pltpu.make_async_copy(ref, ref, sem).wait()


def exchange_kernel(
    home,
    lengths,
    saved,
    made,
    cache_keys,
    cache_values,
    turn_keys,
    turn_values,
    state,
    extras,
    caches,
    band,
    theirs,
    packed,
    recv,
    stored,
    entering,
    arrived,
    own_state,
    other_state,
    extra,
    plane,
    sent,
    got,
    local,
):
    group, me = lax.axis_index("sess"), lax.axis_index("ctx")
    x, deep = group // 2, group % 2
    y, z, core = me // 8, (me // 2) % 4, me % 2
    chip = me // 2
    sibling = me + 1 - 2 * core
    partner = group + 1 - 2 * deep
    x_groups = [((x + i) % 4) * 2 + deep for i in range(1, 4)]
    y_peers = [((y + i) % 4) * 8 + z * 2 + core for i in range(1, 4)]
    z_before = y * 8 + ((z + 3) % 4) * 2 + core
    z_after = [y * 8 + ((z + i) % 4) * 2 + core for i in range(1, 4)]
    onward = (me + 2) % CTX
    kinds = {name: i for i, name in enumerate(EXCHANGES)}

    def copy_in(src, dst, at):
        copy = pltpu.make_async_copy(src, dst, local.at[at])
        copy.start()
        return copy

    half = KVH * HD
    mine = [
        copy_in(cache_keys, caches.at[me, 0], 0),
        copy_in(cache_values, caches.at[me, 1], 1),
        copy_in(turn_keys, band.at[pl.ds(8 * REACH, 8), :, pl.ds(0, half)], 2),
        copy_in(turn_values, band.at[pl.ds(8 * REACH, 8), :, pl.ds(half, half)], 3),
        copy_in(saved, stored.at[group], 4),
    ]

    barrier = pltpu.get_barrier_semaphore()

    def greet(i, nothing):
        peer = ((chip + i) % CHIPS) * 2 + core
        pl.semaphore_signal(barrier, inc=1, device_id=(group, peer), device_id_type=MESH)
        return nothing

    lax.fori_loop(1, CHIPS, greet, 0)
    pl.semaphore_signal(barrier, inc=1, device_id=(group, sibling), device_id_type=MESH)
    for to in [partner] + x_groups:
        pl.semaphore_signal(barrier, inc=1, device_id=(to, me), device_id_type=MESH)
    pl.semaphore_wait(barrier, CHIPS - 1 + 1 + 4)

    def push(kind, src, dst, peer, to=None):
        at = kinds[kind]
        pltpu.make_async_remote_copy(
            src_ref=src,
            dst_ref=dst,
            send_sem=sent.at[at],
            recv_sem=got.at[at],
            device_id=(group if to is None else to, peer),
            device_id_type=MESH,
        ).start()

    counts = {}

    def arrive(kind, ref):
        counts[kind] = ref
        await_bytes(ref, got.at[kinds[kind]])

    def slot(distance):
        return band.at[pl.ds(8 * (REACH - distance), 8)]

    def spread(name, array, at):
        for to in y_peers:
            push(name + "_y", array.at[at], array.at[at], to)

    push("home_z", saved, stored.at[group], me, partner)
    for to in x_groups:
        push("home_x", saved, stored.at[group], me, to)
    push("pair", made.at[1 - core], theirs, sibling)
    mine[2].wait()
    mine[3].wait()
    push("band_2", slot(0), slot(2), onward)
    mine[0].wait()
    mine[1].wait()
    push("cache_1", caches.at[me], caches.at[me], z_before)
    spread("cache", caches, me)
    push("cache_core", caches.at[me], caches.at[me], sibling)

    arrive("home_z", stored.at[0])
    for to in x_groups:
        push("home_x", stored.at[partner], stored.at[partner], me, to)

    one, two = starts_of(lengths)

    def inside(c):
        end = c * TOK + TOK - 1
        first = (end >= one) & (end < two) & (one >= c * TOK)
        second = (end >= two) & (two >= c * TOK)
        return first, second

    arrive("pair", theirs)
    first_one, first_two = inside(2 * chip)
    last_one, last_two = inside(2 * chip + 1)
    fresh = last_one | last_two

    def both(m):
        own = made[core, m]
        other = theirs[m]
        even = jnp.where(core == 0, own, other)
        odd = jnp.where(core == 0, other, own)
        return even, odd

    def combine(i, nothing):
        m = (chip + i) % CHIPS
        even, odd = both(m)
        factor = odd[N : N + 1]
        total = odd[:N] + jnp.where(fresh, 0.0, factor) * even[:N]
        carry = factor * jnp.where(fresh, 1.0, even[N : N + 1])
        packed[m, :N, :] = total.astype(BF16)
        high = carry.astype(BF16).astype(F32)
        tile = iota((16, PAIR), 0)
        rows = jnp.where(tile == 0, high, jnp.where(tile == 1, carry - high, 0.0))
        packed[m, N:, :] = rows.astype(BF16)

        @pl.when(i != 0)
        def _():
            push("summary", packed.at[m], recv.at[chip], 2 * m + core)

        return nothing

    lax.fori_loop(0, CHIPS, combine, 0)
    own_summary = copy_in(packed.at[chip], recv.at[chip], 0)

    arrive("cache_1", caches.at[0])
    push("cache_2", caches.at[z_after[0]], caches.at[z_after[0]], z_before)
    spread("cache", caches, z_after[0])
    push("cache_core", caches.at[z_after[0]], caches.at[z_after[0]], sibling)
    arrive("band_2", slot(2))
    push("band_4", slot(2), slot(4), onward)

    mine[4].wait()
    arrive("home_x", stored.at[pl.ds(0, 6)])
    back = []
    for s in range(SEQS):
        at = home[group * SEQS + s]
        back.append(stored[at // SEQS, at % SEQS].astype(F32))
    extra[0] = back[1].astype(BF16)
    extra[1] = back[2].astype(BF16)
    push("extra_1", extra, plane.at[chip], z_before)
    for to in y_peers:
        push("extra_y", extra, plane.at[chip], to)
    own_extra = copy_in(extra, plane.at[chip], 1)

    arrive("cache_2", caches.at[0])
    push("cache_3", caches.at[z_after[1]], caches.at[z_after[1]], z_before)
    spread("cache", caches, z_after[1])
    push("cache_core", caches.at[z_after[1]], caches.at[z_after[1]], sibling)

    arrive("extra_1", plane.at[0])
    push("extra_2", plane.at[z_after[0] // 2], plane.at[z_after[0] // 2], z_before)
    spread("extra", plane, z_after[0] // 2)
    arrive("extra_2", plane.at[0])
    push("extra_3", plane.at[z_after[1] // 2], plane.at[z_after[1] // 2], z_before)
    spread("extra", plane, z_after[1] // 2)
    arrive("summary", recv.at[pl.ds(0, CHIPS - 1)])
    own_summary.wait()

    def turn(m, held):
        entering[m] = held.astype(BF16)

        @pl.when(m != chip)
        def _():
            push("state", entering.at[m], arrived.at[chip], 2 * m + core)

        even_one, even_two = inside(2 * m)
        odd_one, odd_two = inside(2 * m + 1)
        base = jnp.where(even_two, back[2], jnp.where(even_one, back[1], held))
        base = jnp.where(odd_two, back[2], jnp.where(odd_one, back[1], base))
        carry = recv[m, N : N + 16, :].astype(F32)
        return (carry[0:1] + carry[1:2]) * base + recv[m, :N, :].astype(F32)

    lax.fori_loop(0, CHIPS, turn, back[0])
    own_entering = copy_in(entering.at[chip], arrived.at[chip], 2)


    arrive("extra_3", plane.at[0])
    spread("extra", plane, z_after[2] // 2)
    arrive("cache_3", caches.at[0])
    spread("cache", caches, z_after[2])
    push("cache_core", caches.at[z_after[2]], caches.at[z_after[2]], sibling)
    arrive("band_4", slot(4))
    push("band_core", slot(2 * core), slot(1), sibling)
    push("band_core", slot(2 * core + 2), slot(3), sibling)
    own_extra.wait()
    arrive("extra_y", plane.at[pl.ds(0, 12)])
    push("extra_core", plane, extras.at[core], sibling)
    keep_extra = copy_in(plane, extras.at[core], 0)
    arrive("state", arrived.at[pl.ds(0, CHIPS - 1)])
    own_entering.wait()

    def settle(m, nothing):
        even, _ = both(m)
        first = arrived[m].astype(F32)
        base = jnp.where(
            first_two,
            plane[m, 1].astype(F32),
            jnp.where(first_one, plane[m, 0].astype(F32), first),
        )
        second = even[N : N + 1] * base + even[:N]
        own_state[m] = jnp.where(core == 0, first, second).astype(BF16)
        other_state[m] = jnp.where(core == 0, second, first).astype(BF16)
        return nothing

    lax.fori_loop(0, CHIPS, settle, 0)
    push("state_core", other_state, state.at[core], sibling)
    keep_state = copy_in(own_state, state.at[core], 1)
    arrive("cache_y", caches.at[pl.ds(0, 12)])
    for i in range(4):
        for j in range(1, 4):
            at = ((y + j) % 4) * 8 + ((z + i) % 4) * 2 + core
            push("cache_core", caches.at[at], caches.at[at], sibling)

    arrive("extra_core", extras.at[0])
    arrive("cache_core", caches.at[pl.ds(0, CHIPS)])
    arrive("band_core", band.at[pl.ds(0, 16)])
    arrive("state_core", state.at[0])
    keep_extra.wait()
    keep_state.wait()
    for kind, ref in counts.items():
        await_bytes(ref, sent.at[kinds[kind]])


EXCHANGES = (
    "home_z",
    "home_x",
    "pair",
    "summary",
    "state",
    "state_core",
    "band_2",
    "band_4",
    "band_core",
    "cache_1",
    "cache_2",
    "cache_3",
    "cache_y",
    "cache_core",
    "extra_1",
    "extra_2",
    "extra_3",
    "extra_y",
    "extra_core",
)


def output_kernel(lengths, x, dt, dlog, write, read, gain, state, extra, out, run_rows, step_rows):
    step = pl.program_id(0)
    first = lax.axis_index("ctx") * TOK
    one, two = starts_of(lengths)
    one, two = one - first, two - first
    seen = same_causal(one, two)
    mask = jnp.where(seen, 1.0, 0.0).astype(BF16)
    bias = jnp.where(seen, 0.0, -jnp.inf)
    rates = dlog[...]

    @pl.when(step == 0)
    def _():
        run_rows[...] = nn(mask, rates).T
        step_rows[...] = dt[...].astype(F32).T

    t = iota((TOK, N), 0)
    new_one = (t >= one) & (t < two) & (one >= 0)
    new_two = (t >= two) & (two >= 0)
    spread = nn(rates, spread_matrix(step)).astype(BF16)
    run = nn(mask, spread)
    for b in range(HEADS // G):
        c = read[:, b * N : (b + 1) * N].astype(F32)
        c_in = jnp.where(new_one | new_two, 0.0, c).astype(BF16)
        c_one = jnp.where(new_one, c, 0.0).astype(BF16)
        c_two = jnp.where(new_two, c, 0.0).astype(BF16)
        both = nt(read[:, b * N : (b + 1) * N], write[:, b * N : (b + 1) * N])
        for j in range(G // 2):
            chunk = b * (G // 2) + j
            from_state = (
                nn(c_in, state[chunk % 2, chunk // 2])
                + nn(c_one, extra[chunk % 2, chunk // 2, 0])
                + nn(c_two, extra[chunk % 2, chunk // 2, 1])
            )
            for i in range(2):
                k = chunk * 2 + i
                lanes = slice(k * P_SIZE, (k + 1) * P_SIZE)
                at = pl.ds(step * HEADS + k, 1)
                run_t = run[:, lanes]
                decay = jnp.exp(run_t - run_rows[at, :] + bias)
                mixing = (both * decay * step_rows[at, :]).astype(BF16)
                x_h = x[:, lanes]
                result = (
                    nn(mixing, x_h)
                    + jnp.exp(run_t) * from_state[:, i * P_SIZE : (i + 1) * P_SIZE]
                    + gain[:, lanes] * x_h.astype(F32)
                )
                out[:, lanes] = result.astype(BF16)


def attention_kernel(
    lengths,
    history,
    queries,
    band,
    sinks,
    cache,
    out,
    keys,
    rows,
    scores,
    top,
    total,
    sums,
    bias,
    listed,
    sems,
):
    place = lax.axis_index("ctx")
    first = place * TOK
    one, two = starts_of(lengths)
    edges = [jnp.int32(0), one, two, jnp.int32(CTX * TOK)]
    lives = []
    for s in range(SEQS):
        begin = jnp.maximum(edges[s], first)
        present = begin < jnp.minimum(edges[s + 1], first + TOK)
        lives.append(
            [
                present
                & (begin - edges[s] < j * TOK + TOK - 1)
                & (history[0, s] - WINDOW + j * TOK + TOK - 1 >= SINKS)
                for j in range(4)
            ]
        )
    copies = [
        pltpu.make_async_copy(band, keys.at[pl.ds(0, 8 * SINK_BLOCK)], sems.at[0]),
        pltpu.make_async_copy(sinks, keys.at[pl.ds(8 * SINK_BLOCK, 8)], sems.at[1]),
    ]
    for copy in copies:
        copy.start()

    def history_copies(s):
        return [
            pltpu.make_async_copy(
                cache.at[:, kv, s],
                keys.at[pl.ds(8 * CACHE_BLOCK + 32 * s, 32), :, pl.ds(kv * KVH * HD, KVH * HD)],
                sems.at[2 + 2 * s + kv],
            )
            for kv in range(2)
        ]

    wanted = [lives[s][0] | lives[s][1] | lives[s][2] | lives[s][3] for s in range(SEQS)]
    for s in range(SEQS):

        @pl.when(wanted[s])
        def _():
            for copy in history_copies(s):
                copy.start()

    keys[8 * NULL_BLOCK :] = jnp.zeros((8, 16, 2 * KVH * HD), BF16)

    t = first + iota((TOK, TOK), 0)
    u = iota((TOK, TOK), 1)
    owner = segment(t, one, two)
    offset = t - jnp.where(owner == 2, two, jnp.where(owner == 1, one, 0))
    count = jnp.int32(0)
    head_owner = (first >= one).astype(I32) + (first >= two).astype(I32)
    for b in range(REACH + 1):
        pos = first + (b - REACH) * TOK + u
        gap = t - pos
        ok = (pos >= 0) & (segment(pos, one, two) == owner) & (gap >= 0) & (gap < WINDOW)
        bias[b] = jnp.where(ok, 0.0, -jnp.inf)
        end = first + (b - REACH) * TOK + TOK - 1
        end_owner = (end >= one).astype(I32) + (end >= two).astype(I32)
        live = (end >= 0) & (end_owner >= head_owner)
        listed[count] = b
        count = count + live.astype(I32)
    bias[SINK_BLOCK] = jnp.where(
        (u < SEQS * SINKS) & (u // SINKS == owner), 0.0, -jnp.inf
    )
    listed[count] = SINK_BLOCK
    count = count + 1
    for s in range(SEQS):
        for j in range(4):
            live = lives[s][j]
            block = CACHE_BLOCK + 4 * s + j

            @pl.when(live)
            def _():
                slot = j * TOK + u
                ok = (owner == s) & (slot > offset) & (history[0, s] - WINDOW + slot >= SINKS)
                bias[block] = jnp.where(ok, 0.0, -jnp.inf)

            listed[count] = block
            count = count + live.astype(I32)
    bias[NULL_BLOCK] = jnp.full((TOK, TOK), -jnp.inf, F32)
    listed[count] = NULL_BLOCK
    pairs = lax.div(count + 1, jnp.int32(2))
    for copy in copies:
        copy.wait()
    for s in range(SEQS):

        @pl.when(wanted[s])
        def _():
            for copy in history_copies(s):
                copy.wait()

    per = QH // KVH
    scale = 1.0 / math.sqrt(HD) / math.log(2.0)

    def one_head(number, nothing):
        lanes = pl.ds(pl.multiple_of(number * HD, HD), HD)
        value_lanes = pl.ds(pl.multiple_of(number * HD + KVH * HD, HD), HD)
        for r in range(per):
            wide = pl.ds(pl.multiple_of((number * per + r) * HD, HD), HD)
            rows[r * TOK : (r + 1) * TOK, :] = queries[:, wide]
        top[...] = jnp.full(top.shape, -jnp.inf, F32)
        total[...] = jnp.zeros(total.shape, F32)
        sums[...] = jnp.zeros(sums.shape, F32)

        def score(i, nothing):
            blocks = [listed[2 * i + part] for part in range(2)]
            key = [keys[pl.ds(b * 8, 8), :, lanes].reshape(TOK, HD) for b in blocks]
            key = jnp.concatenate(key, axis=0)
            left_bias, right_bias = bias[blocks[0]], bias[blocks[1]]
            for r in range(per):
                at = slice(r * TOK, (r + 1) * TOK)
                made = nt(rows[at, :], key) * scale
                left = made[:, :TOK] + left_bias
                right = made[:, TOK:] + right_bias
                scores[2 * i, at, :] = left
                scores[2 * i + 1, at, :] = right
                top[at, :] = jnp.maximum(top[at, :], jnp.maximum(left, right))
            return nothing

        lax.fori_loop(0, pairs, score, 0)
        top[...] = jnp.broadcast_to(jnp.max(top[...], axis=1, keepdims=True), top.shape)

        def weigh(i, nothing):
            values = []
            for part in range(2):
                block = listed[2 * i + part]
                values.append(keys[pl.ds(block * 8, 8), :, value_lanes].reshape(TOK, HD))
            value = jnp.concatenate(values, axis=0)
            for r in range(per):
                at = slice(r * TOK, (r + 1) * TOK)
                left = jnp.exp2(scores[2 * i, at, :] - top[at, :])
                right = jnp.exp2(scores[2 * i + 1, at, :] - top[at, :])
                total[at, :] += left + right
                both = jnp.concatenate([left.astype(BF16), right.astype(BF16)], axis=1)
                sums[at, :] += nn(both, value)
            return nothing

        lax.fori_loop(0, pairs, weigh, 0)
        for r in range(per):
            at = slice(r * TOK, (r + 1) * TOK)
            whole = jnp.sum(total[at, :], axis=1, keepdims=True)
            wide = pl.ds(pl.multiple_of((number * per + r) * HD, HD), HD)
            out[:, wide] = (sums[at, :] / whole).astype(BF16)
        return nothing

    lax.fori_loop(0, KVH, one_head, 0)


SMEM = pl.BlockSpec(memory_space=pltpu.SMEM)
VMEM = pl.BlockSpec(memory_space=pltpu.VMEM)
ANY = pl.BlockSpec(memory_space=pl.ANY)
LIMIT = pltpu.CompilerParams(vmem_limit_bytes=60 * 2**20)


def full(shape):
    return pl.BlockSpec(shape, lambda i: (0,) * len(shape))


def lane_block(rows, width):
    return pl.BlockSpec((rows, width), lambda i: (0, i))


def summaries(lengths, x, dt, dlog, write):
    return pl.pallas_call(
        summary_kernel,
        grid=(STEPS,),
        out_shape=jax.ShapeDtypeStruct((2, CHIPS, N + 8, PAIR), F32),
        in_specs=[
            SMEM,
            lane_block(TOK, WIDE),
            full((TOK, H)),
            full((TOK, H)),
            lane_block(TOK, 2 * N),
        ],
        out_specs=pl.BlockSpec((2, CHIPS // STEPS, N + 8, PAIR), lambda i: (0, i, 0, 0)),
        scratch_shapes=[pltpu.VMEM((H, TOK), F32)],
        compiler_params=LIMIT,
    )(lengths, x, dt, dlog, write)


def exchange(groups, home, lengths, saved, made, cache_keys, cache_values, turn_keys, turn_values):
    return pl.pallas_call(
        exchange_kernel,
        out_shape=(
            jax.ShapeDtypeStruct((2, CHIPS, N, PAIR), BF16),
            jax.ShapeDtypeStruct((2, CHIPS, 2, N, PAIR), BF16),
            jax.ShapeDtypeStruct((CTX, 2) + cache_keys.shape, BF16),
            jax.ShapeDtypeStruct((8 * (REACH + 1), 16, 2 * KVH * HD), BF16),
        ),
        in_specs=[SMEM, SMEM, ANY, VMEM, ANY, ANY, ANY, ANY],
        out_specs=(ANY, ANY, ANY, ANY),
        scratch_shapes=[
            pltpu.VMEM((CHIPS, N + 8, PAIR), F32),
            pltpu.VMEM((CHIPS, ROWS, PAIR), BF16),
            pltpu.VMEM((CHIPS, ROWS, PAIR), BF16),
            pltpu.VMEM((groups, SEQS, N, PAIR), BF16),
            pltpu.VMEM((CHIPS, N, PAIR), BF16),
            pltpu.VMEM((CHIPS, N, PAIR), BF16),
            pltpu.VMEM((CHIPS, N, PAIR), BF16),
            pltpu.VMEM((CHIPS, N, PAIR), BF16),
            pltpu.VMEM((2, N, PAIR), BF16),
            pltpu.VMEM((CHIPS, 2, N, PAIR), BF16),
            pltpu.SemaphoreType.DMA((len(EXCHANGES),)),
            pltpu.SemaphoreType.DMA((len(EXCHANGES),)),
            pltpu.SemaphoreType.DMA((5,)),
        ],
        compiler_params=pltpu.CompilerParams(
            collective_id=0, has_side_effects=True, vmem_limit_bytes=60 * 2**20
        ),
    )(home, lengths, saved, made, cache_keys, cache_values, turn_keys, turn_values)


def outputs(lengths, x, dt, dlog, write, read, gain, state, extra):
    return pl.pallas_call(
        output_kernel,
        grid=(STEPS,),
        out_shape=jax.ShapeDtypeStruct((TOK, H * P_SIZE), BF16),
        in_specs=[
            SMEM,
            lane_block(TOK, WIDE),
            full((TOK, H)),
            full((TOK, H)),
            lane_block(TOK, 2 * N),
            lane_block(TOK, 2 * N),
            lane_block(1, WIDE),
            pl.BlockSpec((2, CHIPS // STEPS, N, PAIR), lambda i: (0, i, 0, 0)),
            pl.BlockSpec((2, CHIPS // STEPS, 2, N, PAIR), lambda i: (0, i, 0, 0, 0)),
        ],
        out_specs=lane_block(TOK, WIDE),
        scratch_shapes=[pltpu.VMEM((H, TOK), F32), pltpu.VMEM((H, TOK), F32)],
        compiler_params=LIMIT,
    )(lengths, x, dt, dlog, write, read, gain, state, extra)


def attention(lengths, history, queries, band, sinks, cache):
    rows = (QH // KVH) * TOK
    return pl.pallas_call(
        attention_kernel,
        out_shape=jax.ShapeDtypeStruct((TOK, QH * HD), BF16),
        in_specs=[SMEM, SMEM, VMEM, ANY, ANY, ANY],
        out_specs=VMEM,
        scratch_shapes=[
            pltpu.VMEM((8 * BLOCKS, 16, 2 * KVH * HD), BF16),
            pltpu.VMEM((rows, HD), BF16),
            pltpu.VMEM((BLOCKS + 1, rows, TOK), F32),
            pltpu.VMEM((rows, TOK), F32),
            pltpu.VMEM((rows, TOK), F32),
            pltpu.VMEM((rows, HD), F32),
            pltpu.VMEM((BLOCKS, TOK, TOK), F32),
            pltpu.SMEM((BLOCKS + 1,), I32),
            pltpu.SemaphoreType.DMA((8,)),
        ],
        compiler_params=LIMIT,
        cost_estimate=pl.CostEstimate(
            flops=2_500_000_000, bytes_accessed=8_000_000, transcendentals=5_000_000
        ),
    )(lengths, history, queries, band, sinks, cache)


def shards(
    mamba_input,
    step_size,
    decay_log,
    state_write,
    state_read,
    skip_gain,
    saved_states,
    home_slot,
    turn_lengths,
    history_lengths,
    queries,
    turn_keys,
    turn_values,
    cache_keys,
    cache_values,
    sink_keys,
    sink_values,
):
    x, dt, dlog = mamba_input[0], step_size[0], decay_log[0]
    write, read = state_write[0], state_read[0]
    saved = saved_states[0].astype(BF16).reshape(SEQS, 2, P_SIZE, N)
    saved = saved.transpose(0, 3, 1, 2).reshape(SEQS, N, PAIR)
    sinks = jnp.concatenate(
        [sink_keys[0].reshape(SEQS * SINKS, -1), sink_values[0].reshape(SEQS * SINKS, -1)], axis=1
    )
    sinks = jnp.pad(sinks, ((0, TOK - SEQS * SINKS), (0, 0))).reshape(8, 16, 2 * KVH * HD)
    gain = jnp.repeat(skip_gain, P_SIZE)[None]

    made = summaries(turn_lengths, x, dt, dlog, write)
    groups = lax.axis_size("sess")
    state, extras, caches, band = exchange(
        groups,
        home_slot,
        turn_lengths,
        saved,
        made,
        cache_keys[0],
        cache_values[0],
        turn_keys[0].reshape(8, 16, KVH * HD),
        turn_values[0].reshape(8, 16, KVH * HD),
    )
    attended = attention(turn_lengths, history_lengths, queries[0], band, sinks, caches)
    mixed = outputs(turn_lengths, x, dt, dlog, write, read, gain, state, extras)
    return (mixed[None], attended[None])


def solution(mesh):
    token = P("sess", "ctx", None)
    spread = P("sess", None, "ctx", None)
    return jax.shard_map(
        shards,
        mesh=mesh,
        in_specs=(
            token,
            token,
            token,
            token,
            token,
            P(),
            spread,
            P(),
            P("sess", None),
            P("sess", None),
            token,
            token,
            token,
            spread,
            spread,
            P("sess", None, None, None),
            P("sess", None, None, None),
        ),
        out_specs=(token, token),
        check_vma=False,
    )
```

```python
import functools
import math

import jax
import jax.numpy as jnp
from jax import lax
from jax.experimental import pallas as pl
from jax.experimental.pallas import tpu as pltpu
from jax.sharding import PartitionSpec as P

TOK = 128
REACH = 4
SEQS = 3
SINKS = 4
H = 64
P_SIZE = 128
N = 64
G = 8
QH = 32
KVH = 4
HD = 128
WINDOW = 512
CTX = 32
CHIPS = CTX // 2
MESH = pl.DeviceIdType.MESH

F32 = jnp.float32
BF16 = jnp.bfloat16
I32 = jnp.int32
PAIR = 2 * P_SIZE
ROWS = N + 16
STEPS = 4
HEADS = H // STEPS
WIDE = HEADS * P_SIZE
BLOCKS = REACH + 1 + 1 + SEQS * 4 + 1
SINK_BLOCK = REACH + 1
CACHE_BLOCK = SINK_BLOCK + 1
NULL_BLOCK = BLOCKS - 1


def iota(shape, axis):
    return lax.broadcasted_iota(I32, shape, axis)


def nn(a, b):
    return lax.dot_general(a, b, (((1,), (0,)), ((), ())), preferred_element_type=F32)


def nt(a, b):
    return lax.dot_general(a, b, (((1,), (1,)), ((), ())), preferred_element_type=F32)


def starts_of(lengths):
    first = lengths[0, 0]
    return first, first + lengths[0, 1]


def segment(positions, one, two):
    return (positions >= one).astype(I32) + (positions >= two).astype(I32)


def same_causal(one, two):
    t, u = iota((TOK, TOK), 0), iota((TOK, TOK), 1)
    return (segment(t, one, two) == segment(u, one, two)) & (t >= u)


def spread_matrix(step):
    rows = iota((H, WIDE), 0)
    lanes = iota((H, WIDE), 1)
    return jnp.where(rows == step * HEADS + lanes // P_SIZE, 1.0, 0.0).astype(BF16)


def await_bytes(ref, sem):
    pltpu.make_async_copy(ref, ref, sem).wait()


def exchange_kernel(
    home,
    lengths,
    saved,
    x,
    steps,
    rates,
    write,
    cache_keys,
    cache_values,
    turn_keys,
    turn_values,
    state,
    extras,
    caches,
    band,
    inputs,
    weight,
    made,
    theirs,
    packed,
    recv,
    stored,
    entering,
    arrived,
    own_state,
    other_state,
    extra,
    plane,
    sent,
    got,
    local,
):
    group, me = lax.axis_index("sess"), lax.axis_index("ctx")
    across, deep = group // 2, group % 2
    y, z, core = me // 8, (me // 2) % 4, me % 2
    chip = me // 2
    sibling = me + 1 - 2 * core
    partner = group + 1 - 2 * deep
    x_groups = [((across + i) % 4) * 2 + deep for i in range(1, 4)]
    y_peers = [((y + i) % 4) * 8 + z * 2 + core for i in range(1, 4)]
    z_before = y * 8 + ((z + 3) % 4) * 2 + core
    z_after = [y * 8 + ((z + i) % 4) * 2 + core for i in range(1, 4)]
    onward = (me + 2) % CTX
    kinds = {name: i for i, name in enumerate(EXCHANGES)}

    def copy_in(src, dst, at):
        copy = pltpu.make_async_copy(src, dst, local.at[at])
        copy.start()
        return copy

    half = KVH * HD
    mine = [
        copy_in(cache_keys, caches.at[me, 0], 0),
        copy_in(cache_values, caches.at[me, 1], 1),
        copy_in(turn_keys, band.at[pl.ds(8 * REACH, 8), :, pl.ds(0, half)], 2),
        copy_in(turn_values, band.at[pl.ds(8 * REACH, 8), :, pl.ds(half, half)], 3),
        copy_in(saved, stored.at[group], 4),
        copy_in(x, inputs, 5),
    ]

    barrier = pltpu.get_barrier_semaphore()

    def greet(i, nothing):
        peer = ((chip + i) % CHIPS) * 2 + core
        pl.semaphore_signal(barrier, inc=1, device_id=(group, peer), device_id_type=MESH)
        return nothing

    lax.fori_loop(1, CHIPS, greet, 0)
    pl.semaphore_signal(barrier, inc=1, device_id=(group, sibling), device_id_type=MESH)
    for to in [partner] + x_groups:
        pl.semaphore_signal(barrier, inc=1, device_id=(to, me), device_id_type=MESH)
    pl.semaphore_wait(barrier, CHIPS - 1 + 1 + 4)

    def push(kind, src, dst, peer, to=None):
        at = kinds[kind]
        pltpu.make_async_remote_copy(
            src_ref=src,
            dst_ref=dst,
            send_sem=sent.at[at],
            recv_sem=got.at[at],
            device_id=(group if to is None else to, peer),
            device_id_type=MESH,
        ).start()

    counts = {}

    def arrive(kind, ref):
        counts[kind] = ref
        await_bytes(ref, got.at[kinds[kind]])

    def slot(distance):
        return band.at[pl.ds(8 * (REACH - distance), 8)]

    def spread(name, array, at):
        for to in y_peers:
            push(name + "_y", array.at[at], array.at[at], to)

    push("home_z", saved, stored.at[group], me, partner)
    for to in x_groups:
        push("home_x", saved, stored.at[group], me, to)
    mine[2].wait()
    mine[3].wait()
    push("band_2", slot(0), slot(2), onward)
    mine[0].wait()
    mine[1].wait()
    push("cache_1", caches.at[me], caches.at[me], z_before)
    spread("cache", caches, me)
    push("cache_core", caches.at[me], caches.at[me], sibling)

    one, two = starts_of(lengths)
    here_one, here_two = one - me * TOK, two - me * TOK
    mask = jnp.where(same_causal(here_one, here_two), 1.0, 0.0).astype(BF16)
    run = nt(rates[...], mask)
    u = iota((1, TOK), 1)
    last = (TOK - 1 >= here_one).astype(I32) + (TOK - 1 >= here_two).astype(I32)
    held = segment(u, here_one, here_two) == last
    gap = jnp.where(held, run[:, TOK - 1 :] - run, -jnp.inf)
    weight[...] = jnp.exp(gap) * steps[...].astype(F32)
    turned_rates = rates[...].astype(F32).T.astype(BF16)
    mine[5].wait()

    def summarize(step, nothing):
        turned = write[:, pl.ds(pl.multiple_of(step * 2 * N, 2 * N), 2 * N)].astype(F32).T
        spread_rates = nn(turned_rates, spread_matrix(step)).astype(BF16)
        carry = jnp.exp(nn(mask[TOK - 16 :], spread_rates)[15:16])
        for k in range(HEADS):
            row = weight[pl.ds(step * HEADS + k, 1), :]
            b = k // G
            loads = (row * turned[b * N : (b + 1) * N]).astype(BF16)
            at = pl.multiple_of(step * WIDE + k * P_SIZE, P_SIZE)
            lane = (k % 2) * P_SIZE
            j = k // 2
            made[j % 2, step * (CHIPS // STEPS) + j // 2, :N, lane : lane + P_SIZE] = nn(
                loads, inputs[:, pl.ds(at, P_SIZE)]
            )
        for j in range(HEADS // 2):
            row = carry[:, j * PAIR : (j + 1) * PAIR]
            made[j % 2, step * (CHIPS // STEPS) + j // 2, N:, :] = jnp.broadcast_to(row, (8, PAIR))
        part = pl.ds(step * (CHIPS // STEPS), CHIPS // STEPS)
        push("pair", made.at[1 - core, part], theirs.at[part], sibling)
        return nothing

    lax.fori_loop(0, STEPS, summarize, 0)

    arrive("home_z", stored.at[0])
    for to in x_groups:
        push("home_x", stored.at[partner], stored.at[partner], me, to)

    def inside(c):
        end = c * TOK + TOK - 1
        first = (end >= one) & (end < two) & (one >= c * TOK)
        second = (end >= two) & (two >= c * TOK)
        return first, second

    arrive("pair", theirs)
    first_one, first_two = inside(2 * chip)
    last_one, last_two = inside(2 * chip + 1)
    fresh = last_one | last_two

    def both(m):
        own = made[core, m]
        other = theirs[m]
        even = jnp.where(core == 0, own, other)
        odd = jnp.where(core == 0, other, own)
        return even, odd

    def combine(i, nothing):
        m = (chip + i) % CHIPS
        even, odd = both(m)
        factor = odd[N : N + 1]
        total = odd[:N] + jnp.where(fresh, 0.0, factor) * even[:N]
        carry = factor * jnp.where(fresh, 1.0, even[N : N + 1])
        packed[m, :N, :] = total.astype(BF16)
        high = carry.astype(BF16).astype(F32)
        tile = iota((16, PAIR), 0)
        rows = jnp.where(tile == 0, high, jnp.where(tile == 1, carry - high, 0.0))
        packed[m, N:, :] = rows.astype(BF16)

        @pl.when(i != 0)
        def _():
            push("summary", packed.at[m], recv.at[chip], 2 * m + core)

        return nothing

    lax.fori_loop(0, CHIPS, combine, 0)
    own_summary = copy_in(packed.at[chip], recv.at[chip], 0)

    arrive("cache_1", caches.at[0])
    push("cache_2", caches.at[z_after[0]], caches.at[z_after[0]], z_before)
    spread("cache", caches, z_after[0])
    push("cache_core", caches.at[z_after[0]], caches.at[z_after[0]], sibling)
    arrive("band_2", slot(2))
    push("band_4", slot(2), slot(4), onward)

    mine[4].wait()
    arrive("home_x", stored.at[pl.ds(0, 6)])
    back = []
    for s in range(SEQS):
        at = home[group * SEQS + s]
        back.append(stored[at // SEQS, at % SEQS].astype(F32))
    extra[0] = back[1].astype(BF16)
    extra[1] = back[2].astype(BF16)
    push("extra_1", extra, plane.at[chip], z_before)
    for to in y_peers:
        push("extra_y", extra, plane.at[chip], to)
    own_extra = copy_in(extra, plane.at[chip], 1)

    arrive("cache_2", caches.at[0])
    push("cache_3", caches.at[z_after[1]], caches.at[z_after[1]], z_before)
    spread("cache", caches, z_after[1])
    push("cache_core", caches.at[z_after[1]], caches.at[z_after[1]], sibling)

    arrive("extra_1", plane.at[0])
    push("extra_2", plane.at[z_after[0] // 2], plane.at[z_after[0] // 2], z_before)
    spread("extra", plane, z_after[0] // 2)
    arrive("extra_2", plane.at[0])
    push("extra_3", plane.at[z_after[1] // 2], plane.at[z_after[1] // 2], z_before)
    spread("extra", plane, z_after[1] // 2)
    arrive("summary", recv.at[pl.ds(0, CHIPS - 1)])
    own_summary.wait()

    def turn(m, held):
        entering[m] = held.astype(BF16)

        @pl.when(m != chip)
        def _():
            push("state", entering.at[m], arrived.at[chip], 2 * m + core)

        even_one, even_two = inside(2 * m)
        odd_one, odd_two = inside(2 * m + 1)
        base = jnp.where(even_two, back[2], jnp.where(even_one, back[1], held))
        base = jnp.where(odd_two, back[2], jnp.where(odd_one, back[1], base))
        carry = recv[m, N : N + 16, :].astype(F32)
        return (carry[0:1] + carry[1:2]) * base + recv[m, :N, :].astype(F32)

    lax.fori_loop(0, CHIPS, turn, back[0])
    own_entering = copy_in(entering.at[chip], arrived.at[chip], 2)


    arrive("extra_3", plane.at[0])
    spread("extra", plane, z_after[2] // 2)
    arrive("cache_3", caches.at[0])
    spread("cache", caches, z_after[2])
    push("cache_core", caches.at[z_after[2]], caches.at[z_after[2]], sibling)
    arrive("band_4", slot(4))
    push("band_core", slot(2 * core), slot(1), sibling)
    push("band_core", slot(2 * core + 2), slot(3), sibling)
    own_extra.wait()
    arrive("extra_y", plane.at[pl.ds(0, 12)])
    push("extra_core", plane, extras.at[core], sibling)
    keep_extra = copy_in(plane, extras.at[core], 0)
    arrive("state", arrived.at[pl.ds(0, CHIPS - 1)])
    own_entering.wait()

    def settle(m, nothing):
        even, _ = both(m)
        first = arrived[m].astype(F32)
        base = jnp.where(
            first_two,
            plane[m, 1].astype(F32),
            jnp.where(first_one, plane[m, 0].astype(F32), first),
        )
        second = even[N : N + 1] * base + even[:N]
        own_state[m] = jnp.where(core == 0, first, second).astype(BF16)
        other_state[m] = jnp.where(core == 0, second, first).astype(BF16)
        return nothing

    lax.fori_loop(0, CHIPS, settle, 0)
    push("state_core", other_state, state.at[core], sibling)
    keep_state = copy_in(own_state, state.at[core], 1)
    arrive("cache_y", caches.at[pl.ds(0, 12)])
    for i in range(4):
        for j in range(1, 4):
            at = ((y + j) % 4) * 8 + ((z + i) % 4) * 2 + core
            push("cache_core", caches.at[at], caches.at[at], sibling)

    arrive("extra_core", extras.at[0])
    arrive("cache_core", caches.at[pl.ds(0, CHIPS)])
    arrive("band_core", band.at[pl.ds(0, 16)])
    arrive("state_core", state.at[0])
    keep_extra.wait()
    keep_state.wait()
    for kind, ref in counts.items():
        await_bytes(ref, sent.at[kinds[kind]])


EXCHANGES = (
    "home_z",
    "home_x",
    "pair",
    "summary",
    "state",
    "state_core",
    "band_2",
    "band_4",
    "band_core",
    "cache_1",
    "cache_2",
    "cache_3",
    "cache_y",
    "cache_core",
    "extra_1",
    "extra_2",
    "extra_3",
    "extra_y",
    "extra_core",
)


def output_kernel(lengths, gain, x, steps, rates, write, read, state, extra, out, run_rows, step_rows):
    step = pl.program_id(0)
    first = lax.axis_index("ctx") * TOK
    one, two = starts_of(lengths)
    one, two = one - first, two - first
    seen = same_causal(one, two)
    mask = jnp.where(seen, 1.0, 0.0).astype(BF16)
    bias = jnp.where(seen, 0.0, -jnp.inf)

    @pl.when(step == 0)
    def _():
        run_rows[...] = nt(rates[...], mask)
        step_rows[...] = steps[...].astype(F32)

    t = iota((TOK, N), 0)
    new_one = (t >= one) & (t < two) & (one >= 0)
    new_two = (t >= two) & (two >= 0)
    turned = rates[...].astype(F32).T.astype(BF16)
    run = nn(mask, nn(turned, spread_matrix(step)).astype(BF16))
    for b in range(HEADS // G):
        c = read[:, b * N : (b + 1) * N].astype(F32)
        c_in = jnp.where(new_one | new_two, 0.0, c).astype(BF16)
        c_one = jnp.where(new_one, c, 0.0).astype(BF16)
        c_two = jnp.where(new_two, c, 0.0).astype(BF16)
        both = nt(read[:, b * N : (b + 1) * N], write[:, b * N : (b + 1) * N])
        for j in range(G // 2):
            chunk = b * (G // 2) + j
            from_state = (
                nn(c_in, state[chunk % 2, chunk // 2])
                + nn(c_one, extra[chunk % 2, chunk // 2, 0])
                + nn(c_two, extra[chunk % 2, chunk // 2, 1])
            )
            for i in range(2):
                k = chunk * 2 + i
                lanes = slice(k * P_SIZE, (k + 1) * P_SIZE)
                at = pl.ds(step * HEADS + k, 1)
                run_t = run[:, lanes]
                decay = jnp.exp(run_t - run_rows[at, :] + bias)
                mixing = (both * decay * step_rows[at, :]).astype(BF16)
                x_h = x[:, lanes]
                result = (
                    nn(mixing, x_h)
                    + jnp.exp(run_t) * from_state[:, i * P_SIZE : (i + 1) * P_SIZE]
                    + gain[step * HEADS + k] * x_h.astype(F32)
                )
                out[:, lanes] = result.astype(BF16)


def attention_kernel(
    lengths,
    history,
    queries,
    band,
    sink_keys,
    sink_values,
    cache,
    out,
    keys,
    rows,
    scores,
    top,
    total,
    sums,
    bias,
    listed,
    sems,
):
    place = lax.axis_index("ctx")
    first = place * TOK
    one, two = starts_of(lengths)
    edges = [jnp.int32(0), one, two, jnp.int32(CTX * TOK)]
    lives = []
    for s in range(SEQS):
        begin = jnp.maximum(edges[s], first)
        present = begin < jnp.minimum(edges[s + 1], first + TOK)
        lives.append(
            [
                present
                & (begin - edges[s] < j * TOK + TOK - 1)
                & (history[0, s] - WINDOW + j * TOK + TOK - 1 >= SINKS)
                for j in range(4)
            ]
        )
    copies = [
        pltpu.make_async_copy(band, keys.at[pl.ds(0, 8 * SINK_BLOCK)], sems.at[0]),
    ]
    for copy in copies:
        copy.start()

    def history_copies(s):
        return [
            pltpu.make_async_copy(
                cache.at[:, kv, s],
                keys.at[pl.ds(8 * CACHE_BLOCK + 32 * s, 32), :, pl.ds(kv * KVH * HD, KVH * HD)],
                sems.at[2 + 2 * s + kv],
            )
            for kv in range(2)
        ]

    wanted = [lives[s][0] | lives[s][1] | lives[s][2] | lives[s][3] for s in range(SEQS)]
    for s in range(SEQS):

        @pl.when(wanted[s])
        def _():
            for copy in history_copies(s):
                copy.start()

    keys[8 * NULL_BLOCK :] = jnp.zeros((8, 16, 2 * KVH * HD), BF16)
    half = KVH * HD
    keys[8 * SINK_BLOCK + 1 : 8 * CACHE_BLOCK] = jnp.zeros((7, 16, 2 * half), BF16)
    for kv, sinks in enumerate((sink_keys, sink_values)):
        parts = [sinks[s].astype(F32) for s in range(SEQS)] + [jnp.zeros((4, half), F32)]
        both = jnp.concatenate(parts, axis=0).astype(BF16)
        keys[8 * SINK_BLOCK, :, kv * half : (kv + 1) * half] = both

    t = first + iota((TOK, TOK), 0)
    u = iota((TOK, TOK), 1)
    owner = segment(t, one, two)
    offset = t - jnp.where(owner == 2, two, jnp.where(owner == 1, one, 0))
    count = jnp.int32(0)
    head_owner = (first >= one).astype(I32) + (first >= two).astype(I32)
    for b in range(REACH + 1):
        pos = first + (b - REACH) * TOK + u
        gap = t - pos
        ok = (pos >= 0) & (segment(pos, one, two) == owner) & (gap >= 0) & (gap < WINDOW)
        bias[b] = jnp.where(ok, 0.0, -jnp.inf)
        end = first + (b - REACH) * TOK + TOK - 1
        end_owner = (end >= one).astype(I32) + (end >= two).astype(I32)
        live = (end >= 0) & (end_owner >= head_owner)
        listed[count] = b
        count = count + live.astype(I32)
    bias[SINK_BLOCK] = jnp.where(
        (u < SEQS * SINKS) & (u // SINKS == owner), 0.0, -jnp.inf
    )
    listed[count] = SINK_BLOCK
    count = count + 1
    for s in range(SEQS):
        for j in range(4):
            live = lives[s][j]
            block = CACHE_BLOCK + 4 * s + j

            @pl.when(live)
            def _():
                slot = j * TOK + u
                ok = (owner == s) & (slot > offset) & (history[0, s] - WINDOW + slot >= SINKS)
                bias[block] = jnp.where(ok, 0.0, -jnp.inf)

            listed[count] = block
            count = count + live.astype(I32)
    bias[NULL_BLOCK] = jnp.full((TOK, TOK), -jnp.inf, F32)
    listed[count] = NULL_BLOCK
    pairs = lax.div(count + 1, jnp.int32(2))
    for copy in copies:
        copy.wait()
    for s in range(SEQS):

        @pl.when(wanted[s])
        def _():
            for copy in history_copies(s):
                copy.wait()

    per = QH // KVH
    scale = 1.0 / math.sqrt(HD) / math.log(2.0)

    def one_head(number, nothing):
        lanes = pl.ds(pl.multiple_of(number * HD, HD), HD)
        value_lanes = pl.ds(pl.multiple_of(number * HD + KVH * HD, HD), HD)
        for r in range(per):
            wide = pl.ds(pl.multiple_of((number * per + r) * HD, HD), HD)
            rows[r * TOK : (r + 1) * TOK, :] = queries[:, wide]
        top[...] = jnp.full(top.shape, -jnp.inf, F32)
        total[...] = jnp.zeros(total.shape, F32)
        sums[...] = jnp.zeros(sums.shape, F32)

        def score(i, nothing):
            blocks = [listed[2 * i + part] for part in range(2)]
            key = [keys[pl.ds(b * 8, 8), :, lanes].reshape(TOK, HD) for b in blocks]
            key = jnp.concatenate(key, axis=0)
            left_bias, right_bias = bias[blocks[0]], bias[blocks[1]]
            for r in range(per):
                at = slice(r * TOK, (r + 1) * TOK)
                made = nt(rows[at, :], key) * scale
                left = made[:, :TOK] + left_bias
                right = made[:, TOK:] + right_bias
                scores[2 * i, at, :] = left
                scores[2 * i + 1, at, :] = right
                top[at, :] = jnp.maximum(top[at, :], jnp.maximum(left, right))
            return nothing

        lax.fori_loop(0, pairs, score, 0)
        top[...] = jnp.broadcast_to(jnp.max(top[...], axis=1, keepdims=True), top.shape)

        def weigh(i, nothing):
            values = []
            for part in range(2):
                block = listed[2 * i + part]
                values.append(keys[pl.ds(block * 8, 8), :, value_lanes].reshape(TOK, HD))
            value = jnp.concatenate(values, axis=0)
            for r in range(per):
                at = slice(r * TOK, (r + 1) * TOK)
                left = jnp.exp2(scores[2 * i, at, :] - top[at, :])
                right = jnp.exp2(scores[2 * i + 1, at, :] - top[at, :])
                total[at, :] += left + right
                both = jnp.concatenate([left.astype(BF16), right.astype(BF16)], axis=1)
                sums[at, :] += nn(both, value)
            return nothing

        lax.fori_loop(0, pairs, weigh, 0)
        for r in range(per):
            at = slice(r * TOK, (r + 1) * TOK)
            whole = jnp.sum(total[at, :], axis=1, keepdims=True)
            wide = pl.ds(pl.multiple_of((number * per + r) * HD, HD), HD)
            out[:, wide] = (sums[at, :] / whole).astype(BF16)
        return nothing

    lax.fori_loop(0, KVH, one_head, 0)


SMEM = pl.BlockSpec(memory_space=pltpu.SMEM)
VMEM = pl.BlockSpec(memory_space=pltpu.VMEM)
ANY = pl.BlockSpec(memory_space=pl.ANY)
LIMIT = pltpu.CompilerParams(vmem_limit_bytes=60 * 2**20)


def full(shape):
    return pl.BlockSpec(shape, lambda i: (0,) * len(shape))


def lane_block(rows, width):
    return pl.BlockSpec((rows, width), lambda i: (0, i))


def exchange(
    groups,
    home,
    lengths,
    saved,
    x,
    steps,
    rates,
    write,
    cache_keys,
    cache_values,
    turn_keys,
    turn_values,
):
    return pl.pallas_call(
        exchange_kernel,
        out_shape=(
            jax.ShapeDtypeStruct((2, CHIPS, N, PAIR), BF16),
            jax.ShapeDtypeStruct((2, CHIPS, 2, N, PAIR), BF16),
            jax.ShapeDtypeStruct((CTX, 2) + cache_keys.shape, BF16),
            jax.ShapeDtypeStruct((8 * (REACH + 1), 16, 2 * KVH * HD), BF16),
        ),
        in_specs=[SMEM, SMEM, ANY, ANY, VMEM, VMEM, VMEM, ANY, ANY, ANY, ANY],
        out_specs=(ANY, ANY, ANY, ANY),
        scratch_shapes=[
            pltpu.VMEM((TOK, H * P_SIZE), BF16),
            pltpu.VMEM((H, TOK), F32),
            pltpu.VMEM((2, CHIPS, N + 8, PAIR), F32),
            pltpu.VMEM((CHIPS, N + 8, PAIR), F32),
            pltpu.VMEM((CHIPS, ROWS, PAIR), BF16),
            pltpu.VMEM((CHIPS, ROWS, PAIR), BF16),
            pltpu.VMEM((groups, SEQS, N, PAIR), BF16),
            pltpu.VMEM((CHIPS, N, PAIR), BF16),
            pltpu.VMEM((CHIPS, N, PAIR), BF16),
            pltpu.VMEM((CHIPS, N, PAIR), BF16),
            pltpu.VMEM((CHIPS, N, PAIR), BF16),
            pltpu.VMEM((2, N, PAIR), BF16),
            pltpu.VMEM((CHIPS, 2, N, PAIR), BF16),
            pltpu.SemaphoreType.DMA((len(EXCHANGES),)),
            pltpu.SemaphoreType.DMA((len(EXCHANGES),)),
            pltpu.SemaphoreType.DMA((6,)),
        ],
        compiler_params=pltpu.CompilerParams(
            collective_id=0, has_side_effects=True, vmem_limit_bytes=60 * 2**20
        ),
    )(
        home,
        lengths,
        saved,
        x,
        steps,
        rates,
        write,
        cache_keys,
        cache_values,
        turn_keys,
        turn_values,
    )


def outputs(lengths, gain, x, steps, rates, write, read, state, extra):
    return pl.pallas_call(
        output_kernel,
        grid=(STEPS,),
        out_shape=jax.ShapeDtypeStruct((TOK, H * P_SIZE), BF16),
        in_specs=[
            SMEM,
            SMEM,
            lane_block(TOK, WIDE),
            full((H, TOK)),
            full((H, TOK)),
            lane_block(TOK, 2 * N),
            lane_block(TOK, 2 * N),
            pl.BlockSpec((2, CHIPS // STEPS, N, PAIR), lambda i: (0, i, 0, 0)),
            pl.BlockSpec((2, CHIPS // STEPS, 2, N, PAIR), lambda i: (0, i, 0, 0, 0)),
        ],
        out_specs=lane_block(TOK, WIDE),
        scratch_shapes=[pltpu.VMEM((H, TOK), F32), pltpu.VMEM((H, TOK), F32)],
        compiler_params=LIMIT,
    )(lengths, gain, x, steps, rates, write, read, state, extra)


def attention(lengths, history, queries, band, sink_keys, sink_values, cache):
    rows = (QH // KVH) * TOK
    return pl.pallas_call(
        attention_kernel,
        out_shape=jax.ShapeDtypeStruct((TOK, QH * HD), BF16),
        in_specs=[SMEM, SMEM, VMEM, ANY, VMEM, VMEM, ANY],
        out_specs=VMEM,
        scratch_shapes=[
            pltpu.VMEM((8 * BLOCKS, 16, 2 * KVH * HD), BF16),
            pltpu.VMEM((rows, HD), BF16),
            pltpu.VMEM((BLOCKS + 1, rows, TOK), F32),
            pltpu.VMEM((rows, TOK), F32),
            pltpu.VMEM((rows, TOK), F32),
            pltpu.VMEM((rows, HD), F32),
            pltpu.VMEM((BLOCKS, TOK, TOK), F32),
            pltpu.SMEM((BLOCKS + 1,), I32),
            pltpu.SemaphoreType.DMA((8,)),
        ],
        compiler_params=LIMIT,
        cost_estimate=pl.CostEstimate(
            flops=2_500_000_000, bytes_accessed=8_000_000, transcendentals=5_000_000
        ),
    )(lengths, history, queries, band, sink_keys, sink_values, cache)


def shards(
    mamba_input,
    step_size,
    decay_log,
    state_write,
    state_read,
    skip_gain,
    saved_states,
    home_slot,
    turn_lengths,
    history_lengths,
    queries,
    turn_keys,
    turn_values,
    cache_keys,
    cache_values,
    sink_keys,
    sink_values,
):
    x, steps, rates = mamba_input[0], step_size[0].T, decay_log[0].T
    write, read = state_write[0], state_read[0]
    saved = saved_states[0].astype(BF16).reshape(SEQS, 2, P_SIZE, N)
    saved = saved.transpose(0, 3, 1, 2).reshape(SEQS, N, PAIR)

    groups = lax.axis_size("sess")
    state, extras, caches, band = exchange(
        groups,
        home_slot,
        turn_lengths,
        saved,
        x,
        steps,
        rates,
        write,
        cache_keys[0],
        cache_values[0],
        turn_keys[0].reshape(8, 16, KVH * HD),
        turn_values[0].reshape(8, 16, KVH * HD),
    )
    attended = attention(
        turn_lengths, history_lengths, queries[0], band, sink_keys[0], sink_values[0], caches
    )
    mixed = outputs(turn_lengths, skip_gain, x, steps, rates, write, read, state, extras)
    return (mixed[None], attended[None])


def solution(mesh):
    token = P("sess", "ctx", None)
    spread = P("sess", None, "ctx", None)
    return jax.shard_map(
        shards,
        mesh=mesh,
        in_specs=(
            token,
            token,
            token,
            token,
            token,
            P(),
            spread,
            P(),
            P("sess", None),
            P("sess", None),
            token,
            token,
            token,
            spread,
            spread,
            P("sess", None, None, None),
            P("sess", None, None, None),
        ),
        out_specs=(token, token),
        check_vma=False,
    )
```

```python
import functools
import math

import jax
import jax.numpy as jnp
from jax import lax
from jax.experimental import pallas as pl
from jax.experimental.pallas import tpu as pltpu
from jax.sharding import PartitionSpec as P

TOK = 128
REACH = 4
SEQS = 3
SINKS = 4
H = 64
P_SIZE = 128
N = 64
G = 8
QH = 32
KVH = 4
HD = 128
WINDOW = 512
CTX = 32
CHIPS = CTX // 2
MESH = pl.DeviceIdType.MESH

F32 = jnp.float32
BF16 = jnp.bfloat16
I32 = jnp.int32
PAIR = 2 * P_SIZE
ROWS = N + 16
STEPS = 4
HEADS = H // STEPS
WIDE = HEADS * P_SIZE
BLOCKS = REACH + 1 + 1 + SEQS * 4 + 1
SINK_BLOCK = REACH + 1
CACHE_BLOCK = SINK_BLOCK + 1
NULL_BLOCK = BLOCKS - 1


def iota(shape, axis):
    return lax.broadcasted_iota(I32, shape, axis)


def nn(a, b):
    return lax.dot_general(a, b, (((1,), (0,)), ((), ())), preferred_element_type=F32)


def nt(a, b):
    return lax.dot_general(a, b, (((1,), (1,)), ((), ())), preferred_element_type=F32)


def starts_of(lengths):
    first = lengths[0, 0]
    return first, first + lengths[0, 1]


def segment(positions, one, two):
    return (positions >= one).astype(I32) + (positions >= two).astype(I32)


def same_causal(one, two):
    t, u = iota((TOK, TOK), 0), iota((TOK, TOK), 1)
    return (segment(t, one, two) == segment(u, one, two)) & (t >= u)


def spread_matrix(step):
    rows = iota((H, WIDE), 0)
    lanes = iota((H, WIDE), 1)
    return jnp.where(rows == step * HEADS + lanes // P_SIZE, 1.0, 0.0).astype(BF16)


def await_bytes(ref, sem):
    pltpu.make_async_copy(ref, ref, sem).wait()


def exchange_kernel(
    home,
    lengths,
    gain,
    saved,
    x,
    steps,
    rates,
    write,
    read,
    cache_keys,
    cache_values,
    turn_keys,
    turn_values,
    state,
    extras,
    caches,
    band,
    partial,
    inputs,
    weight,
    run_rows,
    step_rows,
    inner,
    made,
    theirs,
    packed,
    recv,
    stored,
    entering,
    arrived,
    own_state,
    other_state,
    extra,
    plane,
    sent,
    got,
    local,
):
    group, me = lax.axis_index("sess"), lax.axis_index("ctx")
    across, deep = group // 2, group % 2
    y, z, core = me // 8, (me // 2) % 4, me % 2
    chip = me // 2
    sibling = me + 1 - 2 * core
    partner = group + 1 - 2 * deep
    x_groups = [((across + i) % 4) * 2 + deep for i in range(1, 4)]
    y_peers = [((y + i) % 4) * 8 + z * 2 + core for i in range(1, 4)]
    z_before = y * 8 + ((z + 3) % 4) * 2 + core
    z_after = [y * 8 + ((z + i) % 4) * 2 + core for i in range(1, 4)]
    onward = (me + 2) % CTX
    kinds = {name: i for i, name in enumerate(EXCHANGES)}

    def copy_in(src, dst, at):
        copy = pltpu.make_async_copy(src, dst, local.at[at])
        copy.start()
        return copy

    half = KVH * HD
    mine = [
        copy_in(cache_keys, caches.at[me, 0], 0),
        copy_in(cache_values, caches.at[me, 1], 1),
        copy_in(turn_keys, band.at[pl.ds(8 * REACH, 8), :, pl.ds(0, half)], 2),
        copy_in(turn_values, band.at[pl.ds(8 * REACH, 8), :, pl.ds(half, half)], 3),
        copy_in(saved, stored.at[group], 4),
        copy_in(x, inputs, 5),
    ]

    barrier = pltpu.get_barrier_semaphore()

    def greet(i, nothing):
        peer = ((chip + i) % CHIPS) * 2 + core
        pl.semaphore_signal(barrier, inc=1, device_id=(group, peer), device_id_type=MESH)
        return nothing

    lax.fori_loop(1, CHIPS, greet, 0)
    pl.semaphore_signal(barrier, inc=1, device_id=(group, sibling), device_id_type=MESH)
    for to in [partner] + x_groups:
        pl.semaphore_signal(barrier, inc=1, device_id=(to, me), device_id_type=MESH)
    pl.semaphore_wait(barrier, CHIPS - 1 + 1 + 4)

    def push(kind, src, dst, peer, to=None):
        at = kinds[kind]
        pltpu.make_async_remote_copy(
            src_ref=src,
            dst_ref=dst,
            send_sem=sent.at[at],
            recv_sem=got.at[at],
            device_id=(group if to is None else to, peer),
            device_id_type=MESH,
        ).start()

    counts = {}

    def arrive(kind, ref):
        counts[kind] = ref
        await_bytes(ref, got.at[kinds[kind]])

    def slot(distance):
        return band.at[pl.ds(8 * (REACH - distance), 8)]

    def spread(name, array, at):
        for to in y_peers:
            push(name + "_y", array.at[at], array.at[at], to)

    push("home_z", saved, stored.at[group], me, partner)
    for to in x_groups:
        push("home_x", saved, stored.at[group], me, to)
    mine[2].wait()
    mine[3].wait()
    push("band_2", slot(0), slot(2), onward)
    mine[0].wait()
    mine[1].wait()
    push("cache_1", caches.at[me], caches.at[me], z_before)
    spread("cache", caches, me)
    push("cache_core", caches.at[me], caches.at[me], sibling)

    one, two = starts_of(lengths)
    here_one, here_two = one - me * TOK, two - me * TOK
    seen = same_causal(here_one, here_two)
    mask = jnp.where(seen, 1.0, 0.0).astype(BF16)
    bias = jnp.where(seen, 0.0, -jnp.inf)
    run = nt(rates[...], mask)
    run_rows[...] = run
    step_rows[...] = steps[...].astype(F32)
    u = iota((1, TOK), 1)
    last = (TOK - 1 >= here_one).astype(I32) + (TOK - 1 >= here_two).astype(I32)
    held = segment(u, here_one, here_two) == last
    gap = jnp.where(held, run[:, TOK - 1 :] - run, -jnp.inf)
    weight[...] = jnp.exp(gap) * steps[...].astype(F32)
    turned_rates = rates[...].astype(F32).T.astype(BF16)
    mine[5].wait()

    def summarize(step, nothing):
        turned = write[:, pl.ds(pl.multiple_of(step * 2 * N, 2 * N), 2 * N)].astype(F32).T
        spread_rates = nn(turned_rates, spread_matrix(step)).astype(BF16)
        carry = jnp.exp(nn(mask[TOK - 16 :], spread_rates)[15:16])
        for k in range(HEADS):
            row = weight[pl.ds(step * HEADS + k, 1), :]
            b = k // G
            loads = (row * turned[b * N : (b + 1) * N]).astype(BF16)
            at = pl.multiple_of(step * WIDE + k * P_SIZE, P_SIZE)
            lane = (k % 2) * P_SIZE
            j = k // 2
            made[j % 2, step * (CHIPS // STEPS) + j // 2, :N, lane : lane + P_SIZE] = nn(
                loads, inputs[:, pl.ds(at, P_SIZE)]
            )
        for j in range(HEADS // 2):
            row = carry[:, j * PAIR : (j + 1) * PAIR]
            made[j % 2, step * (CHIPS // STEPS) + j // 2, N:, :] = jnp.broadcast_to(row, (8, PAIR))
        part = pl.ds(step * (CHIPS // STEPS), CHIPS // STEPS)
        push("pair", made.at[1 - core, part], theirs.at[part], sibling)
        return nothing

    lax.fori_loop(0, STEPS, summarize, 0)

    arrive("home_z", stored.at[0])
    for to in x_groups:
        push("home_x", stored.at[partner], stored.at[partner], me, to)

    def inside(c):
        end = c * TOK + TOK - 1
        first = (end >= one) & (end < two) & (one >= c * TOK)
        second = (end >= two) & (two >= c * TOK)
        return first, second

    arrive("pair", theirs)
    first_one, first_two = inside(2 * chip)
    last_one, last_two = inside(2 * chip + 1)
    fresh = last_one | last_two

    def both(m):
        own = made[core, m]
        other = theirs[m]
        even = jnp.where(core == 0, own, other)
        odd = jnp.where(core == 0, other, own)
        return even, odd

    def combine(i, nothing):
        m = (chip + i) % CHIPS
        even, odd = both(m)
        factor = odd[N : N + 1]
        total = odd[:N] + jnp.where(fresh, 0.0, factor) * even[:N]
        carry = factor * jnp.where(fresh, 1.0, even[N : N + 1])
        packed[m, :N, :] = total.astype(BF16)
        high = carry.astype(BF16).astype(F32)
        tile = iota((16, PAIR), 0)
        rows = jnp.where(tile == 0, high, jnp.where(tile == 1, carry - high, 0.0))
        packed[m, N:, :] = rows.astype(BF16)

        @pl.when(i != 0)
        def _():
            push("summary", packed.at[m], recv.at[chip], 2 * m + core)

        return nothing

    lax.fori_loop(0, CHIPS, combine, 0)
    own_summary = copy_in(packed.at[chip], recv.at[chip], 0)

    def within(step, nothing):
        spread_rates = nn(turned_rates, spread_matrix(step)).astype(BF16)
        run_wide = nn(mask, spread_rates)
        two_groups = pl.ds(pl.multiple_of(step * 2 * N, 2 * N), 2 * N)
        writes, reads = write[:, two_groups], read[:, two_groups]
        for b in range(HEADS // G):
            crossed = nt(reads[:, b * N : (b + 1) * N], writes[:, b * N : (b + 1) * N])
            for k in range(b * G, (b + 1) * G):
                at = pl.ds(step * HEADS + k, 1)
                lanes = pl.ds(pl.multiple_of(step * WIDE + k * P_SIZE, P_SIZE), P_SIZE)
                decay = run_wide[:, k * P_SIZE : (k + 1) * P_SIZE] - run_rows[at, :] + bias
                mixing = (crossed * jnp.exp(decay) * step_rows[at, :]).astype(BF16)
                x_h = inputs[:, lanes]
                inner[:, lanes] = nn(mixing, x_h) + gain[step * HEADS + k] * x_h.astype(F32)
        return nothing

    def hand_on(step):
        lanes = pl.ds(step * WIDE, WIDE)
        return copy_in(inner.at[:, lanes], partial.at[:, lanes], 6 + step)

    arrive("cache_1", caches.at[0])
    push("cache_2", caches.at[z_after[0]], caches.at[z_after[0]], z_before)
    spread("cache", caches, z_after[0])
    push("cache_core", caches.at[z_after[0]], caches.at[z_after[0]], sibling)
    arrive("band_2", slot(2))
    push("band_4", slot(2), slot(4), onward)

    lax.fori_loop(0, 2, within, 0)
    handed = [hand_on(0), hand_on(1)]

    mine[4].wait()
    arrive("home_x", stored.at[pl.ds(0, 6)])
    back = []
    for s in range(SEQS):
        at = home[group * SEQS + s]
        back.append(stored[at // SEQS, at % SEQS].astype(F32))
    extra[0] = back[1].astype(BF16)
    extra[1] = back[2].astype(BF16)
    push("extra_1", extra, plane.at[chip], z_before)
    for to in y_peers:
        push("extra_y", extra, plane.at[chip], to)
    own_extra = copy_in(extra, plane.at[chip], 1)

    lax.fori_loop(2, STEPS, within, 0)
    handed += [hand_on(2), hand_on(3)]

    arrive("cache_2", caches.at[0])
    push("cache_3", caches.at[z_after[1]], caches.at[z_after[1]], z_before)
    spread("cache", caches, z_after[1])
    push("cache_core", caches.at[z_after[1]], caches.at[z_after[1]], sibling)

    arrive("extra_1", plane.at[0])
    push("extra_2", plane.at[z_after[0] // 2], plane.at[z_after[0] // 2], z_before)
    spread("extra", plane, z_after[0] // 2)
    arrive("extra_2", plane.at[0])
    push("extra_3", plane.at[z_after[1] // 2], plane.at[z_after[1] // 2], z_before)
    spread("extra", plane, z_after[1] // 2)
    arrive("summary", recv.at[pl.ds(0, CHIPS - 1)])
    own_summary.wait()

    def turn(m, held):
        entering[m] = held.astype(BF16)

        @pl.when(m != chip)
        def _():
            push("state", entering.at[m], arrived.at[chip], 2 * m + core)

        even_one, even_two = inside(2 * m)
        odd_one, odd_two = inside(2 * m + 1)
        base = jnp.where(even_two, back[2], jnp.where(even_one, back[1], held))
        base = jnp.where(odd_two, back[2], jnp.where(odd_one, back[1], base))
        carry = recv[m, N : N + 16, :].astype(F32)
        return (carry[0:1] + carry[1:2]) * base + recv[m, :N, :].astype(F32)

    lax.fori_loop(0, CHIPS, turn, back[0])
    own_entering = copy_in(entering.at[chip], arrived.at[chip], 2)


    arrive("extra_3", plane.at[0])
    spread("extra", plane, z_after[2] // 2)
    arrive("cache_3", caches.at[0])
    spread("cache", caches, z_after[2])
    push("cache_core", caches.at[z_after[2]], caches.at[z_after[2]], sibling)
    arrive("band_4", slot(4))
    push("band_core", slot(2 * core), slot(1), sibling)
    push("band_core", slot(2 * core + 2), slot(3), sibling)
    own_extra.wait()
    arrive("extra_y", plane.at[pl.ds(0, 12)])
    push("extra_core", plane, extras.at[core], sibling)
    keep_extra = copy_in(plane, extras.at[core], 0)
    arrive("state", arrived.at[pl.ds(0, CHIPS - 1)])
    own_entering.wait()

    def settle(m, nothing):
        even, _ = both(m)
        first = arrived[m].astype(F32)
        base = jnp.where(
            first_two,
            plane[m, 1].astype(F32),
            jnp.where(first_one, plane[m, 0].astype(F32), first),
        )
        second = even[N : N + 1] * base + even[:N]
        own_state[m] = jnp.where(core == 0, first, second).astype(BF16)
        other_state[m] = jnp.where(core == 0, second, first).astype(BF16)
        return nothing

    lax.fori_loop(0, CHIPS, settle, 0)
    push("state_core", other_state, state.at[core], sibling)
    keep_state = copy_in(own_state, state.at[core], 1)
    arrive("cache_y", caches.at[pl.ds(0, 12)])
    for i in range(4):
        for j in range(1, 4):
            at = ((y + j) % 4) * 8 + ((z + i) % 4) * 2 + core
            push("cache_core", caches.at[at], caches.at[at], sibling)

    arrive("extra_core", extras.at[0])
    arrive("cache_core", caches.at[pl.ds(0, CHIPS)])
    arrive("band_core", band.at[pl.ds(0, 16)])
    arrive("state_core", state.at[0])
    for copy in handed + [keep_extra, keep_state]:
        copy.wait()
    for kind, ref in counts.items():
        await_bytes(ref, sent.at[kinds[kind]])


EXCHANGES = (
    "home_z",
    "home_x",
    "pair",
    "summary",
    "state",
    "state_core",
    "band_2",
    "band_4",
    "band_core",
    "cache_1",
    "cache_2",
    "cache_3",
    "cache_y",
    "cache_core",
    "extra_1",
    "extra_2",
    "extra_3",
    "extra_y",
    "extra_core",
)


def output_kernel(lengths, rates, read, partial, state, extra, out):
    step = pl.program_id(0)
    first = lax.axis_index("ctx") * TOK
    one, two = starts_of(lengths)
    one, two = one - first, two - first
    mask = jnp.where(same_causal(one, two), 1.0, 0.0).astype(BF16)
    t = iota((TOK, N), 0)
    new_one = (t >= one) & (t < two) & (one >= 0)
    new_two = (t >= two) & (two >= 0)
    turned = rates[...].astype(F32).T.astype(BF16)
    run = nn(mask, nn(turned, spread_matrix(step)).astype(BF16))
    for b in range(HEADS // G):
        c = read[:, b * N : (b + 1) * N].astype(F32)
        c_in = jnp.where(new_one | new_two, 0.0, c).astype(BF16)
        c_one = jnp.where(new_one, c, 0.0).astype(BF16)
        c_two = jnp.where(new_two, c, 0.0).astype(BF16)
        for j in range(G // 2):
            chunk = b * (G // 2) + j
            from_state = (
                nn(c_in, state[chunk % 2, chunk // 2])
                + nn(c_one, extra[chunk % 2, chunk // 2, 0])
                + nn(c_two, extra[chunk % 2, chunk // 2, 1])
            )
            lanes = slice(chunk * PAIR, (chunk + 1) * PAIR)
            result = partial[:, lanes] + jnp.exp(run[:, lanes]) * from_state
            out[:, lanes] = result.astype(BF16)


def attention_kernel(
    lengths,
    history,
    queries,
    band,
    sink_keys,
    sink_values,
    cache,
    out,
    keys,
    rows,
    scores,
    top,
    total,
    sums,
    bias,
    listed,
    sems,
):
    place = lax.axis_index("ctx")
    first = place * TOK
    one, two = starts_of(lengths)
    edges = [jnp.int32(0), one, two, jnp.int32(CTX * TOK)]
    lives = []
    for s in range(SEQS):
        begin = jnp.maximum(edges[s], first)
        present = begin < jnp.minimum(edges[s + 1], first + TOK)
        lives.append(
            [
                present
                & (begin - edges[s] < j * TOK + TOK - 1)
                & (history[0, s] - WINDOW + j * TOK + TOK - 1 >= SINKS)
                for j in range(4)
            ]
        )
    copies = [
        pltpu.make_async_copy(band, keys.at[pl.ds(0, 8 * SINK_BLOCK)], sems.at[0]),
    ]
    for copy in copies:
        copy.start()

    def history_copies(s):
        return [
            pltpu.make_async_copy(
                cache.at[:, kv, s],
                keys.at[pl.ds(8 * CACHE_BLOCK + 32 * s, 32), :, pl.ds(kv * KVH * HD, KVH * HD)],
                sems.at[2 + 2 * s + kv],
            )
            for kv in range(2)
        ]

    wanted = [lives[s][0] | lives[s][1] | lives[s][2] | lives[s][3] for s in range(SEQS)]
    for s in range(SEQS):

        @pl.when(wanted[s])
        def _():
            for copy in history_copies(s):
                copy.start()

    keys[8 * NULL_BLOCK :] = jnp.zeros((8, 16, 2 * KVH * HD), BF16)
    half = KVH * HD
    keys[8 * SINK_BLOCK + 1 : 8 * CACHE_BLOCK] = jnp.zeros((7, 16, 2 * half), BF16)
    for kv, sinks in enumerate((sink_keys, sink_values)):
        parts = [sinks[s].astype(F32) for s in range(SEQS)] + [jnp.zeros((4, half), F32)]
        both = jnp.concatenate(parts, axis=0).astype(BF16)
        keys[8 * SINK_BLOCK, :, kv * half : (kv + 1) * half] = both

    t = first + iota((TOK, TOK), 0)
    u = iota((TOK, TOK), 1)
    owner = segment(t, one, two)
    offset = t - jnp.where(owner == 2, two, jnp.where(owner == 1, one, 0))
    count = jnp.int32(0)
    head_owner = (first >= one).astype(I32) + (first >= two).astype(I32)
    for b in range(REACH + 1):
        pos = first + (b - REACH) * TOK + u
        gap = t - pos
        ok = (pos >= 0) & (segment(pos, one, two) == owner) & (gap >= 0) & (gap < WINDOW)
        bias[b] = jnp.where(ok, 0.0, -jnp.inf)
        end = first + (b - REACH) * TOK + TOK - 1
        end_owner = (end >= one).astype(I32) + (end >= two).astype(I32)
        live = (end >= 0) & (end_owner >= head_owner)
        listed[count] = b
        count = count + live.astype(I32)
    bias[SINK_BLOCK] = jnp.where(
        (u < SEQS * SINKS) & (u // SINKS == owner), 0.0, -jnp.inf
    )
    listed[count] = SINK_BLOCK
    count = count + 1
    for s in range(SEQS):
        for j in range(4):
            live = lives[s][j]
            block = CACHE_BLOCK + 4 * s + j

            @pl.when(live)
            def _():
                slot = j * TOK + u
                ok = (owner == s) & (slot > offset) & (history[0, s] - WINDOW + slot >= SINKS)
                bias[block] = jnp.where(ok, 0.0, -jnp.inf)

            listed[count] = block
            count = count + live.astype(I32)
    bias[NULL_BLOCK] = jnp.full((TOK, TOK), -jnp.inf, F32)
    listed[count] = NULL_BLOCK
    pairs = lax.div(count + 1, jnp.int32(2))
    for copy in copies:
        copy.wait()
    for s in range(SEQS):

        @pl.when(wanted[s])
        def _():
            for copy in history_copies(s):
                copy.wait()

    per = QH // KVH
    scale = 1.0 / math.sqrt(HD) / math.log(2.0)

    def one_head(number, nothing):
        lanes = pl.ds(pl.multiple_of(number * HD, HD), HD)
        value_lanes = pl.ds(pl.multiple_of(number * HD + KVH * HD, HD), HD)
        for r in range(per):
            wide = pl.ds(pl.multiple_of((number * per + r) * HD, HD), HD)
            rows[r * TOK : (r + 1) * TOK, :] = queries[:, wide]
        top[...] = jnp.full(top.shape, -jnp.inf, F32)
        total[...] = jnp.zeros(total.shape, F32)
        sums[...] = jnp.zeros(sums.shape, F32)

        def score(i, nothing):
            blocks = [listed[2 * i + part] for part in range(2)]
            key = [keys[pl.ds(b * 8, 8), :, lanes].reshape(TOK, HD) for b in blocks]
            key = jnp.concatenate(key, axis=0)
            left_bias, right_bias = bias[blocks[0]], bias[blocks[1]]
            for r in range(per):
                at = slice(r * TOK, (r + 1) * TOK)
                made = nt(rows[at, :], key) * scale
                left = made[:, :TOK] + left_bias
                right = made[:, TOK:] + right_bias
                scores[2 * i, at, :] = left
                scores[2 * i + 1, at, :] = right
                top[at, :] = jnp.maximum(top[at, :], jnp.maximum(left, right))
            return nothing

        lax.fori_loop(0, pairs, score, 0)
        top[...] = jnp.broadcast_to(jnp.max(top[...], axis=1, keepdims=True), top.shape)

        def weigh(i, nothing):
            values = []
            for part in range(2):
                block = listed[2 * i + part]
                values.append(keys[pl.ds(block * 8, 8), :, value_lanes].reshape(TOK, HD))
            value = jnp.concatenate(values, axis=0)
            for r in range(per):
                at = slice(r * TOK, (r + 1) * TOK)
                left = jnp.exp2(scores[2 * i, at, :] - top[at, :])
                right = jnp.exp2(scores[2 * i + 1, at, :] - top[at, :])
                total[at, :] += left + right
                both = jnp.concatenate([left.astype(BF16), right.astype(BF16)], axis=1)
                sums[at, :] += nn(both, value)
            return nothing

        lax.fori_loop(0, pairs, weigh, 0)
        for r in range(per):
            at = slice(r * TOK, (r + 1) * TOK)
            whole = jnp.sum(total[at, :], axis=1, keepdims=True)
            wide = pl.ds(pl.multiple_of((number * per + r) * HD, HD), HD)
            out[:, wide] = (sums[at, :] / whole).astype(BF16)
        return nothing

    lax.fori_loop(0, KVH, one_head, 0)


SMEM = pl.BlockSpec(memory_space=pltpu.SMEM)
VMEM = pl.BlockSpec(memory_space=pltpu.VMEM)
ANY = pl.BlockSpec(memory_space=pl.ANY)
LIMIT = pltpu.CompilerParams(vmem_limit_bytes=60 * 2**20)


def full(shape):
    return pl.BlockSpec(shape, lambda i: (0,) * len(shape))


def lane_block(rows, width):
    return pl.BlockSpec((rows, width), lambda i: (0, i))


def exchange(
    groups,
    home,
    lengths,
    gain,
    saved,
    x,
    steps,
    rates,
    write,
    read,
    cache_keys,
    cache_values,
    turn_keys,
    turn_values,
):
    return pl.pallas_call(
        exchange_kernel,
        out_shape=(
            jax.ShapeDtypeStruct((2, CHIPS, N, PAIR), BF16),
            jax.ShapeDtypeStruct((2, CHIPS, 2, N, PAIR), BF16),
            jax.ShapeDtypeStruct((CTX, 2) + cache_keys.shape, BF16),
            jax.ShapeDtypeStruct((8 * (REACH + 1), 16, 2 * KVH * HD), BF16),
            jax.ShapeDtypeStruct((TOK, H * P_SIZE), F32),
        ),
        in_specs=[SMEM, SMEM, SMEM, ANY, ANY, VMEM, VMEM, VMEM, VMEM, ANY, ANY, ANY, ANY],
        out_specs=(ANY, ANY, ANY, ANY, ANY),
        scratch_shapes=[
            pltpu.VMEM((TOK, H * P_SIZE), BF16),
            pltpu.VMEM((H, TOK), F32),
            pltpu.VMEM((H, TOK), F32),
            pltpu.VMEM((H, TOK), F32),
            pltpu.VMEM((TOK, H * P_SIZE), F32),
            pltpu.VMEM((2, CHIPS, N + 8, PAIR), F32),
            pltpu.VMEM((CHIPS, N + 8, PAIR), F32),
            pltpu.VMEM((CHIPS, ROWS, PAIR), BF16),
            pltpu.VMEM((CHIPS, ROWS, PAIR), BF16),
            pltpu.VMEM((groups, SEQS, N, PAIR), BF16),
            pltpu.VMEM((CHIPS, N, PAIR), BF16),
            pltpu.VMEM((CHIPS, N, PAIR), BF16),
            pltpu.VMEM((CHIPS, N, PAIR), BF16),
            pltpu.VMEM((CHIPS, N, PAIR), BF16),
            pltpu.VMEM((2, N, PAIR), BF16),
            pltpu.VMEM((CHIPS, 2, N, PAIR), BF16),
            pltpu.SemaphoreType.DMA((len(EXCHANGES),)),
            pltpu.SemaphoreType.DMA((len(EXCHANGES),)),
            pltpu.SemaphoreType.DMA((10,)),
        ],
        compiler_params=pltpu.CompilerParams(
            collective_id=0, has_side_effects=True, vmem_limit_bytes=60 * 2**20
        ),
    )(
        home,
        lengths,
        gain,
        saved,
        x,
        steps,
        rates,
        write,
        read,
        cache_keys,
        cache_values,
        turn_keys,
        turn_values,
    )


def outputs(lengths, rates, read, partial, state, extra):
    return pl.pallas_call(
        output_kernel,
        grid=(STEPS,),
        out_shape=jax.ShapeDtypeStruct((TOK, H * P_SIZE), BF16),
        in_specs=[
            SMEM,
            full((H, TOK)),
            lane_block(TOK, 2 * N),
            lane_block(TOK, WIDE),
            pl.BlockSpec((2, CHIPS // STEPS, N, PAIR), lambda i: (0, i, 0, 0)),
            pl.BlockSpec((2, CHIPS // STEPS, 2, N, PAIR), lambda i: (0, i, 0, 0, 0)),
        ],
        out_specs=lane_block(TOK, WIDE),
        compiler_params=LIMIT,
    )(lengths, rates, read, partial, state, extra)


def attention(lengths, history, queries, band, sink_keys, sink_values, cache):
    rows = (QH // KVH) * TOK
    return pl.pallas_call(
        attention_kernel,
        out_shape=jax.ShapeDtypeStruct((TOK, QH * HD), BF16),
        in_specs=[SMEM, SMEM, VMEM, ANY, VMEM, VMEM, ANY],
        out_specs=VMEM,
        scratch_shapes=[
            pltpu.VMEM((8 * BLOCKS, 16, 2 * KVH * HD), BF16),
            pltpu.VMEM((rows, HD), BF16),
            pltpu.VMEM((BLOCKS + 1, rows, TOK), F32),
            pltpu.VMEM((rows, TOK), F32),
            pltpu.VMEM((rows, TOK), F32),
            pltpu.VMEM((rows, HD), F32),
            pltpu.VMEM((BLOCKS, TOK, TOK), F32),
            pltpu.SMEM((BLOCKS + 1,), I32),
            pltpu.SemaphoreType.DMA((8,)),
        ],
        compiler_params=LIMIT,
        cost_estimate=pl.CostEstimate(
            flops=2_500_000_000, bytes_accessed=8_000_000, transcendentals=5_000_000
        ),
    )(lengths, history, queries, band, sink_keys, sink_values, cache)


def shards(
    mamba_input,
    step_size,
    decay_log,
    state_write,
    state_read,
    skip_gain,
    saved_states,
    home_slot,
    turn_lengths,
    history_lengths,
    queries,
    turn_keys,
    turn_values,
    cache_keys,
    cache_values,
    sink_keys,
    sink_values,
):
    x, steps, rates = mamba_input[0], step_size[0].T, decay_log[0].T
    write, read = state_write[0], state_read[0]
    saved = saved_states[0].astype(BF16).reshape(SEQS, 2, P_SIZE, N)
    saved = saved.transpose(0, 3, 1, 2).reshape(SEQS, N, PAIR)

    groups = lax.axis_size("sess")
    state, extras, caches, band, partial = exchange(
        groups,
        home_slot,
        turn_lengths,
        skip_gain,
        saved,
        x,
        steps,
        rates,
        write,
        read,
        cache_keys[0],
        cache_values[0],
        turn_keys[0].reshape(8, 16, KVH * HD),
        turn_values[0].reshape(8, 16, KVH * HD),
    )
    attended = attention(
        turn_lengths, history_lengths, queries[0], band, sink_keys[0], sink_values[0], caches
    )
    mixed = outputs(turn_lengths, rates, read, partial, state, extras)
    return (mixed[None], attended[None])


def solution(mesh):
    token = P("sess", "ctx", None)
    spread = P("sess", None, "ctx", None)
    return jax.shard_map(
        shards,
        mesh=mesh,
        in_specs=(
            token,
            token,
            token,
            token,
            token,
            P(),
            spread,
            P(),
            P("sess", None),
            P("sess", None),
            token,
            token,
            token,
            spread,
            spread,
            P("sess", None, None, None),
            P("sess", None, None, None),
        ),
        out_specs=(token, token),
        check_vma=False,
    )
```

```python
import functools
import math

import jax
import jax.numpy as jnp
from jax import lax
from jax.experimental import pallas as pl
from jax.experimental.pallas import tpu as pltpu
from jax.sharding import PartitionSpec as P

TOK = 128
HALF = TOK // 2
REACH = 4
SEQS = 3
SINKS = 4
H = 64
P_SIZE = 128
N = 64
G = 8
QH = 32
KVH = 4
HD = 128
WINDOW = 512
CTX = 32
CHIPS = CTX // 2
MESH = pl.DeviceIdType.MESH

F32 = jnp.float32
BF16 = jnp.bfloat16
I32 = jnp.int32
PAIR = 2 * P_SIZE
ROWS = N + 16
STEPS = 4
HEADS = H // STEPS
WIDE = HEADS * P_SIZE
BLOCKS = REACH + 1 + 1 + SEQS * 4 + 1
SINK_BLOCK = REACH + 1
CACHE_BLOCK = SINK_BLOCK + 1
NULL_BLOCK = BLOCKS - 1


def iota(shape, axis):
    return lax.broadcasted_iota(I32, shape, axis)


def nn(a, b):
    return lax.dot_general(a, b, (((1,), (0,)), ((), ())), preferred_element_type=F32)


def nt(a, b):
    return lax.dot_general(a, b, (((1,), (1,)), ((), ())), preferred_element_type=F32)


def starts_of(lengths):
    first = lengths[0, 0]
    return first, first + lengths[0, 1]


def segment(positions, one, two):
    return (positions >= one).astype(I32) + (positions >= two).astype(I32)


def same_causal(one, two):
    t, u = iota((TOK, TOK), 0), iota((TOK, TOK), 1)
    return (segment(t, one, two) == segment(u, one, two)) & (t >= u)


def spread_matrix(step):
    rows = iota((H, WIDE), 0)
    lanes = iota((H, WIDE), 1)
    return jnp.where(rows == step * HEADS + lanes // P_SIZE, 1.0, 0.0).astype(BF16)


def await_bytes(ref, sem):
    pltpu.make_async_copy(ref, ref, sem).wait()


def exchange_kernel(
    home,
    lengths,
    gain,
    saved,
    x,
    steps,
    rates,
    write,
    read,
    cache_keys,
    cache_values,
    turn_keys,
    turn_values,
    state,
    extras,
    caches,
    band,
    partial,
    inputs,
    weight,
    run_rows,
    step_rows,
    inner,
    made,
    theirs,
    packed,
    recv,
    stored,
    entering,
    arrived,
    own_state,
    other_state,
    extra,
    plane,
    sent,
    got,
    local,
):
    group, me = lax.axis_index("sess"), lax.axis_index("ctx")
    across, deep = group // 2, group % 2
    y, z, core = me // 8, (me // 2) % 4, me % 2
    chip = me // 2
    sibling = me + 1 - 2 * core
    partner = group + 1 - 2 * deep
    x_groups = [((across + i) % 4) * 2 + deep for i in range(1, 4)]
    y_peers = [((y + i) % 4) * 8 + z * 2 + core for i in range(1, 4)]
    z_before = y * 8 + ((z + 3) % 4) * 2 + core
    z_after = [y * 8 + ((z + i) % 4) * 2 + core for i in range(1, 4)]
    onward = (me + 2) % CTX
    kinds = {name: i for i, name in enumerate(EXCHANGES)}

    def copy_in(src, dst, at):
        copy = pltpu.make_async_copy(src, dst, local.at[at])
        copy.start()
        return copy

    half = KVH * HD
    mine = [
        copy_in(cache_keys, caches.at[me, 0], 0),
        copy_in(cache_values, caches.at[me, 1], 1),
        copy_in(turn_keys, band.at[pl.ds(8 * REACH, 8), :, pl.ds(0, half)], 2),
        copy_in(turn_values, band.at[pl.ds(8 * REACH, 8), :, pl.ds(half, half)], 3),
        copy_in(saved, stored.at[group], 4),
        copy_in(x, inputs, 5),
    ]

    barrier = pltpu.get_barrier_semaphore()

    def greet(i, nothing):
        peer = ((chip + i) % CHIPS) * 2 + core
        pl.semaphore_signal(barrier, inc=1, device_id=(group, peer), device_id_type=MESH)
        return nothing

    lax.fori_loop(1, CHIPS, greet, 0)
    pl.semaphore_signal(barrier, inc=1, device_id=(group, sibling), device_id_type=MESH)
    for to in [partner] + x_groups:
        pl.semaphore_signal(barrier, inc=1, device_id=(to, me), device_id_type=MESH)
    pl.semaphore_wait(barrier, CHIPS - 1 + 1 + 4)

    def push(kind, src, dst, peer, to=None):
        at = kinds[kind]
        pltpu.make_async_remote_copy(
            src_ref=src,
            dst_ref=dst,
            send_sem=sent.at[at],
            recv_sem=got.at[at],
            device_id=(group if to is None else to, peer),
            device_id_type=MESH,
        ).start()

    counts = {}

    def arrive(kind, ref):
        counts[kind] = ref
        await_bytes(ref, got.at[kinds[kind]])

    def slot(distance):
        return band.at[pl.ds(8 * (REACH - distance), 8)]

    def spread(name, array, at):
        for to in y_peers:
            push(name + "_y", array.at[at], array.at[at], to)

    push("home_z", saved, stored.at[group], me, partner)
    for to in x_groups:
        push("home_x", saved, stored.at[group], me, to)
    mine[2].wait()
    mine[3].wait()
    push("band_2", slot(0), slot(2), onward)
    mine[0].wait()
    mine[1].wait()
    push("cache_1", caches.at[me], caches.at[me], z_before)
    spread("cache", caches, me)
    push("cache_core", caches.at[me], caches.at[me], sibling)

    one, two = starts_of(lengths)
    here_one, here_two = one - me * TOK, two - me * TOK
    seen = same_causal(here_one, here_two)
    mask = jnp.where(seen, 1.0, 0.0).astype(BF16)
    bias = jnp.where(seen, 0.0, -jnp.inf)
    run = nt(rates[...], mask)
    run_rows[...] = run
    step_rows[...] = steps[...].astype(F32)
    u = iota((1, TOK), 1)
    last = (TOK - 1 >= here_one).astype(I32) + (TOK - 1 >= here_two).astype(I32)
    held = segment(u, here_one, here_two) == last
    gap = jnp.where(held, run[:, TOK - 1 :] - run, -jnp.inf)
    weight[...] = jnp.exp(gap) * steps[...].astype(F32)
    turned_rates = rates[...].astype(F32).T.astype(BF16)
    mine[5].wait()

    def summarize(step, nothing):
        turned = write[:, pl.ds(pl.multiple_of(step * 2 * N, 2 * N), 2 * N)].astype(F32).T
        spread_rates = nn(turned_rates, spread_matrix(step)).astype(BF16)
        carry = jnp.exp(nn(mask[TOK - 16 :], spread_rates)[15:16])
        for k in range(HEADS):
            row = weight[pl.ds(step * HEADS + k, 1), :]
            b = k // G
            loads = (row * turned[b * N : (b + 1) * N]).astype(BF16)
            at = pl.multiple_of(step * WIDE + k * P_SIZE, P_SIZE)
            lane = (k % 2) * P_SIZE
            j = k // 2
            made[j % 2, step * (CHIPS // STEPS) + j // 2, :N, lane : lane + P_SIZE] = nn(
                loads, inputs[:, pl.ds(at, P_SIZE)]
            )
        for j in range(HEADS // 2):
            row = carry[:, j * PAIR : (j + 1) * PAIR]
            made[j % 2, step * (CHIPS // STEPS) + j // 2, N:, :] = jnp.broadcast_to(row, (8, PAIR))
        part = pl.ds(step * (CHIPS // STEPS), CHIPS // STEPS)
        push("pair", made.at[1 - core, part], theirs.at[part], sibling)
        return nothing

    lax.fori_loop(0, STEPS, summarize, 0)

    arrive("home_z", stored.at[0])
    for to in x_groups:
        push("home_x", stored.at[partner], stored.at[partner], me, to)

    def inside(c):
        end = c * TOK + TOK - 1
        first = (end >= one) & (end < two) & (one >= c * TOK)
        second = (end >= two) & (two >= c * TOK)
        return first, second

    arrive("pair", theirs)
    first_one, first_two = inside(2 * chip)
    last_one, last_two = inside(2 * chip + 1)
    fresh = last_one | last_two

    def both(m):
        own = made[core, m]
        other = theirs[m]
        even = jnp.where(core == 0, own, other)
        odd = jnp.where(core == 0, other, own)
        return even, odd

    def combine(i, nothing):
        m = (chip + i) % CHIPS
        even, odd = both(m)
        factor = odd[N : N + 1]
        total = odd[:N] + jnp.where(fresh, 0.0, factor) * even[:N]
        carry = factor * jnp.where(fresh, 1.0, even[N : N + 1])
        packed[m, :N, :] = total.astype(BF16)
        high = carry.astype(BF16).astype(F32)
        tile = iota((16, PAIR), 0)
        rows = jnp.where(tile == 0, high, jnp.where(tile == 1, carry - high, 0.0))
        packed[m, N:, :] = rows.astype(BF16)

        @pl.when(i != 0)
        def _():
            push("summary", packed.at[m], recv.at[chip], 2 * m + core)

        return nothing

    lax.fori_loop(0, CHIPS, combine, 0)
    own_summary = copy_in(packed.at[chip], recv.at[chip], 0)

    def within(step, nothing):
        spread_rates = nn(turned_rates, spread_matrix(step)).astype(BF16)
        run_wide = nn(mask, spread_rates)
        two_groups = pl.ds(pl.multiple_of(step * 2 * N, 2 * N), 2 * N)
        writes, reads = write[:, two_groups], read[:, two_groups]
        for b in range(HEADS // G):
            crossed = nt(reads[:, b * N : (b + 1) * N], writes[:, b * N : (b + 1) * N])
            for k in range(b * G, (b + 1) * G):
                at = pl.ds(step * HEADS + k, 1)
                lanes = pl.ds(pl.multiple_of(step * WIDE + k * P_SIZE, P_SIZE), P_SIZE)
                decay = run_wide[:, k * P_SIZE : (k + 1) * P_SIZE] - run_rows[at, :] + bias
                mixing = (crossed * jnp.exp(decay) * step_rows[at, :]).astype(BF16)
                x_h = inputs[:, lanes]
                inner[:, lanes] = nn(mixing, x_h) + gain[step * HEADS + k] * x_h.astype(F32)
        return nothing

    def hand_on(step):
        lanes = pl.ds(step * WIDE, WIDE)
        return copy_in(inner.at[:, lanes], partial.at[:, lanes], 6 + step)

    arrive("cache_1", caches.at[0])
    push("cache_2", caches.at[z_after[0]], caches.at[z_after[0]], z_before)
    spread("cache", caches, z_after[0])
    push("cache_core", caches.at[z_after[0]], caches.at[z_after[0]], sibling)
    arrive("band_2", slot(2))
    push("band_4", slot(2), slot(4), onward)

    lax.fori_loop(0, 2, within, 0)
    handed = [hand_on(0), hand_on(1)]

    mine[4].wait()
    arrive("home_x", stored.at[pl.ds(0, 6)])
    back = []
    for s in range(SEQS):
        at = home[group * SEQS + s]
        back.append(stored[at // SEQS, at % SEQS].astype(F32))
    extra[0] = back[1].astype(BF16)
    extra[1] = back[2].astype(BF16)
    push("extra_1", extra, plane.at[chip], z_before)
    for to in y_peers:
        push("extra_y", extra, plane.at[chip], to)
    own_extra = copy_in(extra, plane.at[chip], 1)

    lax.fori_loop(2, STEPS, within, 0)
    handed += [hand_on(2), hand_on(3)]

    arrive("cache_2", caches.at[0])
    push("cache_3", caches.at[z_after[1]], caches.at[z_after[1]], z_before)
    spread("cache", caches, z_after[1])
    push("cache_core", caches.at[z_after[1]], caches.at[z_after[1]], sibling)

    arrive("extra_1", plane.at[0])
    push("extra_2", plane.at[z_after[0] // 2], plane.at[z_after[0] // 2], z_before)
    spread("extra", plane, z_after[0] // 2)
    arrive("extra_2", plane.at[0])
    push("extra_3", plane.at[z_after[1] // 2], plane.at[z_after[1] // 2], z_before)
    spread("extra", plane, z_after[1] // 2)
    arrive("summary", recv.at[pl.ds(0, CHIPS - 1)])
    own_summary.wait()

    def turn(m, held):
        entering[m] = held.astype(BF16)

        @pl.when(m != chip)
        def _():
            push("state", entering.at[m], arrived.at[chip], 2 * m + core)

        even_one, even_two = inside(2 * m)
        odd_one, odd_two = inside(2 * m + 1)
        base = jnp.where(even_two, back[2], jnp.where(even_one, back[1], held))
        base = jnp.where(odd_two, back[2], jnp.where(odd_one, back[1], base))
        carry = recv[m, N : N + 16, :].astype(F32)
        return (carry[0:1] + carry[1:2]) * base + recv[m, :N, :].astype(F32)

    lax.fori_loop(0, CHIPS, turn, back[0])
    own_entering = copy_in(entering.at[chip], arrived.at[chip], 2)


    arrive("extra_3", plane.at[0])
    spread("extra", plane, z_after[2] // 2)
    arrive("cache_3", caches.at[0])
    spread("cache", caches, z_after[2])
    push("cache_core", caches.at[z_after[2]], caches.at[z_after[2]], sibling)
    arrive("band_4", slot(4))
    push("band_core", slot(2 * core), slot(1), sibling)
    push("band_core", slot(2 * core + 2), slot(3), sibling)
    own_extra.wait()
    arrive("extra_y", plane.at[pl.ds(0, 12)])
    push("extra_core", plane, extras.at[core], sibling)
    keep_extra = copy_in(plane, extras.at[core], 0)
    arrive("state", arrived.at[pl.ds(0, CHIPS - 1)])
    own_entering.wait()

    def settle(m, nothing):
        even, _ = both(m)
        first = arrived[m].astype(F32)
        base = jnp.where(
            first_two,
            plane[m, 1].astype(F32),
            jnp.where(first_one, plane[m, 0].astype(F32), first),
        )
        second = even[N : N + 1] * base + even[:N]
        own_state[m] = jnp.where(core == 0, first, second).astype(BF16)
        other_state[m] = jnp.where(core == 0, second, first).astype(BF16)
        return nothing

    lax.fori_loop(0, CHIPS, settle, 0)
    push("state_core", other_state, state.at[core], sibling)
    keep_state = copy_in(own_state, state.at[core], 1)
    arrive("cache_y", caches.at[pl.ds(0, 12)])
    for i in range(4):
        for j in range(1, 4):
            at = ((y + j) % 4) * 8 + ((z + i) % 4) * 2 + core
            push("cache_core", caches.at[at], caches.at[at], sibling)

    arrive("extra_core", extras.at[0])
    arrive("cache_core", caches.at[pl.ds(0, CHIPS)])
    arrive("band_core", band.at[pl.ds(0, 16)])
    arrive("state_core", state.at[0])
    for copy in handed + [keep_extra, keep_state]:
        copy.wait()
    for kind, ref in counts.items():
        await_bytes(ref, sent.at[kinds[kind]])


EXCHANGES = (
    "home_z",
    "home_x",
    "pair",
    "summary",
    "state",
    "state_core",
    "band_2",
    "band_4",
    "band_core",
    "cache_1",
    "cache_2",
    "cache_3",
    "cache_y",
    "cache_core",
    "extra_1",
    "extra_2",
    "extra_3",
    "extra_y",
    "extra_core",
)


def output_kernel(lengths, rates, read, partial, state, extra, out):
    step = pl.program_id(0)
    first = lax.axis_index("ctx") * TOK
    one, two = starts_of(lengths)
    one, two = one - first, two - first
    mask = jnp.where(same_causal(one, two), 1.0, 0.0).astype(BF16)
    t = iota((TOK, N), 0)
    new_one = (t >= one) & (t < two) & (one >= 0)
    new_two = (t >= two) & (two >= 0)
    turned = rates[...].astype(F32).T.astype(BF16)
    run = nn(mask, nn(turned, spread_matrix(step)).astype(BF16))
    for b in range(HEADS // G):
        c = read[:, b * N : (b + 1) * N].astype(F32)
        c_in = jnp.where(new_one | new_two, 0.0, c).astype(BF16)
        c_one = jnp.where(new_one, c, 0.0).astype(BF16)
        c_two = jnp.where(new_two, c, 0.0).astype(BF16)
        for j in range(G // 2):
            chunk = b * (G // 2) + j
            from_state = (
                nn(c_in, state[chunk % 2, chunk // 2])
                + nn(c_one, extra[chunk % 2, chunk // 2, 0])
                + nn(c_two, extra[chunk % 2, chunk // 2, 1])
            )
            lanes = slice(chunk * PAIR, (chunk + 1) * PAIR)
            result = partial[:, lanes] + jnp.exp(run[:, lanes]) * from_state
            out[:, lanes] = result.astype(BF16)


def attention_kernel(
    lengths,
    history,
    queries,
    band,
    sink_keys,
    sink_values,
    cache,
    out,
    keys,
    rows,
    scores,
    top,
    total,
    sums,
    bias,
    listed,
    sems,
):
    place = lax.axis_index("ctx")
    first = place * TOK
    one, two = starts_of(lengths)
    edges = [jnp.int32(0), one, two, jnp.int32(CTX * TOK)]
    lives = []
    for s in range(SEQS):
        lives.append([])
        for part in range(2):
            from_token = first + part * HALF
            begin = jnp.maximum(edges[s], from_token)
            present = begin < jnp.minimum(edges[s + 1], from_token + HALF)
            lives[s].append(
                [
                    present
                    & (begin - edges[s] < j * TOK + TOK - 1)
                    & (history[0, s] - WINDOW + j * TOK + TOK - 1 >= SINKS)
                    for j in range(4)
                ]
            )
    copies = [
        pltpu.make_async_copy(band, keys.at[pl.ds(0, 8 * SINK_BLOCK)], sems.at[0]),
    ]
    for copy in copies:
        copy.start()

    def history_copies(s):
        return [
            pltpu.make_async_copy(
                cache.at[:, kv, s],
                keys.at[pl.ds(8 * CACHE_BLOCK + 32 * s, 32), :, pl.ds(kv * KVH * HD, KVH * HD)],
                sems.at[2 + 2 * s + kv],
            )
            for kv in range(2)
        ]

    needed = [[lives[s][0][j] | lives[s][1][j] for j in range(4)] for s in range(SEQS)]
    wanted = [needed[s][0] | needed[s][1] | needed[s][2] | needed[s][3] for s in range(SEQS)]
    for s in range(SEQS):

        @pl.when(wanted[s])
        def _():
            for copy in history_copies(s):
                copy.start()

    keys[8 * NULL_BLOCK :] = jnp.zeros((8, 16, 2 * KVH * HD), BF16)
    half = KVH * HD
    keys[8 * SINK_BLOCK + 1 : 8 * CACHE_BLOCK] = jnp.zeros((7, 16, 2 * half), BF16)
    for kv, sinks in enumerate((sink_keys, sink_values)):
        parts = [sinks[s].astype(F32) for s in range(SEQS)] + [jnp.zeros((4, half), F32)]
        both = jnp.concatenate(parts, axis=0).astype(BF16)
        keys[8 * SINK_BLOCK, :, kv * half : (kv + 1) * half] = both

    t = first + iota((TOK, TOK), 0)
    u = iota((TOK, TOK), 1)
    owner = segment(t, one, two)
    offset = t - jnp.where(owner == 2, two, jnp.where(owner == 1, one, 0))
    for b in range(REACH + 1):
        pos = first + (b - REACH) * TOK + u
        gap = t - pos
        ok = (pos >= 0) & (segment(pos, one, two) == owner) & (gap >= 0) & (gap < WINDOW)
        bias[b] = jnp.where(ok, 0.0, -jnp.inf)
    bias[SINK_BLOCK] = jnp.where((u < SEQS * SINKS) & (u // SINKS == owner), 0.0, -jnp.inf)
    for s in range(SEQS):
        for j in range(4):

            @pl.when(needed[s][j])
            def _():
                slot = j * TOK + u
                ok = (owner == s) & (slot > offset) & (history[0, s] - WINDOW + slot >= SINKS)
                bias[CACHE_BLOCK + 4 * s + j] = jnp.where(ok, 0.0, -jnp.inf)

    bias[NULL_BLOCK] = jnp.full((TOK, TOK), -jnp.inf, F32)
    pairs = []
    for part in range(2):
        count = jnp.int32(0)
        from_token = first + part * HALF
        from_owner = (from_token >= one).astype(I32) + (from_token >= two).astype(I32)
        for b in range(REACH + 1):
            end = first + (b - REACH) * TOK + TOK - 1
            end_owner = (end >= one).astype(I32) + (end >= two).astype(I32)
            live = (end >= 0) & (end_owner >= from_owner)
            listed[part, count] = b
            count = count + live.astype(I32)
        listed[part, count] = SINK_BLOCK
        count = count + 1
        for s in range(SEQS):
            for j in range(4):
                listed[part, count] = CACHE_BLOCK + 4 * s + j
                count = count + lives[s][part][j].astype(I32)
        listed[part, count] = NULL_BLOCK
        pairs.append(lax.div(count + 1, jnp.int32(2)))
    for copy in copies:
        copy.wait()
    for s in range(SEQS):

        @pl.when(wanted[s])
        def _():
            for copy in history_copies(s):
                copy.wait()

    per = QH // KVH
    scale = 1.0 / math.sqrt(HD) / math.log(2.0)

    def one_head(number, nothing):
        lanes = pl.ds(pl.multiple_of(number * HD, HD), HD)
        value_lanes = pl.ds(pl.multiple_of(number * HD + KVH * HD, HD), HD)

        def wide(r):
            return pl.ds(pl.multiple_of((number * per + r) * HD, HD), HD)

        for part in range(2):
            tokens = slice(part * HALF, (part + 1) * HALF)
            for r in range(per):
                rows[r * HALF : (r + 1) * HALF, :] = queries[tokens, wide(r)]
            top[...] = jnp.full(top.shape, -jnp.inf, F32)
            total[...] = jnp.zeros(total.shape, F32)
            sums[...] = jnp.zeros(sums.shape, F32)

            def score(i, nothing, part=part, tokens=tokens):
                blocks = [listed[part, 2 * i + side] for side in range(2)]
                key = [keys[pl.ds(b * 8, 8), :, lanes].reshape(TOK, HD) for b in blocks]
                key = jnp.concatenate(key, axis=0)
                shift = [bias[b, tokens, :] for b in blocks]
                shift = [jnp.concatenate([b, b], axis=0) for b in shift]
                for r in range(per // 2):
                    at = slice(r * TOK, (r + 1) * TOK)
                    made = nt(rows[at, :], key) * scale
                    left = made[:, :TOK] + shift[0]
                    right = made[:, TOK:] + shift[1]
                    scores[2 * i, at, :] = left
                    scores[2 * i + 1, at, :] = right
                    top[at, :] = jnp.maximum(top[at, :], jnp.maximum(left, right))
                return nothing

            lax.fori_loop(0, pairs[part], score, 0)
            top[...] = jnp.broadcast_to(jnp.max(top[...], axis=1, keepdims=True), top.shape)

            def weigh(i, nothing, part=part):
                blocks = [listed[part, 2 * i + side] for side in range(2)]
                value = [keys[pl.ds(b * 8, 8), :, value_lanes].reshape(TOK, HD) for b in blocks]
                value = jnp.concatenate(value, axis=0)
                for r in range(per // 2):
                    at = slice(r * TOK, (r + 1) * TOK)
                    left = jnp.exp2(scores[2 * i, at, :] - top[at, :])
                    right = jnp.exp2(scores[2 * i + 1, at, :] - top[at, :])
                    total[at, :] += left + right
                    both = jnp.concatenate([left.astype(BF16), right.astype(BF16)], axis=1)
                    sums[at, :] += nn(both, value)
                return nothing

            lax.fori_loop(0, pairs[part], weigh, 0)
            for r in range(per):
                at = slice(r * HALF, (r + 1) * HALF)
                whole = jnp.sum(total[at, :], axis=1, keepdims=True)
                out[tokens, wide(r)] = (sums[at, :] / whole).astype(BF16)
        return nothing

    lax.fori_loop(0, KVH, one_head, 0)


SMEM = pl.BlockSpec(memory_space=pltpu.SMEM)
VMEM = pl.BlockSpec(memory_space=pltpu.VMEM)
ANY = pl.BlockSpec(memory_space=pl.ANY)
LIMIT = pltpu.CompilerParams(vmem_limit_bytes=60 * 2**20)


def full(shape):
    return pl.BlockSpec(shape, lambda i: (0,) * len(shape))


def lane_block(rows, width):
    return pl.BlockSpec((rows, width), lambda i: (0, i))


def exchange(
    groups,
    home,
    lengths,
    gain,
    saved,
    x,
    steps,
    rates,
    write,
    read,
    cache_keys,
    cache_values,
    turn_keys,
    turn_values,
):
    return pl.pallas_call(
        exchange_kernel,
        out_shape=(
            jax.ShapeDtypeStruct((2, CHIPS, N, PAIR), BF16),
            jax.ShapeDtypeStruct((2, CHIPS, 2, N, PAIR), BF16),
            jax.ShapeDtypeStruct((CTX, 2) + cache_keys.shape, BF16),
            jax.ShapeDtypeStruct((8 * (REACH + 1), 16, 2 * KVH * HD), BF16),
            jax.ShapeDtypeStruct((TOK, H * P_SIZE), F32),
        ),
        in_specs=[SMEM, SMEM, SMEM, ANY, ANY, VMEM, VMEM, VMEM, VMEM, ANY, ANY, ANY, ANY],
        out_specs=(ANY, ANY, ANY, ANY, ANY),
        scratch_shapes=[
            pltpu.VMEM((TOK, H * P_SIZE), BF16),
            pltpu.VMEM((H, TOK), F32),
            pltpu.VMEM((H, TOK), F32),
            pltpu.VMEM((H, TOK), F32),
            pltpu.VMEM((TOK, H * P_SIZE), F32),
            pltpu.VMEM((2, CHIPS, N + 8, PAIR), F32),
            pltpu.VMEM((CHIPS, N + 8, PAIR), F32),
            pltpu.VMEM((CHIPS, ROWS, PAIR), BF16),
            pltpu.VMEM((CHIPS, ROWS, PAIR), BF16),
            pltpu.VMEM((groups, SEQS, N, PAIR), BF16),
            pltpu.VMEM((CHIPS, N, PAIR), BF16),
            pltpu.VMEM((CHIPS, N, PAIR), BF16),
            pltpu.VMEM((CHIPS, N, PAIR), BF16),
            pltpu.VMEM((CHIPS, N, PAIR), BF16),
            pltpu.VMEM((2, N, PAIR), BF16),
            pltpu.VMEM((CHIPS, 2, N, PAIR), BF16),
            pltpu.SemaphoreType.DMA((len(EXCHANGES),)),
            pltpu.SemaphoreType.DMA((len(EXCHANGES),)),
            pltpu.SemaphoreType.DMA((10,)),
        ],
        compiler_params=pltpu.CompilerParams(
            collective_id=0, has_side_effects=True, vmem_limit_bytes=60 * 2**20
        ),
    )(
        home,
        lengths,
        gain,
        saved,
        x,
        steps,
        rates,
        write,
        read,
        cache_keys,
        cache_values,
        turn_keys,
        turn_values,
    )


def outputs(lengths, rates, read, partial, state, extra):
    return pl.pallas_call(
        output_kernel,
        grid=(STEPS,),
        out_shape=jax.ShapeDtypeStruct((TOK, H * P_SIZE), BF16),
        in_specs=[
            SMEM,
            full((H, TOK)),
            lane_block(TOK, 2 * N),
            lane_block(TOK, WIDE),
            pl.BlockSpec((2, CHIPS // STEPS, N, PAIR), lambda i: (0, i, 0, 0)),
            pl.BlockSpec((2, CHIPS // STEPS, 2, N, PAIR), lambda i: (0, i, 0, 0, 0)),
        ],
        out_specs=lane_block(TOK, WIDE),
        compiler_params=LIMIT,
    )(lengths, rates, read, partial, state, extra)


def attention(lengths, history, queries, band, sink_keys, sink_values, cache):
    rows = (QH // KVH) * HALF
    return pl.pallas_call(
        attention_kernel,
        out_shape=jax.ShapeDtypeStruct((TOK, QH * HD), BF16),
        in_specs=[SMEM, SMEM, VMEM, ANY, VMEM, VMEM, ANY],
        out_specs=VMEM,
        scratch_shapes=[
            pltpu.VMEM((8 * BLOCKS, 16, 2 * KVH * HD), BF16),
            pltpu.VMEM((rows, HD), BF16),
            pltpu.VMEM((BLOCKS + 1, rows, TOK), F32),
            pltpu.VMEM((rows, TOK), F32),
            pltpu.VMEM((rows, TOK), F32),
            pltpu.VMEM((rows, HD), F32),
            pltpu.VMEM((BLOCKS, TOK, TOK), F32),
            pltpu.SMEM((2, BLOCKS + 1), I32),
            pltpu.SemaphoreType.DMA((8,)),
        ],
        compiler_params=LIMIT,
        cost_estimate=pl.CostEstimate(
            flops=2_500_000_000, bytes_accessed=8_000_000, transcendentals=5_000_000
        ),
    )(lengths, history, queries, band, sink_keys, sink_values, cache)


def shards(
    mamba_input,
    step_size,
    decay_log,
    state_write,
    state_read,
    skip_gain,
    saved_states,
    home_slot,
    turn_lengths,
    history_lengths,
    queries,
    turn_keys,
    turn_values,
    cache_keys,
    cache_values,
    sink_keys,
    sink_values,
):
    x, steps, rates = mamba_input[0], step_size[0].T, decay_log[0].T
    write, read = state_write[0], state_read[0]
    saved = saved_states[0].astype(BF16).reshape(SEQS, 2, P_SIZE, N)
    saved = saved.transpose(0, 3, 1, 2).reshape(SEQS, N, PAIR)

    groups = lax.axis_size("sess")
    state, extras, caches, band, partial = exchange(
        groups,
        home_slot,
        turn_lengths,
        skip_gain,
        saved,
        x,
        steps,
        rates,
        write,
        read,
        cache_keys[0],
        cache_values[0],
        turn_keys[0].reshape(8, 16, KVH * HD),
        turn_values[0].reshape(8, 16, KVH * HD),
    )
    attended = attention(
        turn_lengths, history_lengths, queries[0], band, sink_keys[0], sink_values[0], caches
    )
    mixed = outputs(turn_lengths, rates, read, partial, state, extras)
    return (mixed[None], attended[None])


def solution(mesh):
    token = P("sess", "ctx", None)
    spread = P("sess", None, "ctx", None)
    return jax.shard_map(
        shards,
        mesh=mesh,
        in_specs=(
            token,
            token,
            token,
            token,
            token,
            P(),
            spread,
            P(),
            P("sess", None),
            P("sess", None),
            token,
            token,
            token,
            spread,
            spread,
            P("sess", None, None, None),
            P("sess", None, None, None),
        ),
        out_specs=(token, token),
        check_vma=False,
    )
```

```python
import functools
import math

import jax
import jax.numpy as jnp
from jax import lax
from jax.experimental import pallas as pl
from jax.experimental.pallas import tpu as pltpu
from jax.sharding import PartitionSpec as P

TOK = 128
REACH = 4
SEQS = 3
SINKS = 4
H = 64
P_SIZE = 128
N = 64
G = 8
QH = 32
KVH = 4
HD = 128
WINDOW = 512
CTX = 32
CHIPS = CTX // 2
MESH = pl.DeviceIdType.MESH

F32 = jnp.float32
BF16 = jnp.bfloat16
I32 = jnp.int32
PAIR = 2 * P_SIZE
ROWS = N + 16
STEPS = 4
HEADS = H // STEPS
WIDE = HEADS * P_SIZE
BLOCKS = REACH + 1 + 1 + SEQS * 4 + 1
SINK_BLOCK = REACH + 1
CACHE_BLOCK = SINK_BLOCK + 1
NULL_BLOCK = BLOCKS - 1


def iota(shape, axis):
    return lax.broadcasted_iota(I32, shape, axis)


def nn(a, b):
    return lax.dot_general(a, b, (((1,), (0,)), ((), ())), preferred_element_type=F32)


def nt(a, b):
    return lax.dot_general(a, b, (((1,), (1,)), ((), ())), preferred_element_type=F32)


def starts_of(lengths):
    first = lengths[0, 0]
    return first, first + lengths[0, 1]


def segment(positions, one, two):
    return (positions >= one).astype(I32) + (positions >= two).astype(I32)


def same_causal(one, two):
    t, u = iota((TOK, TOK), 0), iota((TOK, TOK), 1)
    return (segment(t, one, two) == segment(u, one, two)) & (t >= u)


def spread_matrix(step):
    rows = iota((H, WIDE), 0)
    lanes = iota((H, WIDE), 1)
    return jnp.where(rows == step * HEADS + lanes // P_SIZE, 1.0, 0.0).astype(BF16)


def await_bytes(ref, sem):
    pltpu.make_async_copy(ref, ref, sem).wait()


def exchange_kernel(
    home,
    lengths,
    gain,
    saved,
    x,
    steps,
    rates,
    write,
    read,
    cache_keys,
    cache_values,
    turn_keys,
    turn_values,
    state,
    extras,
    caches,
    band,
    partial,
    inputs,
    weight,
    run_rows,
    step_rows,
    inner,
    made,
    theirs,
    packed,
    recv,
    stored,
    entering,
    arrived,
    own_state,
    other_state,
    extra,
    plane,
    sent,
    got,
    local,
):
    group, me = lax.axis_index("sess"), lax.axis_index("ctx")
    across, deep = group // 2, group % 2
    y, z, core = me // 8, (me // 2) % 4, me % 2
    chip = me // 2
    sibling = me + 1 - 2 * core
    partner = group + 1 - 2 * deep
    x_groups = [((across + i) % 4) * 2 + deep for i in range(1, 4)]
    y_peers = [((y + i) % 4) * 8 + z * 2 + core for i in range(1, 4)]
    z_before = y * 8 + ((z + 3) % 4) * 2 + core
    z_after = [y * 8 + ((z + i) % 4) * 2 + core for i in range(1, 4)]
    onward = (me + 2) % CTX
    kinds = {name: i for i, name in enumerate(EXCHANGES)}

    def copy_in(src, dst, at):
        copy = pltpu.make_async_copy(src, dst, local.at[at])
        copy.start()
        return copy

    half = KVH * HD
    mine = [
        copy_in(cache_keys, caches.at[me, 0], 0),
        copy_in(cache_values, caches.at[me, 1], 1),
        copy_in(turn_keys, band.at[pl.ds(8 * REACH, 8), :, pl.ds(0, half)], 2),
        copy_in(turn_values, band.at[pl.ds(8 * REACH, 8), :, pl.ds(half, half)], 3),
        copy_in(saved, stored.at[group], 4),
        copy_in(x, inputs, 5),
    ]

    barrier = pltpu.get_barrier_semaphore()

    def greet(i, nothing):
        peer = ((chip + i) % CHIPS) * 2 + core
        pl.semaphore_signal(barrier, inc=1, device_id=(group, peer), device_id_type=MESH)
        return nothing

    lax.fori_loop(1, CHIPS, greet, 0)
    pl.semaphore_signal(barrier, inc=1, device_id=(group, sibling), device_id_type=MESH)
    for to in [partner] + x_groups:
        pl.semaphore_signal(barrier, inc=1, device_id=(to, me), device_id_type=MESH)
    pl.semaphore_wait(barrier, CHIPS - 1 + 1 + 4)

    def push(kind, src, dst, peer, to=None):
        at = kinds[kind]
        pltpu.make_async_remote_copy(
            src_ref=src,
            dst_ref=dst,
            send_sem=sent.at[at],
            recv_sem=got.at[at],
            device_id=(group if to is None else to, peer),
            device_id_type=MESH,
        ).start()

    counts = {}

    def arrive(kind, ref):
        counts[kind] = ref
        await_bytes(ref, got.at[kinds[kind]])

    def slot(distance):
        return band.at[pl.ds(8 * (REACH - distance), 8)]

    def spread(name, array, at):
        for to in y_peers:
            push(name + "_y", array.at[at], array.at[at], to)

    push("home_z", saved, stored.at[group], me, partner)
    for to in x_groups:
        push("home_x", saved, stored.at[group], me, to)
    mine[2].wait()
    mine[3].wait()
    push("band_2", slot(0), slot(2), onward)
    mine[0].wait()
    mine[1].wait()
    push("cache_1", caches.at[me], caches.at[me], z_before)
    spread("cache", caches, me)
    push("cache_core", caches.at[me], caches.at[me], sibling)

    one, two = starts_of(lengths)
    here_one, here_two = one - me * TOK, two - me * TOK
    seen = same_causal(here_one, here_two)
    mask = jnp.where(seen, 1.0, 0.0).astype(BF16)
    bias = jnp.where(seen, 0.0, -jnp.inf)
    run = nt(rates[...], mask)
    run_rows[...] = run
    step_rows[...] = steps[...].astype(F32)
    u = iota((1, TOK), 1)
    last = (TOK - 1 >= here_one).astype(I32) + (TOK - 1 >= here_two).astype(I32)
    held = segment(u, here_one, here_two) == last
    gap = jnp.where(held, run[:, TOK - 1 :] - run, -jnp.inf)
    weight[...] = jnp.exp(gap) * steps[...].astype(F32)
    turned_rates = rates[...].astype(F32).T.astype(BF16)
    mine[5].wait()

    def summarize(step, nothing):
        turned = write[:, pl.ds(pl.multiple_of(step * 2 * N, 2 * N), 2 * N)].astype(F32).T
        spread_rates = nn(turned_rates, spread_matrix(step)).astype(BF16)
        carry = jnp.exp(nn(mask[TOK - 16 :], spread_rates)[15:16])
        for k in range(HEADS):
            row = weight[pl.ds(step * HEADS + k, 1), :]
            b = k // G
            loads = (row * turned[b * N : (b + 1) * N]).astype(BF16)
            at = pl.multiple_of(step * WIDE + k * P_SIZE, P_SIZE)
            lane = (k % 2) * P_SIZE
            j = k // 2
            made[j % 2, step * (CHIPS // STEPS) + j // 2, :N, lane : lane + P_SIZE] = nn(
                loads, inputs[:, pl.ds(at, P_SIZE)]
            )
        for j in range(HEADS // 2):
            row = carry[:, j * PAIR : (j + 1) * PAIR]
            made[j % 2, step * (CHIPS // STEPS) + j // 2, N:, :] = jnp.broadcast_to(row, (8, PAIR))
        part = pl.ds(step * (CHIPS // STEPS), CHIPS // STEPS)
        push("pair", made.at[1 - core, part], theirs.at[part], sibling)
        return nothing

    lax.fori_loop(0, STEPS, summarize, 0)

    arrive("home_z", stored.at[0])
    for to in x_groups:
        push("home_x", stored.at[partner], stored.at[partner], me, to)

    def inside(c):
        end = c * TOK + TOK - 1
        first = (end >= one) & (end < two) & (one >= c * TOK)
        second = (end >= two) & (two >= c * TOK)
        return first, second

    arrive("pair", theirs)
    first_one, first_two = inside(2 * chip)
    last_one, last_two = inside(2 * chip + 1)
    fresh = last_one | last_two

    def both(m):
        own = made[core, m]
        other = theirs[m]
        even = jnp.where(core == 0, own, other)
        odd = jnp.where(core == 0, other, own)
        return even, odd

    def combine(i, nothing):
        m = (chip + i) % CHIPS
        even, odd = both(m)
        factor = odd[N : N + 1]
        total = odd[:N] + jnp.where(fresh, 0.0, factor) * even[:N]
        carry = factor * jnp.where(fresh, 1.0, even[N : N + 1])
        packed[m, :N, :] = total.astype(BF16)
        high = carry.astype(BF16).astype(F32)
        tile = iota((16, PAIR), 0)
        rows = jnp.where(tile == 0, high, jnp.where(tile == 1, carry - high, 0.0))
        packed[m, N:, :] = rows.astype(BF16)

        @pl.when(i != 0)
        def _():
            push("summary", packed.at[m], recv.at[chip], 2 * m + core)

        return nothing

    lax.fori_loop(0, CHIPS, combine, 0)
    own_summary = copy_in(packed.at[chip], recv.at[chip], 0)

    def within(step, nothing):
        spread_rates = nn(turned_rates, spread_matrix(step)).astype(BF16)
        run_wide = nn(mask, spread_rates)
        two_groups = pl.ds(pl.multiple_of(step * 2 * N, 2 * N), 2 * N)
        writes, reads = write[:, two_groups], read[:, two_groups]
        for b in range(HEADS // G):
            crossed = nt(reads[:, b * N : (b + 1) * N], writes[:, b * N : (b + 1) * N])
            for k in range(b * G, (b + 1) * G):
                at = pl.ds(step * HEADS + k, 1)
                lanes = pl.ds(pl.multiple_of(step * WIDE + k * P_SIZE, P_SIZE), P_SIZE)
                decay = run_wide[:, k * P_SIZE : (k + 1) * P_SIZE] - run_rows[at, :] + bias
                mixing = (crossed * jnp.exp(decay) * step_rows[at, :]).astype(BF16)
                x_h = inputs[:, lanes]
                inner[:, lanes] = nn(mixing, x_h) + gain[step * HEADS + k] * x_h.astype(F32)
        return nothing

    def hand_on(step):
        lanes = pl.ds(step * WIDE, WIDE)
        return copy_in(inner.at[:, lanes], partial.at[:, lanes], 6 + step)

    arrive("cache_1", caches.at[0])
    push("cache_2", caches.at[z_after[0]], caches.at[z_after[0]], z_before)
    spread("cache", caches, z_after[0])
    push("cache_core", caches.at[z_after[0]], caches.at[z_after[0]], sibling)
    arrive("band_2", slot(2))
    push("band_4", slot(2), slot(4), onward)

    lax.fori_loop(0, 2, within, 0)
    handed = [hand_on(0), hand_on(1)]

    mine[4].wait()
    arrive("home_x", stored.at[pl.ds(0, 6)])
    back = []
    for s in range(SEQS):
        at = home[group * SEQS + s]
        back.append(stored[at // SEQS, at % SEQS].astype(F32))
    extra[0] = back[1].astype(BF16)
    extra[1] = back[2].astype(BF16)
    push("extra_1", extra, plane.at[chip], z_before)
    for to in y_peers:
        push("extra_y", extra, plane.at[chip], to)
    own_extra = copy_in(extra, plane.at[chip], 1)

    lax.fori_loop(2, STEPS, within, 0)
    handed += [hand_on(2), hand_on(3)]

    arrive("cache_2", caches.at[0])
    push("cache_3", caches.at[z_after[1]], caches.at[z_after[1]], z_before)
    spread("cache", caches, z_after[1])
    push("cache_core", caches.at[z_after[1]], caches.at[z_after[1]], sibling)

    arrive("extra_1", plane.at[0])
    push("extra_2", plane.at[z_after[0] // 2], plane.at[z_after[0] // 2], z_before)
    spread("extra", plane, z_after[0] // 2)
    arrive("extra_2", plane.at[0])
    push("extra_3", plane.at[z_after[1] // 2], plane.at[z_after[1] // 2], z_before)
    spread("extra", plane, z_after[1] // 2)
    arrive("summary", recv.at[pl.ds(0, CHIPS - 1)])
    own_summary.wait()

    def turn(m, held):
        entering[m] = held.astype(BF16)

        @pl.when(m != chip)
        def _():
            push("state", entering.at[m], arrived.at[chip], 2 * m + core)

        even_one, even_two = inside(2 * m)
        odd_one, odd_two = inside(2 * m + 1)
        base = jnp.where(even_two, back[2], jnp.where(even_one, back[1], held))
        base = jnp.where(odd_two, back[2], jnp.where(odd_one, back[1], base))
        carry = recv[m, N : N + 16, :].astype(F32)
        return (carry[0:1] + carry[1:2]) * base + recv[m, :N, :].astype(F32)

    lax.fori_loop(0, CHIPS, turn, back[0])
    own_entering = copy_in(entering.at[chip], arrived.at[chip], 2)


    arrive("extra_3", plane.at[0])
    spread("extra", plane, z_after[2] // 2)
    arrive("cache_3", caches.at[0])
    spread("cache", caches, z_after[2])
    push("cache_core", caches.at[z_after[2]], caches.at[z_after[2]], sibling)
    arrive("band_4", slot(4))
    push("band_core", slot(2 * core), slot(1), sibling)
    push("band_core", slot(2 * core + 2), slot(3), sibling)
    own_extra.wait()
    arrive("extra_y", plane.at[pl.ds(0, 12)])
    push("extra_core", plane, extras.at[core], sibling)
    keep_extra = copy_in(plane, extras.at[core], 0)
    arrive("state", arrived.at[pl.ds(0, CHIPS - 1)])
    own_entering.wait()

    def settle(m, nothing):
        even, _ = both(m)
        first = arrived[m].astype(F32)
        base = jnp.where(
            first_two,
            plane[m, 1].astype(F32),
            jnp.where(first_one, plane[m, 0].astype(F32), first),
        )
        second = even[N : N + 1] * base + even[:N]
        own_state[m] = jnp.where(core == 0, first, second).astype(BF16)
        other_state[m] = jnp.where(core == 0, second, first).astype(BF16)
        return nothing

    lax.fori_loop(0, CHIPS, settle, 0)
    push("state_core", other_state, state.at[core], sibling)
    keep_state = copy_in(own_state, state.at[core], 1)
    arrive("cache_y", caches.at[pl.ds(0, 12)])
    for i in range(4):
        for j in range(1, 4):
            at = ((y + j) % 4) * 8 + ((z + i) % 4) * 2 + core
            push("cache_core", caches.at[at], caches.at[at], sibling)

    arrive("extra_core", extras.at[0])
    arrive("cache_core", caches.at[pl.ds(0, CHIPS)])
    arrive("band_core", band.at[pl.ds(0, 16)])
    arrive("state_core", state.at[0])
    for copy in handed + [keep_extra, keep_state]:
        copy.wait()
    for kind, ref in counts.items():
        await_bytes(ref, sent.at[kinds[kind]])


EXCHANGES = (
    "home_z",
    "home_x",
    "pair",
    "summary",
    "state",
    "state_core",
    "band_2",
    "band_4",
    "band_core",
    "cache_1",
    "cache_2",
    "cache_3",
    "cache_y",
    "cache_core",
    "extra_1",
    "extra_2",
    "extra_3",
    "extra_y",
    "extra_core",
)


def output_kernel(lengths, rates, read, partial, state, extra, out):
    step = pl.program_id(0)
    first = lax.axis_index("ctx") * TOK
    one, two = starts_of(lengths)
    one, two = one - first, two - first
    mask = jnp.where(same_causal(one, two), 1.0, 0.0).astype(BF16)
    t = iota((TOK, N), 0)
    new_one = (t >= one) & (t < two) & (one >= 0)
    new_two = (t >= two) & (two >= 0)
    turned = rates[...].astype(F32).T.astype(BF16)
    run = nn(mask, nn(turned, spread_matrix(step)).astype(BF16))
    for b in range(HEADS // G):
        c = read[:, b * N : (b + 1) * N].astype(F32)
        c_in = jnp.where(new_one | new_two, 0.0, c).astype(BF16)
        c_one = jnp.where(new_one, c, 0.0).astype(BF16)
        c_two = jnp.where(new_two, c, 0.0).astype(BF16)
        for j in range(G // 2):
            chunk = b * (G // 2) + j
            from_state = (
                nn(c_in, state[chunk % 2, chunk // 2])
                + nn(c_one, extra[chunk % 2, chunk // 2, 0])
                + nn(c_two, extra[chunk % 2, chunk // 2, 1])
            )
            lanes = slice(chunk * PAIR, (chunk + 1) * PAIR)
            result = partial[:, lanes] + jnp.exp(run[:, lanes]) * from_state
            out[:, lanes] = result.astype(BF16)


def attention_kernel(
    lengths,
    history,
    queries,
    band,
    sink_keys,
    sink_values,
    cache,
    out,
    keys,
    rows,
    scores,
    top,
    total,
    sums,
    bias,
    listed,
    sems,
):
    place = lax.axis_index("ctx")
    first = place * TOK
    one, two = starts_of(lengths)
    edges = [jnp.int32(0), one, two, jnp.int32(CTX * TOK)]
    lives = []
    for s in range(SEQS):
        begin = jnp.maximum(edges[s], first)
        present = begin < jnp.minimum(edges[s + 1], first + TOK)
        lives.append(
            [
                present
                & (begin - edges[s] < j * TOK + TOK - 1)
                & (history[0, s] - WINDOW + j * TOK + TOK - 1 >= SINKS)
                for j in range(4)
            ]
        )
    copies = [
        pltpu.make_async_copy(band, keys.at[pl.ds(0, 8 * SINK_BLOCK)], sems.at[0]),
    ]
    for copy in copies:
        copy.start()

    def history_copies(s):
        return [
            pltpu.make_async_copy(
                cache.at[:, kv, s],
                keys.at[pl.ds(8 * CACHE_BLOCK + 32 * s, 32), :, pl.ds(kv * KVH * HD, KVH * HD)],
                sems.at[2 + 2 * s + kv],
            )
            for kv in range(2)
        ]

    wanted = [lives[s][0] | lives[s][1] | lives[s][2] | lives[s][3] for s in range(SEQS)]
    for s in range(SEQS):

        @pl.when(wanted[s])
        def _():
            for copy in history_copies(s):
                copy.start()

    keys[8 * NULL_BLOCK :] = jnp.zeros((8, 16, 2 * KVH * HD), BF16)
    half = KVH * HD
    keys[8 * SINK_BLOCK + 1 : 8 * CACHE_BLOCK] = jnp.zeros((7, 16, 2 * half), BF16)
    for kv, sinks in enumerate((sink_keys, sink_values)):
        parts = [sinks[s].astype(F32) for s in range(SEQS)] + [jnp.zeros((4, half), F32)]
        both = jnp.concatenate(parts, axis=0).astype(BF16)
        keys[8 * SINK_BLOCK, :, kv * half : (kv + 1) * half] = both

    t = first + iota((TOK, TOK), 0)
    u = iota((TOK, TOK), 1)
    owner = segment(t, one, two)
    offset = t - jnp.where(owner == 2, two, jnp.where(owner == 1, one, 0))
    count = jnp.int32(0)
    head_owner = (first >= one).astype(I32) + (first >= two).astype(I32)
    for b in range(REACH + 1):
        pos = first + (b - REACH) * TOK + u
        gap = t - pos
        ok = (pos >= 0) & (segment(pos, one, two) == owner) & (gap >= 0) & (gap < WINDOW)
        bias[b] = jnp.where(ok, 0.0, -jnp.inf)
        end = first + (b - REACH) * TOK + TOK - 1
        end_owner = (end >= one).astype(I32) + (end >= two).astype(I32)
        live = (end >= 0) & (end_owner >= head_owner)
        listed[count] = b
        count = count + live.astype(I32)
    bias[SINK_BLOCK] = jnp.where(
        (u < SEQS * SINKS) & (u // SINKS == owner), 0.0, -jnp.inf
    )
    listed[count] = SINK_BLOCK
    count = count + 1
    for s in range(SEQS):
        for j in range(4):
            live = lives[s][j]
            block = CACHE_BLOCK + 4 * s + j

            @pl.when(live)
            def _():
                slot = j * TOK + u
                ok = (owner == s) & (slot > offset) & (history[0, s] - WINDOW + slot >= SINKS)
                bias[block] = jnp.where(ok, 0.0, -jnp.inf)

            listed[count] = block
            count = count + live.astype(I32)
    bias[NULL_BLOCK] = jnp.full((TOK, TOK), -jnp.inf, F32)
    listed[count] = NULL_BLOCK
    pairs = lax.div(count + 1, jnp.int32(2))
    for copy in copies:
        copy.wait()
    for s in range(SEQS):

        @pl.when(wanted[s])
        def _():
            for copy in history_copies(s):
                copy.wait()

    per = QH // KVH
    scale = 1.0 / math.sqrt(HD) / math.log(2.0)

    def heads(pair, nothing):
        def lanes(h, shift=0):
            return pl.ds(pl.multiple_of((pair * 2 + h) * HD + shift, HD), HD)

        def wide(h, r):
            return pl.ds(pl.multiple_of(((pair * 2 + h) * per + r) * HD, HD), HD)

        for h in range(2):
            for r in range(per):
                rows[h, r * TOK : (r + 1) * TOK, :] = queries[:, wide(h, r)]
        top[...] = jnp.full(top.shape, -jnp.inf, F32)
        total[...] = jnp.zeros(total.shape, F32)
        sums[...] = jnp.zeros(sums.shape, F32)

        def score(i, nothing):
            blocks = [listed[2 * i + side] for side in range(2)]
            left_bias, right_bias = bias[blocks[0]], bias[blocks[1]]
            for h in range(2):
                key = [keys[pl.ds(b * 8, 8), :, lanes(h)].reshape(TOK, HD) for b in blocks]
                key = jnp.concatenate(key, axis=0)
                for r in range(per):
                    at = slice(r * TOK, (r + 1) * TOK)
                    made = nt(rows[h, at, :], key) * scale
                    left = made[:, :TOK] + left_bias
                    right = made[:, TOK:] + right_bias
                    scores[2 * i, h, at, :] = left
                    scores[2 * i + 1, h, at, :] = right
                    top[h, at, :] = jnp.maximum(top[h, at, :], jnp.maximum(left, right))
            return nothing

        lax.fori_loop(0, pairs, score, 0)
        top[...] = jnp.broadcast_to(jnp.max(top[...], axis=2, keepdims=True), top.shape)

        def weigh(i, nothing):
            blocks = [listed[2 * i + side] for side in range(2)]
            for h in range(2):
                value = [
                    keys[pl.ds(b * 8, 8), :, lanes(h, KVH * HD)].reshape(TOK, HD) for b in blocks
                ]
                value = jnp.concatenate(value, axis=0)
                for r in range(per):
                    at = slice(r * TOK, (r + 1) * TOK)
                    left = jnp.exp2(scores[2 * i, h, at, :] - top[h, at, :])
                    right = jnp.exp2(scores[2 * i + 1, h, at, :] - top[h, at, :])
                    total[h, at, :] += left + right
                    both = jnp.concatenate([left.astype(BF16), right.astype(BF16)], axis=1)
                    sums[h, at, :] += nn(both, value)
            return nothing

        lax.fori_loop(0, pairs, weigh, 0)
        for h in range(2):
            for r in range(per):
                at = slice(r * TOK, (r + 1) * TOK)
                whole = jnp.sum(total[h, at, :], axis=1, keepdims=True)
                out[:, wide(h, r)] = (sums[h, at, :] / whole).astype(BF16)
        return nothing

    lax.fori_loop(0, KVH // 2, heads, 0)


SMEM = pl.BlockSpec(memory_space=pltpu.SMEM)
VMEM = pl.BlockSpec(memory_space=pltpu.VMEM)
ANY = pl.BlockSpec(memory_space=pl.ANY)
LIMIT = pltpu.CompilerParams(vmem_limit_bytes=60 * 2**20)


def full(shape):
    return pl.BlockSpec(shape, lambda i: (0,) * len(shape))


def lane_block(rows, width):
    return pl.BlockSpec((rows, width), lambda i: (0, i))


def exchange(
    groups,
    home,
    lengths,
    gain,
    saved,
    x,
    steps,
    rates,
    write,
    read,
    cache_keys,
    cache_values,
    turn_keys,
    turn_values,
):
    return pl.pallas_call(
        exchange_kernel,
        out_shape=(
            jax.ShapeDtypeStruct((2, CHIPS, N, PAIR), BF16),
            jax.ShapeDtypeStruct((2, CHIPS, 2, N, PAIR), BF16),
            jax.ShapeDtypeStruct((CTX, 2) + cache_keys.shape, BF16),
            jax.ShapeDtypeStruct((8 * (REACH + 1), 16, 2 * KVH * HD), BF16),
            jax.ShapeDtypeStruct((TOK, H * P_SIZE), F32),
        ),
        in_specs=[SMEM, SMEM, SMEM, ANY, ANY, VMEM, VMEM, VMEM, VMEM, ANY, ANY, ANY, ANY],
        out_specs=(ANY, ANY, ANY, ANY, ANY),
        scratch_shapes=[
            pltpu.VMEM((TOK, H * P_SIZE), BF16),
            pltpu.VMEM((H, TOK), F32),
            pltpu.VMEM((H, TOK), F32),
            pltpu.VMEM((H, TOK), F32),
            pltpu.VMEM((TOK, H * P_SIZE), F32),
            pltpu.VMEM((2, CHIPS, N + 8, PAIR), F32),
            pltpu.VMEM((CHIPS, N + 8, PAIR), F32),
            pltpu.VMEM((CHIPS, ROWS, PAIR), BF16),
            pltpu.VMEM((CHIPS, ROWS, PAIR), BF16),
            pltpu.VMEM((groups, SEQS, N, PAIR), BF16),
            pltpu.VMEM((CHIPS, N, PAIR), BF16),
            pltpu.VMEM((CHIPS, N, PAIR), BF16),
            pltpu.VMEM((CHIPS, N, PAIR), BF16),
            pltpu.VMEM((CHIPS, N, PAIR), BF16),
            pltpu.VMEM((2, N, PAIR), BF16),
            pltpu.VMEM((CHIPS, 2, N, PAIR), BF16),
            pltpu.SemaphoreType.DMA((len(EXCHANGES),)),
            pltpu.SemaphoreType.DMA((len(EXCHANGES),)),
            pltpu.SemaphoreType.DMA((10,)),
        ],
        compiler_params=pltpu.CompilerParams(
            collective_id=0, has_side_effects=True, vmem_limit_bytes=60 * 2**20
        ),
    )(
        home,
        lengths,
        gain,
        saved,
        x,
        steps,
        rates,
        write,
        read,
        cache_keys,
        cache_values,
        turn_keys,
        turn_values,
    )


def outputs(lengths, rates, read, partial, state, extra):
    return pl.pallas_call(
        output_kernel,
        grid=(STEPS,),
        out_shape=jax.ShapeDtypeStruct((TOK, H * P_SIZE), BF16),
        in_specs=[
            SMEM,
            full((H, TOK)),
            lane_block(TOK, 2 * N),
            lane_block(TOK, WIDE),
            pl.BlockSpec((2, CHIPS // STEPS, N, PAIR), lambda i: (0, i, 0, 0)),
            pl.BlockSpec((2, CHIPS // STEPS, 2, N, PAIR), lambda i: (0, i, 0, 0, 0)),
        ],
        out_specs=lane_block(TOK, WIDE),
        compiler_params=LIMIT,
    )(lengths, rates, read, partial, state, extra)


def attention(lengths, history, queries, band, sink_keys, sink_values, cache):
    rows = (QH // KVH) * TOK
    return pl.pallas_call(
        attention_kernel,
        out_shape=jax.ShapeDtypeStruct((TOK, QH * HD), BF16),
        in_specs=[SMEM, SMEM, VMEM, ANY, VMEM, VMEM, ANY],
        out_specs=VMEM,
        scratch_shapes=[
            pltpu.VMEM((8 * BLOCKS, 16, 2 * KVH * HD), BF16),
            pltpu.VMEM((2, rows, HD), BF16),
            pltpu.VMEM((BLOCKS + 1, 2, rows, TOK), F32),
            pltpu.VMEM((2, rows, TOK), F32),
            pltpu.VMEM((2, rows, TOK), F32),
            pltpu.VMEM((2, rows, HD), F32),
            pltpu.VMEM((BLOCKS, TOK, TOK), F32),
            pltpu.SMEM((BLOCKS + 1,), I32),
            pltpu.SemaphoreType.DMA((8,)),
        ],
        compiler_params=LIMIT,
        cost_estimate=pl.CostEstimate(
            flops=2_500_000_000, bytes_accessed=8_000_000, transcendentals=5_000_000
        ),
    )(lengths, history, queries, band, sink_keys, sink_values, cache)


def shards(
    mamba_input,
    step_size,
    decay_log,
    state_write,
    state_read,
    skip_gain,
    saved_states,
    home_slot,
    turn_lengths,
    history_lengths,
    queries,
    turn_keys,
    turn_values,
    cache_keys,
    cache_values,
    sink_keys,
    sink_values,
):
    x, steps, rates = mamba_input[0], step_size[0].T, decay_log[0].T
    write, read = state_write[0], state_read[0]
    saved = saved_states[0].astype(BF16).reshape(SEQS, 2, P_SIZE, N)
    saved = saved.transpose(0, 3, 1, 2).reshape(SEQS, N, PAIR)

    groups = lax.axis_size("sess")
    state, extras, caches, band, partial = exchange(
        groups,
        home_slot,
        turn_lengths,
        skip_gain,
        saved,
        x,
        steps,
        rates,
        write,
        read,
        cache_keys[0],
        cache_values[0],
        turn_keys[0].reshape(8, 16, KVH * HD),
        turn_values[0].reshape(8, 16, KVH * HD),
    )
    attended = attention(
        turn_lengths, history_lengths, queries[0], band, sink_keys[0], sink_values[0], caches
    )
    mixed = outputs(turn_lengths, rates, read, partial, state, extras)
    return (mixed[None], attended[None])


def solution(mesh):
    token = P("sess", "ctx", None)
    spread = P("sess", None, "ctx", None)
    return jax.shard_map(
        shards,
        mesh=mesh,
        in_specs=(
            token,
            token,
            token,
            token,
            token,
            P(),
            spread,
            P(),
            P("sess", None),
            P("sess", None),
            token,
            token,
            token,
            spread,
            spread,
            P("sess", None, None, None),
            P("sess", None, None, None),
        ),
        out_specs=(token, token),
        check_vma=False,
    )
```
